128 devices in a mesh: ctx: 8 (over x, core), ch: 16 (over z, y).
Axes of the slice: x: 4, y: 4, z: 4, core: 2. Of those that a mesh axis runs over, the one named last changes fastest.
Arguments:
- mr_query: bfloat16 [16384, 8192], P(('ctx', 'ch')), may hold values from -6 to 6
- mr_key: bfloat16 [16384, 8192], P(('ctx', 'ch')), may hold values from -6 to 6
- mr_value: bfloat16 [16384, 8192], P(('ctx', 'ch')), may hold values from -6 to 6
- li_query: bfloat16 [16384, 8192], P(('ctx', 'ch')), may hold values from -6 to 6
- li_key: bfloat16 [16384, 8192], P(('ctx', 'ch')), may hold values from -6 to 6
- out_cotangent: bfloat16 [16384, 8192], P(('ctx', 'ch')), may hold values from -6 to 6
- mr_short: bfloat16 [3, 3, 8192], replicated, may hold values from -3.5 to 3.5
- li_short: bfloat16 [3, 3, 8192], replicated, may hold values from -3.5 to 3.5
- mr_filter: bfloat16 [128, 512], replicated, may hold values from -0.5 to 0.5
- li_rate: float32 [512, 16], replicated, may hold values from 0 to 1, as said below
- li_residue: float32 [512, 16], replicated, may hold values from -1 to 1, as said below
- li_skip: float32 [8192], replicated, may hold values from -4 to 4
Outputs:
- output: bfloat16 [16384, 8192], P(('ctx', 'ch'))
- grad_mr_query: bfloat16 [16384, 8192], P(('ctx', 'ch'))
- grad_mr_key: bfloat16 [16384, 8192], P(('ctx', 'ch'))
- grad_mr_value: bfloat16 [16384, 8192], P(('ctx', 'ch'))
- grad_li_query: bfloat16 [16384, 8192], P(('ctx', 'ch'))
- grad_li_key: bfloat16 [16384, 8192], P(('ctx', 'ch'))
The draws below stay inside these ranges and needn't reach their ends.
Inputs may be any that keep to these rules, and one draw needn't show every extreme that they name: `li_rate`: positive decay rates, one for each of a group's 16 modes. `li_residue`: real residues, one for each of a group's 16 modes.
All inputs are finite; a program needn't handle non-finite values.
Results may differ from the reference program's by a relative error of at most 0.011.
Values may be sent and summed in bfloat16 or wider, within the bound.
No kernel may reach another device: no remote copies, remote signals or barrier semaphores. Data moves between devices by JAX's collectives and lax.ppermute only.
A program may use at most 576 MiB of HBM per device.

```python
import math
import jax
import jax.numpy as jnp
from jax import lax

D = 8192
GROUP = 16
MODES = 16
SHORT = 3
MR_TAPS = 128
GROUPS = 512
TOKENS = 16384


def shared_rates(key, slow_share):
    pick_key, slow_key, fast_key = jax.random.split(key, 3)
    table_shape = (D // GROUP, MODES)
    slow_modes = jax.random.bernoulli(pick_key, slow_share, table_shape)
    slow_rate = jnp.exp(jax.random.uniform(slow_key, table_shape, jnp.float32, math.log(0.05 / TOKENS), math.log(2.0 / TOKENS)))
    fast_rate = jnp.exp(jax.random.uniform(fast_key, table_shape, jnp.float32, math.log(2.0 / TOKENS), math.log(1.0 / 25.0)))
    return jnp.where(slow_modes, slow_rate, fast_rate)


def draw_li_rate(key, part):
    slow_share = 0.5
    decay_rates = shared_rates(key, slow_share)
    return decay_rates


def draw_li_residue(key, part):
    slow_share = 0.5
    decay_rates = shared_rates(key, slow_share)
    key = jax.random.fold_in(key, 11)
    normal_draw = jax.random.truncated_normal(key, -4.0, 4.0, decay_rates.shape, jnp.float32)
    return 0.3 * normal_draw * jnp.sqrt(2.0 * decay_rates + 1.0 / TOKENS)


def block_levels(rng, dims, cuts, smallest, high):
    def one(axis_at, parts):
        draws = jax.random.uniform(jax.random.fold_in(jax.random.fold_in(rng, 6), axis_at), (parts,), jnp.float32, smallest / len(cuts), high / len(cuts))
        return jnp.repeat(jnp.exp(draws), dims[axis_at] // parts).reshape((-1,) + (1,) * (len(dims) - axis_at - 1))

    gain = one(*cuts[0])
    for cut in cuts[1:]:
        gain = gain * one(*cut)
    return gain


def scatter_about(own_key, dims, scale, most, shards=(), kind=jnp.bfloat16):
    values = scale * jax.random.normal(own_key, dims, jnp.float32)
    if shards:
        values = values * block_levels(own_key, dims, shards, -0.22, 0.18)
    return jnp.clip(values, -most, most).astype(kind)


def setup_inputs(seed: int = 0) -> dict:
    key_of = jax.random.split(jax.random.key(seed), 13)
    return {
        "mr_query": scatter_about(key_of[0], (TOKENS, D), 1.0, 6.0, ((0, 128),)),
        "mr_key": scatter_about(key_of[1], (TOKENS, D), 1.0, 6.0, ((0, 128),)),
        "mr_value": scatter_about(key_of[2], (TOKENS, D), 1.0, 6.0, ((0, 128),)),
        "li_query": scatter_about(key_of[3], (TOKENS, D), 1.0, 6.0, ((0, 128),)),
        "li_key": scatter_about(key_of[4], (TOKENS, D), 1.0, 6.0, ((0, 128),)),
        "out_cotangent": scatter_about(key_of[5], (TOKENS, D), 1.0, 6.0, ((0, 128),)),
        "mr_short": scatter_about(key_of[6], (3, SHORT, D), SHORT ** -0.5, 3.5),
        "li_short": scatter_about(key_of[7], (3, SHORT, D), SHORT ** -0.5, 3.5),
        "mr_filter": scatter_about(key_of[8], (MR_TAPS, GROUPS), MR_TAPS ** -0.5, 0.5),
        "li_rate": draw_li_rate(jax.random.fold_in(key_of[12], 71), 0),
        "li_residue": draw_li_residue(jax.random.fold_in(key_of[12], 71), 0),
        "li_skip": scatter_about(key_of[11], (D,), 1.0, 4.0, (), jnp.float32),
    }


HIGHEST = lax.Precision.HIGHEST


def contract(pattern, first_operand, second_operand):
    return jnp.einsum(pattern, first_operand, second_operand, precision=HIGHEST)


def lag_tables():
    steps_in = jnp.arange(MR_TAPS, dtype=jnp.int32)
    lagged = steps_in[:, None] - steps_in[None, :]
    tap_index = steps_in[:, None, None]
    lower_table = (lagged[None, :, :] == tap_index).astype(jnp.float32)
    upper_table = (lagged[None, :, :] + MR_TAPS == tap_index).astype(jnp.float32)
    return lower_table, upper_table


def toeplitz(filters, table):
    return contract("kg,kij->gij", filters, table)


def short_forward(signal, margin, filter_taps):
    count_rows = signal.shape[0]
    extended = jnp.concatenate([margin.astype(jnp.float32), signal.astype(jnp.float32)], 0)
    result = jnp.zeros((count_rows, signal.shape[1]), jnp.float32)
    for offset in range(SHORT):
        first_row = SHORT - 1 - offset
        result = result + filter_taps[offset].astype(jnp.float32) * extended[first_row:first_row + count_rows]
    return result


def short_backward(signal, margin, filter_taps):
    count_rows = signal.shape[0]
    extended = jnp.concatenate([signal, margin], 0)
    result = jnp.zeros((count_rows, signal.shape[1]), jnp.float32)
    for offset in range(SHORT):
        result = result + filter_taps[offset].astype(jnp.float32) * extended[offset:offset + count_rows]
    return result


def split_blocks(signal, groups):
    count_rows, channels = signal.shape
    return signal.reshape(count_rows // MR_TAPS, MR_TAPS, groups, channels // groups)


def causal_medium(signal, near_toeplitz, far_toeplitz, before_block):
    groups = near_toeplitz.shape[0]
    blocks = split_blocks(signal, groups)
    prior_blocks = jnp.concatenate([split_blocks(before_block, groups), blocks[:-1]], 0)
    result = contract("gij,bjgc->bigc", near_toeplitz, blocks) + contract("gij,bjgc->bigc", far_toeplitz, prior_blocks)
    return result.reshape(signal.shape)


def anticausal_medium(signal, near_toeplitz, far_toeplitz, after_block):
    groups = near_toeplitz.shape[0]
    blocks = split_blocks(signal, groups)
    later_blocks = jnp.concatenate([blocks[1:], split_blocks(after_block, groups)], 0)
    result = contract("gij,bigc->bjgc", near_toeplitz, blocks) + contract("gij,bigc->bjgc", far_toeplitz, later_blocks)
    return result.reshape(signal.shape)


def modal_tables(li_rate, li_residue, lower_table):
    positions = jnp.arange(MR_TAPS, dtype=jnp.float32)
    powers = jnp.exp(-li_rate[:, :, None] * positions)
    impulse = contract("gn,gnk->kg", li_residue, powers)
    near_long = toeplitz(impulse, lower_table)
    emit_table = li_residue[:, :, None] * jnp.exp(-li_rate[:, :, None] * (positions + 1.0))
    absorb_table = jnp.exp(-li_rate[:, :, None] * (MR_TAPS - 1.0 - positions))
    emit_back = li_residue[:, :, None] * jnp.exp(-li_rate[:, :, None] * (MR_TAPS - positions))
    return near_long, emit_table, absorb_table, emit_back, powers


def long_forward(signal, near_long, emit_table, end_states, block_decay, incoming):
    groups = near_long.shape[0]
    blocks = split_blocks(signal, groups)

    def advance(carried, end_state):
        return block_decay[:, :, None] * carried + end_state, carried

    unused, start_states = lax.scan(advance, incoming, end_states)
    result = contract("gij,bjgc->bigc", near_long, blocks) + contract("gni,bgnc->bigc", emit_table, start_states)
    return result.reshape(signal.shape)


def long_backward(signal, near_long, emit_back, owned_states, block_decay, incoming):
    groups = near_long.shape[0]
    blocks = split_blocks(signal, groups)

    def retreat(carried, own_state):
        return own_state + block_decay[:, :, None] * carried, carried

    unused, closing_states = lax.scan(retreat, incoming, owned_states, reverse=True)
    result = contract("gij,bigc->bjgc", near_long, blocks) + contract("gnj,bgnc->bjgc", emit_back, closing_states)
    return result.reshape(signal.shape)


def pair_block(mr_query, mr_key, mr_value, li_query, li_key, out_cotangent, mr_short, li_short, mr_filter, li_rate, li_residue, li_skip):
    count_rows, channels = mr_query.shape
    groups = channels // GROUP
    lower_table, upper_table = lag_tables()
    near_medium = toeplitz(mr_filter.astype(jnp.float32), lower_table)
    far_medium = toeplitz(mr_filter.astype(jnp.float32), upper_table)
    blank_edge = jnp.zeros((SHORT - 1, channels), jnp.float32)
    blank_block = jnp.zeros((MR_TAPS, channels), jnp.float32)
    blank_state = jnp.zeros((groups, MODES, GROUP), jnp.float32)
    query_one = short_forward(mr_query, blank_edge, mr_short[0])
    keys_one = short_forward(mr_key, blank_edge, mr_short[1])
    value_one = short_forward(mr_value, blank_edge, mr_short[2])
    prod_one = keys_one * value_one
    conv_one = causal_medium(prod_one, near_medium, far_medium, blank_block)
    mixed_one = (query_one * conv_one).astype(jnp.bfloat16)
    query_two = short_forward(li_query, blank_edge, li_short[0])
    keys_two = short_forward(li_key, blank_edge, li_short[1])
    value_two = short_forward(mixed_one, blank_edge, li_short[2])
    prod_two = keys_two * value_two
    near_long, emit_table, absorb_table, emit_back, absorb_back = modal_tables(li_rate, li_residue, lower_table)
    block_decay = jnp.exp(-li_rate * MR_TAPS)
    end_states = contract("gnj,bjgc->bgnc", absorb_table, split_blocks(prod_two, groups))
    conv_two = long_forward(prod_two, near_long, emit_table, end_states, block_decay, blank_state) + li_skip * prod_two
    output = (query_two * conv_two).astype(jnp.bfloat16)
    upstream = out_cotangent.astype(jnp.float32)
    query_two_grad = upstream * conv_two
    conv_two_grad = upstream * query_two
    owned_states = contract("gnj,bjgc->bgnc", absorb_back, split_blocks(conv_two_grad, groups))
    prod_two_grad = long_backward(conv_two_grad, near_long, emit_back, owned_states, block_decay, blank_state) + li_skip * conv_two_grad
    grad_li_query = short_backward(query_two_grad, blank_edge, li_short[0]).astype(jnp.bfloat16)
    grad_li_key = short_backward(prod_two_grad * value_two, blank_edge, li_short[1]).astype(jnp.bfloat16)
    mixed_grad = short_backward(prod_two_grad * keys_two, blank_edge, li_short[2])
    conv_one_grad = mixed_grad * query_one
    prod_one_grad = anticausal_medium(conv_one_grad, near_medium, far_medium, blank_block)
    grad_mr_query = short_backward(mixed_grad * conv_one, blank_edge, mr_short[0]).astype(jnp.bfloat16)
    grad_mr_key = short_backward(prod_one_grad * value_one, blank_edge, mr_short[1]).astype(jnp.bfloat16)
    grad_mr_value = short_backward(prod_one_grad * keys_one, blank_edge, mr_short[2]).astype(jnp.bfloat16)
    return output, grad_mr_query, grad_mr_key, grad_mr_value, grad_li_query, grad_li_key


def reference(mr_query, mr_key, mr_value, li_query, li_key, out_cotangent, mr_short, li_short, mr_filter, li_rate, li_residue, li_skip):
    block_width = math.gcd(D, 512)
    blocks_count = D // block_width
    block_groups = block_width // GROUP

    def one_block(block_index, outputs):
        column_start = (block_index * block_width).astype(jnp.int32)
        group_start = (block_index * block_groups).astype(jnp.int32)

        def columns_of(array):
            return lax.dynamic_slice_in_dim(array, column_start, block_width, 1)

        results = pair_block(
            columns_of(mr_query), columns_of(mr_key), columns_of(mr_value),
            columns_of(li_query), columns_of(li_key), columns_of(out_cotangent),
            lax.dynamic_slice_in_dim(mr_short, column_start, block_width, 2),
            lax.dynamic_slice_in_dim(li_short, column_start, block_width, 2),
            lax.dynamic_slice_in_dim(mr_filter, group_start, block_groups, 1),
            lax.dynamic_slice_in_dim(li_rate, group_start, block_groups, 0),
            lax.dynamic_slice_in_dim(li_residue, group_start, block_groups, 0),
            lax.dynamic_slice_in_dim(li_skip, column_start, block_width, 0))
        return tuple(lax.dynamic_update_slice_in_dim(target, piece, column_start, 1) for target, piece in zip(outputs, results))

    initial = tuple(jnp.zeros((TOKENS, D), jnp.bfloat16) for copy_index in range(6))
    return lax.fori_loop(0, blocks_count, one_block, initial)
```

```python
import functools

import jax
import jax.numpy as jnp
from jax import lax
from jax.experimental import pallas as pl
from jax.experimental.pallas import tpu as pltpu
from jax.sharding import PartitionSpec as P

GROUP = 16
SHORT = 3
MR_TAPS = 128
MODES = 16
ROWS = 128
LANES = 128
TILE_GROUPS = LANES // GROUP
AXES = ("ctx", "ch")
BF16 = jnp.bfloat16
F32 = jnp.float32

MR_Q, MR_K, MR_V, LI_Q, LI_K, LI_V, SKIP, LAST_TAP, IMPULSE_0, IMPULSE_1 = 0, 3, 6, 9, 12, 15, 18, 19, 20, 21
TABLE_ROWS = 24


def lane_call(body, name, width, ins, outs, scratch, flops):
    channels = next(a.shape[1] for a, kind in ins if kind == "r")
    width = min(width, channels)
    tiles = width // LANES

    def spec(shape, kind):
        if kind == "r":
            return pl.BlockSpec((shape[0], width), lambda i: (0, i))
        if kind == "g":
            return pl.BlockSpec((width // GROUP, shape[1]), lambda i: (i, 0))
        return pl.BlockSpec((2 * tiles, 8, LANES), lambda i: (i, 0, 0))

    def view(ref, kind, t):
        if kind == "r":
            return ref.at[:, pl.ds(pl.multiple_of(t * LANES, LANES), LANES)]
        if kind == "g":
            return ref.at[pl.ds(pl.multiple_of(t * TILE_GROUPS, TILE_GROUPS), TILE_GROUPS), :]
        return ref.at[pl.ds(2 * t, 2)]

    kinds = [kind for _, kind in ins] + [kind for _, _, kind in outs]

    def kernel(*refs):
        arrays, extra = refs[: len(kinds)], refs[len(kinds) :]

        def step(t, unused):
            body(*[view(ref, kind, t) for ref, kind in zip(arrays, kinds)], *extra)
            return unused

        lax.fori_loop(0, tiles, step, 0)

    moved = sum(a.size * a.dtype.itemsize for a, _ in ins)
    out_shape = [jax.ShapeDtypeStruct(shape, dtype) for shape, dtype, _ in outs]
    moved += sum(s.size * s.dtype.itemsize for s in out_shape)
    return pl.pallas_call(
        kernel,
        name=name,
        grid=(channels // width,),
        in_specs=[spec(a.shape, kind) for a, kind in ins],
        out_specs=[spec(shape, kind) for shape, _, kind in outs],
        out_shape=out_shape,
        scratch_shapes=scratch,
        compiler_params=pltpu.CompilerParams(vmem_limit_bytes=32 * 1024 * 1024),
        cost_estimate=pl.CostEstimate(flops=flops, bytes_accessed=moved, transcendentals=0),
    )(*[a for a, _ in ins])


EXT = pltpu.VMEM((ROWS + 16, LANES), F32)


def turned(x, by):
    return pltpu.roll(x, by, 0) if by else x


def fill(ext, value, prev8=None, next8=None):
    ext[8 : 8 + ROWS, :] = value
    if prev8 is not None:
        ext[0:8, :] = prev8
    if next8 is not None:
        ext[8 + ROWS :, :] = next8


def taps(table, first):
    return [table[first + j : first + j + 1, :] for j in range(SHORT)]


def short_forward(ext, weights, rows=ROWS):
    return (
        weights[0] * ext[8 : 8 + rows, :]
        + weights[1] * ext[7 : 7 + rows, :]
        + weights[2] * ext[6 : 6 + rows, :]
    )


def short_backward(ext, weights):
    return (
        weights[0] * ext[8 : 8 + ROWS, :]
        + weights[1] * ext[9 : 9 + ROWS, :]
        + weights[2] * ext[10 : 10 + ROWS, :]
    )


def iota(shape, dim):
    return lax.broadcasted_iota(jnp.int32, shape, dim)


def circulant(base, g):
    row = jnp.broadcast_to(base[g : g + 1, :], (ROWS, LANES))
    return pltpu.roll(row, 0, 1, stride=1, stride_axis=0)


def paired(signal):
    odd = ((iota((ROWS, LANES), 1) // GROUP) % 2).astype(F32)
    upper = signal * (1.0 - odd).astype(signal.dtype)
    lower = signal * odd.astype(signal.dtype)
    return jnp.concatenate([upper, lower], 0)


def pick_pairs(products, rows):
    pair = iota((rows, LANES), 1) // (2 * GROUP)
    total = products[0:rows]
    for p in range(1, TILE_GROUPS // 2):
        total = jnp.where(pair == p, products[p * rows : (p + 1) * rows], total)
    return total


def toeplitz_product(base_ref, keep, signal, tables):
    base = base_ref[...]
    for g in range(TILE_GROUPS):
        p, half = g // 2, g % 2
        table = jnp.where(keep, circulant(base, g), 0.0).astype(BF16)
        tables[p * ROWS : (p + 1) * ROWS, half * LANES : (half + 1) * LANES] = table
    products = jnp.dot(tables[...], paired(signal), preferred_element_type=F32)
    return pick_pairs(products, ROWS)


def own_group():
    return (iota((LANES, LANES), 0) // MODES == iota((LANES, LANES), 1) // GROUP).astype(F32)


def spread(state):
    return (jnp.concatenate([state] * TILE_GROUPS, 0) * own_group()).astype(BF16)


def absorb(powers, signal):
    every = lax.dot_general(
        powers.astype(BF16), signal, (((0,), (0,)), ((), ())), preferred_element_type=F32
    )
    return (every * own_group()).reshape(TILE_GROUPS, MODES, LANES).sum(0)


def store_state(ref, state):
    ref[...] = state.reshape(2, 8, LANES)


def load_state(ref):
    return ref[...].reshape(MODES, LANES)


def product_one_body(key, value, prev_kv, table, out, ext_k, ext_v):
    weights = table[...]
    margin = prev_kv[...].astype(F32)
    fill(ext_k, key[...].astype(F32), turned(margin, 4))
    fill(ext_v, value[...].astype(F32), margin)
    keys_one = short_forward(ext_k, taps(weights, MR_K))
    value_one = short_forward(ext_v, taps(weights, MR_V))
    out[...] = (keys_one * value_one).astype(BF16)


def upstream_body(li_query, upstream, prev_rest, table, rate, cotangent, state, ext):
    weights = table[...]
    margin = prev_rest[...].astype(F32)
    fill(ext, li_query[...].astype(F32), turned(margin, 2))
    query_two = short_forward(ext, taps(weights, LI_Q))
    rounded = (upstream[...].astype(F32) * query_two).astype(BF16)
    cotangent[...] = rounded
    position = iota((ROWS, LANES), 0).astype(F32)
    store_state(state, absorb(jnp.exp(-rate[...] * position), rounded))


def long_back_near_body(cotangent, table, base, out, tables):
    keep = iota((ROWS, LANES), 1) >= iota((ROWS, LANES), 0)
    signal = cotangent[...]
    near = toeplitz_product(base, keep, signal, tables)
    out[...] = near + table[SKIP : SKIP + 1, :] * signal.astype(F32)


def medium_near_body(
    signal, query, prev_kv, prev_rest, table, base, out, tail, ext, tables
):
    weights = table[...]
    keep = iota((ROWS, LANES), 1) <= iota((ROWS, LANES), 0)
    near = toeplitz_product(base, keep, signal[...], tables)
    out[...] = near
    margin = prev_kv[...].astype(F32)
    w_k, w_v = taps(weights, MR_K), taps(weights, MR_V)
    key_before = w_k[0] * margin[3:4] + w_k[1] * margin[2:3] + w_k[2] * margin[1:2]
    value_before = w_v[0] * margin[7:8] + w_v[1] * margin[6:7] + w_v[2] * margin[5:6]
    before = (key_before * value_before).astype(BF16).astype(F32)
    far = weights[LAST_TAP : LAST_TAP + 1] * before
    fill(ext, query[...].astype(F32), turned(prev_rest[...].astype(F32), 4))
    query_one = short_forward(ext, taps(weights, MR_Q))
    first = query_one[ROWS - 2 : ROWS - 1] * (near[ROWS - 2 : ROWS - 1] + far)
    second = query_one[ROWS - 1 :] * near[ROWS - 1 :]
    tail[0:1, :] = first.astype(BF16).astype(F32)
    tail[1:2, :] = second.astype(BF16).astype(F32)


def long_back_body(
    near, closing, cotangent, li_query, li_key, query, prev_rest, next_rest, table, rate, residue,
    grad_two, grad_two_after, mixed_grad, out, mixed_head, out_head,
    ext_q, ext_k, ext_g, ext_o,
):
    weights = table[...]
    before = prev_rest[...].astype(F32)
    after = next_rest[...].astype(F32)[0:8]
    fill(ext_q, li_query[...].astype(F32), None, after)
    w = taps(weights, LI_Q)
    base = 8 + ROWS
    query_after = w[0] * ext_q[base : base + 8, :] + w[1] * ext_q[base - 1 : base + 7, :] + w[2] * ext_q[base - 2 : base + 6, :]
    cot_after = turned(after, 4) * query_after
    state = load_state(closing)
    distance = (ROWS - iota((ROWS + 16, LANES), 0)).astype(F32)
    emit = (residue[...] * jnp.exp(-rate[...] * distance)).astype(BF16)
    emitted = jnp.dot(emit, spread(state), preferred_element_type=F32)
    later = jnp.dot(emit[ROWS:], spread(state - cot_after[0:1]), preferred_element_type=F32)
    skip = weights[SKIP : SKIP + 1]
    own = near[...] + emitted[0:ROWS]
    at_row = iota((8, LANES), 0)
    past = jnp.where(at_row == 0, emitted[ROWS : ROWS + 8], later[0:8]) + skip * cot_after
    past = jnp.where(at_row < 2, past, 0.0)
    grad_two[...] = own.astype(BF16)
    grad_two_after[...] = past
    fill(ext_k, li_key[...].astype(F32), before, turned(after, 6))
    keys_two = short_forward(ext_k, taps(weights, LI_K), ROWS + 8)
    fill(ext_g, own * keys_two[0:ROWS], None, past * keys_two[ROWS:])
    mixed = short_backward(ext_g, taps(weights, LI_V))
    fill(ext_o, query[...].astype(F32), turned(before, 4))
    conv_grad = mixed * short_forward(ext_o, taps(weights, MR_Q))
    mixed_grad[...] = mixed.astype(BF16)
    mixed_head[...] = mixed[0:2]
    out[...] = conv_grad.astype(BF16)
    out_head[...] = conv_grad[0:1]


def medium_far_body(
    before, near, query, li_key, prev_rest, prev_tail, table, base, rate,
    conv_one, value_two, prod_two, state, head, ext_q, ext_k, ext_m, tables,
):
    weights = table[...]
    keep = iota((ROWS, LANES), 1) > iota((ROWS, LANES), 0)
    conv = near[...] + toeplitz_product(base, keep, before[...], tables)
    margin = prev_rest[...].astype(F32)
    fill(ext_q, query[...].astype(F32), turned(margin, 4))
    query_one = short_forward(ext_q, taps(weights, MR_Q))
    fill(ext_m, (query_one * conv).astype(BF16).astype(F32))
    ext_m[6:8, :] = prev_tail[...]
    value = short_forward(ext_m, taps(weights, LI_V))
    fill(ext_k, li_key[...].astype(F32), margin)
    keys_two = short_forward(ext_k, taps(weights, LI_K))
    product = (keys_two * value).astype(BF16)
    conv_one[...] = conv.astype(BF16)
    value_two[...] = value.astype(BF16)
    prod_two[...] = product
    head[0:2, :] = product[0:16].astype(F32)[0:2]
    head[2:4, :] = value[0:2]
    head[4:6, :] = conv[0:2]
    position = (ROWS - 1 - iota((ROWS, LANES), 0)).astype(F32)
    store_state(state, absorb(jnp.exp(-rate[...] * position), product))


def long_near_body(
    prod_two, grad_two, grad_two_after, value_two, mixed_grad, mixed_after, conv_one, next_head,
    table, base, near, grad_li_key, grad_mr_query, ext_k, ext_q, tables,
):
    weights = table[...]
    keep = iota((ROWS, LANES), 1) <= iota((ROWS, LANES), 0)
    signal = prod_two[...]
    product = toeplitz_product(base, keep, signal, tables)
    near[...] = product + weights[SKIP : SKIP + 1] * signal.astype(F32)
    fill(ext_k, grad_two[...].astype(F32) * value_two[...].astype(F32))
    ext_k[8 + ROWS : 10 + ROWS, :] = grad_two_after[0:2, :] * next_head[2:4, :]
    grad_li_key[...] = short_backward(ext_k, taps(weights, LI_K)).astype(BF16)
    fill(ext_q, mixed_grad[...].astype(F32) * conv_one[...].astype(F32))
    ext_q[8 + ROWS : 10 + ROWS, :] = mixed_after[...] * next_head[4:6, :]
    grad_mr_query[...] = short_backward(ext_q, taps(weights, MR_Q)).astype(BF16)


def long_body(
    near, start, end, li_query, upstream, prev_rest, next_rest, next_head, table, rate, residue,
    out, grad_li_query, ext_q, ext_g,
):
    weights = table[...]
    distance = (iota((ROWS + 16, LANES), 0) + 1).astype(F32)
    emit = (residue[...] * jnp.exp(-rate[...] * distance)).astype(BF16)
    emitted = jnp.dot(emit, spread(load_state(start)), preferred_element_type=F32)
    conv = near[...] + emitted[0:ROWS]
    margin = prev_rest[...].astype(F32)
    fill(ext_q, li_query[...].astype(F32), turned(margin, 2))
    query_two = short_forward(ext_q, taps(weights, LI_Q))
    out[...] = (query_two * conv).astype(BF16)
    ended = jnp.dot(emit[0:16], spread(load_state(end)), preferred_element_type=F32)
    at_once = weights[IMPULSE_0 : IMPULSE_0 + 1] + weights[SKIP : SKIP + 1]
    first, second = next_head[0:1, :], next_head[1:2, :]
    past = emitted[ROWS : ROWS + 8] + ended[0:8]
    past_first = past[0:1] + at_once * first
    past_second = past[1:2] + weights[IMPULSE_1 : IMPULSE_1 + 1] * first + at_once * second
    after = turned(next_rest[...].astype(F32)[0:8], 4)
    fill(ext_g, upstream[...].astype(F32) * conv)
    ext_g[8 + ROWS : 9 + ROWS, :] = after[0:1] * past_first
    ext_g[9 + ROWS : 10 + ROWS, :] = after[1:2] * past_second
    grad_li_query[...] = short_backward(ext_g, taps(weights, LI_Q)).astype(BF16)


def medium_back_near_body(cotangent, base, out, tables):
    keep = iota((ROWS, LANES), 1) >= iota((ROWS, LANES), 0)
    out[...] = toeplitz_product(base, keep, cotangent[...], tables)


def medium_back_body(
    near, after, after_next, key, value, prev_kv, next_rest, table, base_ref,
    grad_key, grad_value, ext_k, ext_v, ext_gk, ext_gv, tables,
):
    weights = table[...]
    base = base_ref[...]
    row, lane = iota((ROWS, LANES), 0), iota((ROWS, LANES), 1)
    rows = ROWS + 16
    for g in range(TILE_GROUPS):
        p, half = g // 2, g % 2
        whole = circulant(base, g)
        at = slice(half * LANES, (half + 1) * LANES)
        tables[p * rows : p * rows + ROWS, at] = jnp.where(lane < row, whole, 0.0).astype(BF16)
        tables[p * rows + ROWS : (p + 1) * rows, at] = jnp.where(
            lane[0:16] >= row[0:16], whole[0:16], 0.0
        ).astype(BF16)
    products = pick_pairs(
        jnp.dot(tables[...], paired(after[...]), preferred_element_type=F32), rows
    )
    grad = near[...] + products[0:ROWS]
    beyond = weights[LAST_TAP : LAST_TAP + 1] * after_next[...].astype(BF16).astype(F32)
    at_row = iota((8, LANES), 0)
    past = products[ROWS : ROWS + 8] + jnp.where(at_row == 1, beyond, 0.0)
    before = prev_kv[...].astype(F32)
    following = next_rest[...].astype(F32)
    fill(ext_k, key[...].astype(F32), turned(before, 4), turned(following[0:8], 2))
    fill(ext_v, value[...].astype(F32), before, following[8:16])
    keys_one = short_forward(ext_k, taps(weights, MR_K), ROWS + 8)
    value_one = short_forward(ext_v, taps(weights, MR_V), ROWS + 8)
    fill(ext_gk, grad * value_one[0:ROWS], None, past * value_one[ROWS:])
    fill(ext_gv, grad * keys_one[0:ROWS], None, past * keys_one[ROWS:])
    grad_key[...] = short_backward(ext_gk, taps(weights, MR_K)).astype(BF16)
    grad_value[...] = short_backward(ext_gv, taps(weights, MR_V)).astype(BF16)


def scan_states(states, rates, backward):
    count = states.shape[0]

    def kernel(states_ref, rates_ref, out_ref):
        decay = jnp.exp(rates_ref[...] * (-float(ROWS)))

        def step(k, carried):
            b = count - 1 - k if backward else k
            out_ref[b] = carried
            return decay * carried + states_ref[b]

        lax.fori_loop(0, count, step, jnp.zeros((8, LANES), F32), unroll=8)

    return pl.pallas_call(
        kernel,
        name="scan_back" if backward else "scan_forward",
        out_shape=jax.ShapeDtypeStruct(states.shape, F32),
        in_specs=[pl.BlockSpec(memory_space=pltpu.VMEM)] * 2,
        out_specs=pl.BlockSpec(memory_space=pltpu.VMEM),
        cost_estimate=pl.CostEstimate(flops=0, bytes_accessed=8 * states.size, transcendentals=0),
    )(states, rates)


def sent(array, by):
    size = lax.axis_size(AXES)
    pairs = [(i, i + by) for i in range(size) if 0 <= i + by < size]
    return lax.ppermute(array, AXES, pairs)


def exchanged(array):
    return lax.all_to_all(array, AXES, split_axis=0, concat_axis=0, tiled=True)


def by_channel(per_group):
    return jnp.repeat(per_group, GROUP)[None, :]


def reversed_base(base):
    return jnp.concatenate([base[:, :1], base[:, :0:-1]], 1)


def per_device(
    mr_query, mr_key, mr_value, li_query, li_key, upstream,
    mr_short, li_short, mr_filter, li_rate, li_residue, li_skip,
):
    channels = mr_query.shape[1]
    tiles = channels // LANES
    devices = lax.axis_size(AXES)
    assert mr_query.shape[0] == ROWS and devices == 2 * tiles
    rows = (ROWS, channels)
    states = (2 * tiles, 8, LANES)

    prev_kv = sent(jnp.concatenate([mr_key[ROWS - 4 :], mr_value[ROWS - 4 :]], 0), 1)
    prev_rest = sent(
        jnp.concatenate([mr_query[ROWS - 4 :], li_query[ROWS - 2 :], li_key[ROWS - 2 :]], 0), 1
    )
    next_rest = sent(
        jnp.concatenate(
            [li_query[:2], li_key[:2], upstream[:2], mr_key[:2], mr_value[:2],
             jnp.zeros((6, channels), BF16)], 0
        ),
        -1,
    )

    positions = jnp.arange(MR_TAPS, dtype=F32)
    impulse = jnp.sum(
        li_residue[:, :, None] * jnp.exp(-li_rate[:, :, None] * positions), axis=1
    )
    taps_by_group = mr_filter.astype(F32).T
    base_medium_back = taps_by_group
    base_medium = reversed_base(taps_by_group)
    base_long_back = impulse
    base_long = reversed_base(impulse)
    table = jnp.concatenate(
        [
            mr_short.reshape(9, channels).astype(F32),
            li_short.reshape(9, channels).astype(F32),
            li_skip[None, :],
            by_channel(taps_by_group[:, MR_TAPS - 1]),
            by_channel(impulse[:, 0]),
            by_channel(impulse[:, 1]),
            jnp.zeros((TABLE_ROWS - 22, channels), F32),
        ],
        0,
    )
    rate = li_rate.reshape(1, channels)
    residue = li_residue.reshape(1, channels)
    me = lax.axis_index(AXES)
    my_rates = lax.dynamic_slice(
        li_rate, ((me // 2) * TILE_GROUPS, (me % 2) * 8), (TILE_GROUPS, 8)
    )
    my_rates = jnp.repeat(my_rates.T, GROUP, axis=1)

    wide = pltpu.VMEM((TILE_GROUPS // 2 * ROWS, 2 * LANES), BF16)
    wider = pltpu.VMEM((TILE_GROUPS // 2 * (ROWS + 16), 2 * LANES), BF16)
    heavy = 2 * 512 * 128 * 256 * 128 * 2
    call = functools.partial(lane_call)

    (signal_one,) = call(
        product_one_body, "product_one", 1024,
        [(mr_key, "r"), (mr_value, "r"), (prev_kv, "r"), (table, "r")],
        [(rows, BF16, "r")], [EXT, EXT], 0,
    )
    before_one = sent(signal_one, 1)

    cotangent, state_back = call(
        upstream_body, "upstream", 1024,
        [(li_query, "r"), (upstream, "r"), (prev_rest, "r"), (table, "r"), (rate, "r")],
        [(rows, BF16, "r"), (states, F32, "s")], [EXT], 0,
    )
    gathered_back = exchanged(state_back)

    (near_back,) = call(
        long_back_near_body, "long_back_near", 1024,
        [(cotangent, "r"), (table, "r"), (base_long_back, "g")],
        [(rows, F32, "r")], [wide], heavy,
    )
    near_one, tail = call(
        medium_near_body, "medium_near", 1024,
        [(signal_one, "r"), (mr_query, "r"), (prev_kv, "r"), (prev_rest, "r"), (table, "r"),
         (base_medium, "g")],
        [(rows, F32, "r"), ((2, channels), F32, "r")], [EXT, wide], heavy,
    )
    prev_tail = sent(tail, 1)

    closing = exchanged(scan_states(gathered_back, my_rates, True))

    grad_two, grad_two_after, mixed_grad, conv_grad, mixed_head, conv_head = call(
        long_back_body, "long_back", 1024,
        [(near_back, "r"), (closing, "s"), (cotangent, "r"), (li_query, "r"), (li_key, "r"),
         (mr_query, "r"), (prev_rest, "r"), (next_rest, "r"), (table, "r"), (rate, "r"),
         (residue, "r")],
        [(rows, BF16, "r"), ((8, channels), F32, "r"), (rows, BF16, "r"), (rows, BF16, "r"),
         ((2, channels), F32, "r"), ((1, channels), F32, "r")],
        [EXT, EXT, EXT, EXT], 0,
    )
    after_one = sent(conv_grad, -1)
    mixed_after = sent(mixed_head, -1)
    after_next = sent(conv_head, -2)

    conv_one, value_two, prod_two, state, head = call(
        medium_far_body, "medium_far", 1024,
        [(before_one, "r"), (near_one, "r"), (mr_query, "r"), (li_key, "r"), (prev_rest, "r"),
         (prev_tail, "r"), (table, "r"), (base_medium, "g"), (rate, "r")],
        [(rows, BF16, "r"), (rows, BF16, "r"), (rows, BF16, "r"), (states, F32, "s"),
         ((6, channels), F32, "r")],
        [EXT, EXT, EXT, wide], heavy,
    )
    next_head = sent(head, -1)
    gathered = exchanged(state)

    near_two, grad_li_key, grad_mr_query = call(
        long_near_body, "long_near", 1024,
        [(prod_two, "r"), (grad_two, "r"), (grad_two_after, "r"), (value_two, "r"),
         (mixed_grad, "r"), (mixed_after, "r"), (conv_one, "r"), (next_head, "r"), (table, "r"),
         (base_long, "g")],
        [(rows, F32, "r"), (rows, BF16, "r"), (rows, BF16, "r")], [EXT, EXT, wide], heavy,
    )
    (near_grad,) = call(
        medium_back_near_body, "medium_back_near", 1024,
        [(conv_grad, "r"), (base_medium_back, "g")],
        [(rows, F32, "r")], [wide], heavy,
    )

    start = exchanged(scan_states(gathered, my_rates, False))

    output, grad_li_query = call(
        long_body, "long_forward", 1024,
        [(near_two, "r"), (start, "s"), (state, "s"), (li_query, "r"), (upstream, "r"),
         (prev_rest, "r"), (next_rest, "r"), (next_head, "r"), (table, "r"), (rate, "r"),
         (residue, "r")],
        [(rows, BF16, "r"), (rows, BF16, "r")], [EXT, EXT], 0,
    )
    grad_mr_key, grad_mr_value = call(
        medium_back_body, "medium_back", 1024,
        [(near_grad, "r"), (after_one, "r"), (after_next, "r"), (mr_key, "r"), (mr_value, "r"),
         (prev_kv, "r"), (next_rest, "r"), (table, "r"), (base_medium_back, "g")],
        [(rows, BF16, "r"), (rows, BF16, "r")], [EXT, EXT, EXT, EXT, wider], heavy,
    )
    return (output, grad_mr_query, grad_mr_key, grad_mr_value, grad_li_query, grad_li_key)


def solution(mesh):
    split = P(("ctx", "ch"), None)
    return jax.shard_map(
        per_device,
        mesh=mesh,
        in_specs=(split,) * 6 + (P(),) * 6,
        out_specs=(split,) * 6,
        check_vma=False,
    )
```

```python
import jax
import jax.numpy as jnp
from jax import lax
from jax.experimental import pallas as pl
from jax.experimental.pallas import tpu as pltpu
from jax.sharding import PartitionSpec as P

GROUP = 16
SHORT = 3
MR_TAPS = 128
MODES = 16
ROWS = 128
LANES = 128
STRIP = 32
STRIPS = ROWS // STRIP
TILE_GROUPS = LANES // GROUP
AXES = ("ctx", "ch")
BF16 = jnp.bfloat16
F32 = jnp.float32
VMEM_LIMIT = 56 * 1024 * 1024

MR_Q, MR_K, MR_V, LI_Q, LI_K, LI_V, SKIP = 0, 3, 6, 9, 12, 15, 18
TABLE_ROWS = 24


def cost(microseconds):
    return pl.CostEstimate(
        flops=0, bytes_accessed=int(microseconds * 3.6e6), transcendentals=0
    )


def lane_call(body, name, channels, ins, outs, scratch, us, part=(0, 1), into=None, width=1024, unroll=2):
    span = channels // part[1]
    width = min(width, span)
    tiles = width // LANES
    blocks = span // width
    into = into or {}

    def spec(shape, kind):
        whole = {"r": shape[-1], "g": shape[0] * GROUP, "s": shape[0] * (LANES // 2)}[kind] == channels
        first = part[0] * blocks if whole else 0
        if kind == "r":
            return pl.BlockSpec((shape[0], width), lambda i: (0, first + i))
        if kind == "g":
            return pl.BlockSpec((width // GROUP, shape[1]), lambda i: (first + i, 0))
        return pl.BlockSpec((2 * tiles, 8, LANES), lambda i: (first + i, 0, 0))

    def view(ref, kind, t):
        if kind == "r":
            return ref.at[:, pl.ds(pl.multiple_of(t * LANES, LANES), LANES)]
        if kind == "g":
            return ref.at[pl.ds(pl.multiple_of(t * TILE_GROUPS, TILE_GROUPS), TILE_GROUPS), :]
        return ref.at[pl.ds(2 * t, 2)]

    kinds = [kind for _, kind in ins] + [kind for _, _, kind in outs]
    count_in, count_out = len(ins), len(outs)

    def kernel(*refs):
        arrays = refs[:count_in] + refs[count_in + len(into) : count_in + len(into) + count_out]
        extra = refs[count_in + len(into) + count_out :]

        def step(k, unused):
            for u in range(unroll):
                t = k * unroll + u
                body(
                    *[view(ref, kind, t) for ref, kind in zip(arrays, kinds)],
                    *[ref.at[u] for ref in extra],
                )
            return unused

        lax.fori_loop(0, tiles // unroll, step, 0)

    return pl.pallas_call(
        kernel,
        name=name,
        grid=(blocks,),
        in_specs=[spec(a.shape, kind) for a, kind in ins]
        + [pl.BlockSpec(memory_space=pl.ANY)] * len(into),
        out_specs=[spec(shape, kind) for shape, _, kind in outs],
        out_shape=[jax.ShapeDtypeStruct(shape, dtype) for shape, dtype, _ in outs],
        scratch_shapes=[pltpu.VMEM((unroll, *shape), dtype) for shape, dtype in scratch],
        input_output_aliases={count_in + n: at for n, at in enumerate(into)},
        compiler_params=pltpu.CompilerParams(vmem_limit_bytes=VMEM_LIMIT),
        cost_estimate=cost(us),
    )(*[a for a, _ in ins], *into.values())


EXT = ((ROWS + 16, LANES), F32)


def turned(x, by):
    return pltpu.roll(x, by, 0) if by else x


def fill(ext, value, prev8=None, next8=None):
    ext[8 : 8 + ROWS, :] = value
    if prev8 is not None:
        ext[0:8, :] = prev8
    if next8 is not None:
        ext[8 + ROWS :, :] = next8


def taps(table, first):
    return [table[first + j : first + j + 1, :] for j in range(SHORT)]


def short_forward(ext, weights, rows=ROWS):
    return (
        weights[0] * ext[8 : 8 + rows, :]
        + weights[1] * ext[7 : 7 + rows, :]
        + weights[2] * ext[6 : 6 + rows, :]
    )


def short_backward(ext, weights):
    return (
        weights[0] * ext[8 : 8 + ROWS, :]
        + weights[1] * ext[9 : 9 + ROWS, :]
        + weights[2] * ext[10 : 10 + ROWS, :]
    )


def iota(shape, dim):
    return lax.broadcasted_iota(jnp.int32, shape, dim)


def circulant(base, g, rows, shift=0):
    row = jnp.broadcast_to(base[g : g + 1, :], (rows, LANES))
    return pltpu.roll(row, shift, 1, stride=1, stride_axis=0)


def pick(products, rows, count):
    columns = LANES // count
    owner = iota((rows, LANES), 1) // columns
    picked = []
    for q in range(products.shape[1] // LANES):
        at = slice(q * LANES, (q + 1) * LANES)
        total = products[0:rows, at]
        for p in range(1, count):
            total = jnp.where(owner == p, products[p * rows : (p + 1) * rows, at], total)
        picked.append(total)
    return jnp.concatenate(picked, 0)


def windows(signal, first, length):
    count = signal.shape[0]
    parts = []
    for q in range(STRIPS):
        low, high = STRIP * q + first, STRIP * q + first + length
        inside = signal[max(low, 0) : min(high, count)]
        pieces = [inside]
        if low < 0:
            pieces.insert(0, jnp.zeros((-low, LANES), signal.dtype))
        if high > count:
            pieces.append(jnp.zeros((high - count, LANES), signal.dtype))
        parts.append(jnp.concatenate(pieces, 0) if len(pieces) > 1 else inside)
    return jnp.concatenate(parts, 1)


def split_groups(signal):
    odd = ((iota(signal.shape, 1) // GROUP) % 2).astype(F32)
    return signal * (1.0 - odd).astype(signal.dtype), signal * odd.astype(signal.dtype)


def long_product(base_ref, signal, tables, backward):
    base = base_ref[...]
    row, lane = iota((STRIP, LANES), 0), iota((STRIP, LANES), 1)
    first = 0 if backward else STRIP - LANES
    keep = lane >= row if backward else lane + first <= row
    for g in range(TILE_GROUPS):
        p, half = g // 2, g % 2
        table = jnp.where(keep, circulant(base, g, STRIP, -first), 0.0).astype(BF16)
        tables[p * STRIP : (p + 1) * STRIP, half * LANES : (half + 1) * LANES] = table
    even, odd = split_groups(signal)
    right = jnp.concatenate([windows(even, first, LANES), windows(odd, first, LANES)], 0)
    return pick(jnp.dot(tables[...], right, preferred_element_type=F32), STRIP, TILE_GROUPS // 2)


def medium_product(base_ref, pair, tables, backward):
    base = base_ref[...]
    row, lane = iota((STRIP, LANES), 0), iota((STRIP, LANES), 1)
    for g in range(TILE_GROUPS):
        whole = circulant(base, g, STRIP)
        keep = lane >= row if backward else lane > row
        rows = slice(g * STRIP, (g + 1) * STRIP)
        tables[rows, 0:LANES] = jnp.where(keep, whole, 0.0).astype(BF16)
        tables[rows, LANES:] = jnp.where(keep, 0.0, whole).astype(BF16)
    products = jnp.dot(tables[...], windows(pair, 0, 2 * LANES), preferred_element_type=F32)
    return pick(products, STRIP, TILE_GROUPS)


def on_channels(base, column):
    own = iota((TILE_GROUPS, LANES), 0) == iota((TILE_GROUPS, LANES), 1) // GROUP
    return jnp.where(own, base[:, column : column + 1], 0.0).sum(0, keepdims=True)


def own_group():
    return (iota((LANES, LANES), 0) // MODES == iota((LANES, LANES), 1) // GROUP).astype(F32)


def spread(state):
    return (jnp.concatenate([state] * TILE_GROUPS, 0) * own_group()).astype(BF16)


def absorb(powers, signal):
    every = lax.dot_general(
        powers.astype(BF16), signal, (((0,), (0,)), ((), ())), preferred_element_type=F32
    )
    return (every * own_group()).reshape(TILE_GROUPS, MODES, LANES).sum(0)


def store_state(ref, state):
    ref[...] = state.reshape(2, 8, LANES)


def load_state(ref):
    return ref[...].reshape(MODES, LANES)


def margins_before(ref):
    rows = ref[...].astype(F32)
    return rows[0:8], rows[8:16]


def margins_after(ref):
    rows = ref[...].astype(F32)
    return rows[0:8], rows[8:16]


def edges(mr_query, mr_key, mr_value, li_query, li_key, upstream):
    channels = mr_query.shape[1]
    width = min(2048, channels)

    def kernel(q_end, k_end, v_end, lq_end, lk_end, lq, lk, g, k, v, last, first, last_kv, a, b):
        a[0:4, :] = k_end[...].astype(F32)[12:16]
        a[4:8, :] = v_end[...].astype(F32)[12:16]
        a[8:12, :] = q_end[...].astype(F32)[12:16]
        a[12:14, :] = lq_end[...].astype(F32)[14:16]
        a[14:16, :] = lk_end[...].astype(F32)[14:16]
        for n, ref in enumerate((lq, lk, g, k, v)):
            b[2 * n : 2 * n + 2, :] = ref[...].astype(F32)[0:2]
        b[10:16, :] = jnp.zeros((6, width), F32)
        last[...] = a[...].astype(BF16)
        first[...] = b[...].astype(BF16)
        last_kv[...] = a[0:8, :].astype(BF16)

    low = pl.BlockSpec((16, width), lambda i: (ROWS // 16 - 1, i))
    high = pl.BlockSpec((16, width), lambda i: (0, i))
    small = jax.ShapeDtypeStruct((16, channels), BF16)
    return pl.pallas_call(
        kernel,
        name="edges",
        grid=(channels // width,),
        in_specs=[low] * 5 + [high] * 5,
        out_specs=[high, high, pl.BlockSpec((8, width), lambda i: (0, i))],
        out_shape=[small, small, jax.ShapeDtypeStruct((8, channels), BF16)],
        scratch_shapes=[pltpu.VMEM((16, width), F32)] * 2,
        compiler_params=pltpu.CompilerParams(vmem_limit_bytes=VMEM_LIMIT),
        cost_estimate=cost(3.5),
    )(mr_query, mr_key, mr_value, li_query, li_key, li_query, li_key, upstream, mr_key, mr_value)


def make_tables(mr_short, li_short, li_skip, mr_filter, li_rate, li_residue):
    groups = mr_filter.shape[1]
    channels = groups * GROUP
    block = min(128, groups)
    width = block * GROUP

    def kernel(mr, li, skip, filters, rate, residue, table, medium, medium_back, long, long_back):
        for n in range(3):
            table[3 * n : 3 * n + 3, :] = mr[n].astype(F32)
            table[9 + 3 * n : 12 + 3 * n, :] = li[n].astype(F32)
        table[SKIP : SKIP + 1, :] = skip[...]
        table[SKIP + 1 :, :] = jnp.zeros((TABLE_ROWS - SKIP - 1, width), F32)
        row, lane = iota((LANES, LANES), 0), iota((LANES, LANES), 1)
        same = (row == lane).astype(F32).astype(BF16)
        turn = (row == (LANES - lane) % LANES).astype(F32).astype(BF16)
        by_rows = (((0,), (0,)), ((), ()))
        medium[...] = lax.dot_general(filters[...], turn, by_rows, preferred_element_type=F32)
        medium_back[...] = lax.dot_general(filters[...], same, by_rows, preferred_element_type=F32)
        position = iota((block, LANES), 1).astype(F32)
        impulse = jnp.zeros((block, LANES), F32)
        for n in range(MODES):
            impulse += residue[:, n : n + 1] * jnp.exp(-rate[:, n : n + 1] * position)
        long_back[...] = impulse
        long[...] = jnp.dot(impulse.astype(BF16), turn, preferred_element_type=F32)

    shorts = pl.BlockSpec((3, 3, width), lambda i: (0, 0, i))
    modes = pl.BlockSpec((block, MODES), lambda i: (i, 0))
    by_tap = pl.BlockSpec((block, LANES), lambda i: (i, 0))
    shapes = [jax.ShapeDtypeStruct((TABLE_ROWS, channels), F32)]
    shapes += [jax.ShapeDtypeStruct((groups, LANES), F32)] * 4
    return pl.pallas_call(
        kernel,
        name="tables",
        grid=(groups // block,),
        in_specs=[
            shorts, shorts, pl.BlockSpec((1, width), lambda i: (0, i)),
            pl.BlockSpec((MR_TAPS, block), lambda i: (0, i)), modes, modes,
        ],
        out_specs=[pl.BlockSpec((TABLE_ROWS, width), lambda i: (0, i))] + [by_tap] * 4,
        out_shape=shapes,
        compiler_params=pltpu.CompilerParams(vmem_limit_bytes=VMEM_LIMIT),
        cost_estimate=cost(5),
    )(mr_short, li_short, li_skip, mr_filter, li_rate, li_residue)


def product_one_body(key, value, prev, table, out, ext_k, ext_v):
    weights = table[...]
    margin, _ = margins_before(prev)
    fill(ext_k, key[...].astype(F32), turned(margin, 4))
    fill(ext_v, value[...].astype(F32), margin)
    keys_one = short_forward(ext_k, taps(weights, MR_K))
    value_one = short_forward(ext_v, taps(weights, MR_V))
    out[...] = (keys_one * value_one).astype(BF16)


def upstream_body(li_query, upstream, prev, table, rate, cotangent, state, ext):
    weights = table[...]
    _, margin = margins_before(prev)
    fill(ext, li_query[...].astype(F32), turned(margin, 2))
    query_two = short_forward(ext, taps(weights, LI_Q))
    rounded = (upstream[...].astype(F32) * query_two).astype(BF16)
    position = iota((ROWS, LANES), 0).astype(F32)
    store_state(state, absorb(jnp.exp(-rate[...] * position), rounded))
    cotangent[...] = rounded


def long_back_near_body(cotangent, table, base, near, tables):
    signal = cotangent[...]
    product = long_product(base, signal, tables, True)
    near[...] = product + table[SKIP : SKIP + 1, :] * signal.astype(F32)


def long_back_body(
    near, closing, li_query, li_key, query, prev, following, table, rate, residue,
    grad_two, grad_two_after, mixed_grad, mixed_head, out_head, out,
    ext_q, ext_k, ext_g, ext_o,
):
    weights = table[...]
    _, before = margins_before(prev)
    after, _ = margins_after(following)
    fill(ext_q, li_query[...].astype(F32), None, after)
    w = taps(weights, LI_Q)
    base = 8 + ROWS
    query_after = (
        w[0] * ext_q[base : base + 8, :]
        + w[1] * ext_q[base - 1 : base + 7, :]
        + w[2] * ext_q[base - 2 : base + 6, :]
    )
    cot_after = turned(after, 4) * query_after
    state = load_state(closing)
    distance = (ROWS - iota((ROWS + 16, LANES), 0)).astype(F32)
    emit = (residue[...] * jnp.exp(-rate[...] * distance)).astype(BF16)
    emitted = jnp.dot(emit, spread(state), preferred_element_type=F32)
    later = jnp.dot(emit[ROWS:], spread(state - cot_after[0:1]), preferred_element_type=F32)
    skip = weights[SKIP : SKIP + 1]
    own = near[...] + emitted[0:ROWS]
    at_row = iota((8, LANES), 0)
    past = jnp.where(at_row == 0, emitted[ROWS : ROWS + 8], later[0:8]) + skip * cot_after
    past = jnp.where(at_row < 2, past, 0.0)
    grad_two[...] = own.astype(BF16)
    grad_two_after[...] = past[0:2]
    fill(ext_k, li_key[...].astype(F32), before, turned(after, 6))
    keys_two = short_forward(ext_k, taps(weights, LI_K), ROWS + 8)
    fill(ext_g, own * keys_two[0:ROWS], None, past * keys_two[ROWS:])
    mixed = short_backward(ext_g, taps(weights, LI_V))
    fill(ext_o, query[...].astype(F32), turned(before, 4))
    conv_grad = mixed * short_forward(ext_o, taps(weights, MR_Q))
    mixed_grad[...] = mixed.astype(BF16)
    mixed_head[...] = mixed[0:2]
    out[...] = conv_grad.astype(BF16)
    out_head[...] = conv_grad[0:1]


def forward_body(
    before, before_kv, signal, query, li_key, prev, table, base_ref, base_long, rate,
    conv_one, value_two, near, state, head, ext_q, ext_k, ext_m, tables, tables_edge, tables_long,
):
    weights = table[...]
    earlier = before[...]
    pair = jnp.concatenate([earlier, signal[...]], 0)
    conv = medium_product(base_ref, pair, tables, False)
    base = base_ref[...]
    row, lane = iota((16, LANES), 0), iota((16, LANES), 1)
    for g in range(TILE_GROUPS):
        whole = circulant(base, g, 16, ROWS - 16)
        tables_edge[g * 16 : (g + 1) * 16, :] = jnp.where(
            lane <= row + (ROWS - 16), whole, 0.0
        ).astype(BF16)
    edge = pick(jnp.dot(tables_edge[...], earlier, preferred_element_type=F32), 16, TILE_GROUPS)
    raw = before_kv[...].astype(F32)
    w_k, w_v = taps(weights, MR_K), taps(weights, MR_V)
    key_last = w_k[0] * raw[3:4] + w_k[1] * raw[2:3] + w_k[2] * raw[1:2]
    value_last = w_v[0] * raw[7:8] + w_v[1] * raw[6:7] + w_v[2] * raw[5:6]
    far = on_channels(base, 1) * (key_last * value_last).astype(BF16).astype(F32)
    conv_before = edge[8:16] + jnp.where(iota((8, LANES), 0) == 6, far, 0.0)
    _, margin = margins_before(prev)
    fill(ext_q, query[...].astype(F32), turned(margin, 4))
    w = taps(weights, MR_Q)
    query_one = short_forward(ext_q, w)
    query_before = w[0] * margin[0:8] + w[1] * turned(margin, 1) + w[2] * turned(margin, 2)
    mixed_before = turned(query_before, 4) * conv_before
    fill(
        ext_m,
        (query_one * conv).astype(BF16).astype(F32),
        mixed_before.astype(BF16).astype(F32),
    )
    value = short_forward(ext_m, taps(weights, LI_V))
    fill(ext_k, li_key[...].astype(F32), margin)
    keys_two = short_forward(ext_k, taps(weights, LI_K))
    product = keys_two * value
    rounded = product.astype(BF16)
    position = (ROWS - 1 - iota((ROWS, LANES), 0)).astype(F32)
    store_state(state, absorb(jnp.exp(-rate[...] * position), rounded))
    conv_one[...] = conv.astype(BF16)
    value_two[...] = value.astype(BF16)
    near[...] = (
        long_product(base_long, rounded, tables_long, False) + weights[SKIP : SKIP + 1] * product
    )
    head[0:2, :] = product[0:2]
    head[2:4, :] = value[0:2]
    head[4:6, :] = conv[0:2]


def long_body(
    near, start, end, li_query, upstream, prev, following, next_head, grad_two, grad_two_after,
    value_two, table, rate, residue, base_back,
    out, grad_li_query, grad_li_key, ext_q, ext_g, ext_k,
):
    weights = table[...]
    distance = (iota((ROWS + 16, LANES), 0) + 1).astype(F32)
    emit = (residue[...] * jnp.exp(-rate[...] * distance)).astype(BF16)
    emitted = jnp.dot(emit, spread(load_state(start)), preferred_element_type=F32)
    conv = near[...] + emitted[0:ROWS]
    _, margin = margins_before(prev)
    fill(ext_q, li_query[...].astype(F32), turned(margin, 2))
    query_two = short_forward(ext_q, taps(weights, LI_Q))
    out[...] = (query_two * conv).astype(BF16)
    ended = jnp.dot(emit[0:16], spread(load_state(end)), preferred_element_type=F32)
    impulse = base_back[...]
    at_once = on_channels(impulse, 0) + weights[SKIP : SKIP + 1]
    first, second = next_head[0:1, :], next_head[1:2, :]
    past = emitted[ROWS : ROWS + 8] + ended[0:8]
    past_first = past[0:1] + at_once * first
    past_second = past[1:2] + on_channels(impulse, 1) * first + at_once * second
    after, _ = margins_after(following)
    fill(ext_g, upstream[...].astype(F32) * conv)
    ext_g[8 + ROWS : 9 + ROWS, :] = after[4:5] * past_first
    ext_g[9 + ROWS : 10 + ROWS, :] = after[5:6] * past_second
    grad_li_query[...] = short_backward(ext_g, taps(weights, LI_Q)).astype(BF16)
    fill(ext_k, grad_two[...].astype(F32) * value_two[...].astype(F32))
    ext_k[8 + ROWS : 10 + ROWS, :] = grad_two_after[...] * next_head[2:4, :]
    grad_li_key[...] = short_backward(ext_k, taps(weights, LI_K)).astype(BF16)


def medium_back_body(
    conv_grad, after, after_next, key, value, prev, following, mixed_grad, mixed_after,
    conv_one, next_head, table, base_ref,
    grad_query, grad_key, grad_value, ext_k, ext_v, ext_gk, ext_gv, ext_q, tables,
):
    weights = table[...]
    later = after[...]
    pair = jnp.concatenate([conv_grad[...], later], 0)
    grad = medium_product(base_ref, pair, tables, True)
    left = jnp.concatenate(
        [tables[g * STRIP : g * STRIP + 16, 0:LANES] for g in range(TILE_GROUPS)], 0
    )
    edge = pick(jnp.dot(left, later, preferred_element_type=F32), 16, TILE_GROUPS)
    far = on_channels(base_ref[...], MR_TAPS - 1) * after_next[...].astype(BF16).astype(F32)
    past = edge[0:8] + jnp.where(iota((8, LANES), 0) == 1, far, 0.0)
    before, _ = margins_before(prev)
    next_a, next_b = margins_after(following)
    fill(ext_k, key[...].astype(F32), turned(before, 4), turned(next_a, 2))
    fill(ext_v, value[...].astype(F32), before, next_b)
    keys_one = short_forward(ext_k, taps(weights, MR_K), ROWS + 8)
    value_one = short_forward(ext_v, taps(weights, MR_V), ROWS + 8)
    fill(ext_gk, grad * value_one[0:ROWS], None, past * value_one[ROWS:])
    fill(ext_gv, grad * keys_one[0:ROWS], None, past * keys_one[ROWS:])
    grad_key[...] = short_backward(ext_gk, taps(weights, MR_K)).astype(BF16)
    grad_value[...] = short_backward(ext_gv, taps(weights, MR_V)).astype(BF16)
    fill(ext_q, mixed_grad[...].astype(F32) * conv_one[...].astype(F32))
    ext_q[8 + ROWS : 10 + ROWS, :] = mixed_after[...] * next_head[4:6, :]
    grad_query[...] = short_backward(ext_q, taps(weights, MR_Q)).astype(BF16)


def scan_states(states, rates, backward):
    count = states.shape[0]

    def kernel(states_ref, rates_ref, out_ref):
        decay = jnp.exp(rates_ref[...] * (-float(ROWS)))

        def step(k, carried):
            b = count - 1 - k if backward else k
            out_ref[b] = carried
            return decay * carried + states_ref[b]

        lax.fori_loop(0, count, step, jnp.zeros((8, LANES), F32), unroll=8)

    out_shape = jax.ShapeDtypeStruct(states.shape, F32)
    return pl.pallas_call(
        kernel,
        name="scan_back" if backward else "scan_forward",
        out_shape=out_shape,
        in_specs=[pl.BlockSpec(memory_space=pltpu.VMEM)] * 2,
        out_specs=pl.BlockSpec(memory_space=pltpu.VMEM),
        cost_estimate=cost(2),
    )(states, rates)


def sent(array, by):
    size = lax.axis_size(AXES)
    pairs = [(i, i + by) for i in range(size) if 0 <= i + by < size]
    return lax.ppermute(array, AXES, pairs)


def exchanged(array):
    return lax.all_to_all(array, AXES, split_axis=0, concat_axis=0, tiled=True)


def after(array, *others):
    return lax.optimization_barrier((array, *others))[0]


def per_device(
    mr_query, mr_key, mr_value, li_query, li_key, upstream,
    mr_short, li_short, mr_filter, li_rate, li_residue, li_skip,
):
    channels = mr_query.shape[1]
    tiles = channels // LANES
    assert mr_query.shape[0] == ROWS and lax.axis_size(AXES) == 2 * tiles
    rows = (ROWS, channels)
    full, full32 = (rows, BF16, "r"), (rows, F32, "r")
    half = ((ROWS, channels // 2), BF16, "r")
    state_out = ((2 * tiles, 8, LANES), F32, "s")
    halves = ((0, 2), (1, 2))

    def few(n):
        return ((n, channels), F32, "r")

    last_rows, first_rows, last_kv = edges(mr_query, mr_key, mr_value, li_query, li_key, upstream)
    prev = sent(last_rows, 1)
    following = sent(first_rows, -1)
    before_kv = sent(last_kv, 2)

    table, medium, medium_turned, long, long_turned = make_tables(
        mr_short, li_short, li_skip[None, :], mr_filter, li_rate, li_residue
    )
    rate = li_rate.reshape(1, channels)
    residue = li_residue.reshape(1, channels)
    me = lax.axis_index(AXES)
    my_rates = lax.dynamic_slice(
        li_rate, ((me // 2) * TILE_GROUPS, (me % 2) * 8), (TILE_GROUPS, 8)
    )
    my_rates = jnp.repeat(my_rates.T, GROUP, axis=1)

    tables_long = ((TILE_GROUPS // 2 * STRIP, 2 * LANES), BF16)
    tables_medium = ((TILE_GROUPS * STRIP, 2 * LANES), BF16)
    tables_edge = ((TILE_GROUPS * 16, LANES), BF16)

    cotangent, state_back = lane_call(
        upstream_body, "upstream", channels,
        [(li_query, "r"), (upstream, "r"), (prev, "r"), (table, "r"), (rate, "r")],
        [full, state_out], [EXT], 7,
    )
    gathered_back = after(exchanged(state_back), following, before_kv)
    signal_one = [
        lane_call(
            product_one_body, "product_one", channels,
            [(mr_key, "r"), (mr_value, "r"), (prev, "r"), (table, "r")],
            [half], [EXT, EXT], 4, part,
        )[0]
        for part in halves
    ]
    (near_back,) = lane_call(
        long_back_near_body, "long_back_near", channels,
        [(cotangent, "r"), (table, "r"), (long_turned, "g")],
        [full32], [tables_long], 6,
    )
    closing = exchanged(scan_states(gathered_back, my_rates, True))
    before_one = [sent(after(signal, closing), 1) for signal in signal_one]

    outs = [full, few(2), full, few(2), few(1), half]
    into = {}
    conv_grad = []
    for part in halves:
        got = lane_call(
            long_back_body, "long_back", channels,
            [(near_back, "r"), (closing, "s"), (li_query, "r"), (li_key, "r"), (mr_query, "r"),
             (prev, "r"), (following, "r"), (table, "r"), (rate, "r"), (residue, "r")],
            outs, [EXT, EXT, EXT, EXT], 6.5, part, into,
        )
        conv_grad.append(got[5])
        into = dict(enumerate(got[:5]))
    grad_two, grad_two_after, mixed_grad, mixed_head, conv_head, _ = got
    after_one = [sent(signal, -1) for signal in conv_grad]
    mixed_after = sent(mixed_head, -1)
    after_next = sent(conv_head, -2)

    into = {}
    for n, part in enumerate(halves):
        got = lane_call(
            forward_body, "forward", channels,
            [(before_one[n], "r"), (before_kv, "r"), (signal_one[n], "r"), (mr_query, "r"),
             (li_key, "r"), (prev, "r"), (table, "r"), (medium, "g"), (long, "g"), (rate, "r")],
            [full, full, full32, state_out, few(6)],
            [EXT, EXT, EXT, tables_medium, tables_edge, tables_long], 15, part, into,
        )
        into = dict(enumerate(got))
    conv_one, value_two, near, state, head = got
    next_head = sent(head, -1)
    start = exchanged(scan_states(exchanged(state), my_rates, False))

    output, grad_li_query, grad_li_key = lane_call(
        long_body, "long_forward", channels,
        [(near, "r"), (start, "s"), (state, "s"), (li_query, "r"), (upstream, "r"), (prev, "r"),
         (following, "r"), (next_head, "r"), (grad_two, "r"), (grad_two_after, "r"),
         (value_two, "r"), (table, "r"), (rate, "r"), (residue, "r"), (long_turned, "g")],
        [full, full, full], [EXT, EXT, EXT], 14,
    )
    into = {}
    for n, part in enumerate(halves):
        got = lane_call(
            medium_back_body, "medium_back", channels,
            [(conv_grad[n], "r"), (after_one[n], "r"), (after_next, "r"), (mr_key, "r"),
             (mr_value, "r"), (prev, "r"), (following, "r"), (mixed_grad, "r"),
             (mixed_after, "r"), (conv_one, "r"), (next_head, "r"), (table, "r"),
             (medium_turned, "g")],
            [full, full, full], [EXT, EXT, EXT, EXT, EXT, tables_medium], 8.5, part, into,
        )
        into = dict(enumerate(got))
    grad_mr_query, grad_mr_key, grad_mr_value = got
    return (output, grad_mr_query, grad_mr_key, grad_mr_value, grad_li_query, grad_li_key)


def solution(mesh):
    split = P(("ctx", "ch"), None)
    return jax.shard_map(
        per_device,
        mesh=mesh,
        in_specs=(split,) * 6 + (P(),) * 6,
        out_specs=(split,) * 6,
        check_vma=False,
    )
```

```python
import jax
import jax.numpy as jnp
from jax import lax
from jax.experimental import pallas as pl
from jax.experimental.pallas import tpu as pltpu
from jax.sharding import PartitionSpec as P

GROUP = 16
SHORT = 3
MR_TAPS = 128
MODES = 16
ROWS = 128
LANES = 128
STRIP = 32
STRIPS = ROWS // STRIP
TILE_GROUPS = LANES // GROUP
AXES = ("ctx", "ch")
BF16 = jnp.bfloat16
F32 = jnp.float32
VMEM_LIMIT = 56 * 1024 * 1024

MR_Q, MR_K, MR_V, LI_Q, LI_K, LI_V, SKIP = 0, 3, 6, 9, 12, 15, 18
TABLE_ROWS = 24


def cost(microseconds):
    return pl.CostEstimate(
        flops=0, bytes_accessed=int(microseconds * 3.6e6), transcendentals=0
    )


def hint(start, of):
    return start if isinstance(start, int) else pl.multiple_of(start, of)


def lane_call(body, name, channels, ins, outs, scratch, us, part=(0, 1), into=None, width=1024, unroll=8):
    span = channels // part[1]
    width = min(width, span)
    tiles = width // LANES
    unroll = min(unroll, tiles)
    blocks = span // width
    into = into or {}

    def spec(shape, kind):
        whole = {"r": shape[-1], "g": shape[0] * GROUP, "s": shape[0] * (LANES // 2)}[kind] == channels
        first = part[0] * blocks if whole else 0
        if kind == "r":
            return pl.BlockSpec((shape[0], width), lambda i: (0, first + i))
        if kind == "g":
            return pl.BlockSpec((width // GROUP, shape[1]), lambda i: (first + i, 0))
        return pl.BlockSpec((2 * tiles, 8, LANES), lambda i: (first + i, 0, 0))

    def view(ref, kind, t):
        if kind == "r":
            return ref.at[:, pl.ds(hint(t * LANES, LANES), LANES)]
        if kind == "g":
            return ref.at[pl.ds(hint(t * TILE_GROUPS, TILE_GROUPS), TILE_GROUPS), :]
        return ref.at[pl.ds(2 * t, 2)]

    kinds = [kind for _, kind in ins] + [kind for _, _, kind in outs]
    count_in, count_out = len(ins), len(outs)

    def kernel(*refs):
        arrays = refs[:count_in] + refs[count_in + len(into) : count_in + len(into) + count_out]
        extra = refs[count_in + len(into) + count_out :]

        def step(k, unused):
            for u in range(unroll):
                t = u if unroll == tiles else k * unroll + u
                body(
                    *[view(ref, kind, t) for ref, kind in zip(arrays, kinds)],
                    *[ref.at[u] for ref in extra],
                )
            return unused

        if unroll == tiles:
            step(0, 0)
        else:
            lax.fori_loop(0, tiles // unroll, step, 0)

    return pl.pallas_call(
        kernel,
        name=name,
        grid=(blocks,),
        in_specs=[spec(a.shape, kind) for a, kind in ins]
        + [pl.BlockSpec(memory_space=pl.ANY)] * len(into),
        out_specs=[spec(shape, kind) for shape, _, kind in outs],
        out_shape=[jax.ShapeDtypeStruct(shape, dtype) for shape, dtype, _ in outs],
        scratch_shapes=[pltpu.VMEM((unroll, *shape), dtype) for shape, dtype in scratch],
        input_output_aliases={count_in + n: at for n, at in enumerate(into)},
        compiler_params=pltpu.CompilerParams(vmem_limit_bytes=VMEM_LIMIT),
        cost_estimate=cost(us),
    )(*[a for a, _ in ins], *into.values())


EXT = ((ROWS + 16, LANES), F32)


def turned(x, by):
    return pltpu.roll(x, by, 0) if by else x


def fill(ext, value, prev8=None, next8=None):
    ext[8 : 8 + ROWS, :] = value
    if prev8 is not None:
        ext[0:8, :] = prev8
    if next8 is not None:
        ext[8 + ROWS :, :] = next8


def taps(table, first):
    return [table[first + j : first + j + 1, :] for j in range(SHORT)]


def short_forward(ext, weights, rows=ROWS):
    return (
        weights[0] * ext[8 : 8 + rows, :]
        + weights[1] * ext[7 : 7 + rows, :]
        + weights[2] * ext[6 : 6 + rows, :]
    )


def short_backward(ext, weights):
    return (
        weights[0] * ext[8 : 8 + ROWS, :]
        + weights[1] * ext[9 : 9 + ROWS, :]
        + weights[2] * ext[10 : 10 + ROWS, :]
    )


def iota(shape, dim):
    return lax.broadcasted_iota(jnp.int32, shape, dim)


def circulant(base, g, rows, shift=0):
    row = jnp.broadcast_to(base[g : g + 1, :], (rows, LANES))
    return pltpu.roll(row, shift, 1, stride=1, stride_axis=0)


def pick(products, rows, count):
    columns = LANES // count
    owner = iota((rows, LANES), 1) // columns
    picked = []
    for q in range(products.shape[1] // LANES):
        at = slice(q * LANES, (q + 1) * LANES)
        total = products[0:rows, at]
        for p in range(1, count):
            total = jnp.where(owner == p, products[p * rows : (p + 1) * rows, at], total)
        picked.append(total)
    return jnp.concatenate(picked, 0)


def windows(signal, first, length):
    count = signal.shape[0]
    parts = []
    for q in range(STRIPS):
        low, high = STRIP * q + first, STRIP * q + first + length
        inside = signal[max(low, 0) : min(high, count)]
        pieces = [inside]
        if low < 0:
            pieces.insert(0, jnp.zeros((-low, LANES), signal.dtype))
        if high > count:
            pieces.append(jnp.zeros((high - count, LANES), signal.dtype))
        parts.append(jnp.concatenate(pieces, 0) if len(pieces) > 1 else inside)
    return jnp.concatenate(parts, 1)


def split_groups(signal):
    odd = ((iota(signal.shape, 1) // GROUP) % 2).astype(F32)
    return signal * (1.0 - odd).astype(signal.dtype), signal * odd.astype(signal.dtype)


def long_product(base_ref, signal, backward):
    base = base_ref[...]
    row, lane = iota((STRIP, LANES), 0), iota((STRIP, LANES), 1)
    first = 0 if backward else STRIP - LANES
    keep = lane >= row if backward else lane + first <= row
    tables = [
        jnp.where(keep, circulant(base, g, STRIP, -first), 0.0).astype(BF16)
        for g in range(TILE_GROUPS)
    ]
    left = jnp.concatenate(
        [jnp.concatenate(tables[0::2], 0), jnp.concatenate(tables[1::2], 0)], 1
    )
    even, odd = split_groups(signal)
    right = jnp.concatenate([windows(even, first, LANES), windows(odd, first, LANES)], 0)
    return pick(jnp.dot(left, right, preferred_element_type=F32), STRIP, TILE_GROUPS // 2)


def medium_product(base_ref, pair, backward):
    base = base_ref[...]
    row, lane = iota((STRIP, LANES), 0), iota((STRIP, LANES), 1)
    keep = lane >= row if backward else lane > row
    wholes = [circulant(base, g, STRIP) for g in range(TILE_GROUPS)]
    first = [jnp.where(keep, whole, 0.0).astype(BF16) for whole in wholes]
    second = [jnp.where(keep, 0.0, whole).astype(BF16) for whole in wholes]
    left = jnp.concatenate([jnp.concatenate(first, 0), jnp.concatenate(second, 0)], 1)
    products = jnp.dot(left, windows(pair, 0, 2 * LANES), preferred_element_type=F32)
    return pick(products, STRIP, TILE_GROUPS), first


def on_channels(base, column):
    own = iota((TILE_GROUPS, LANES), 0) == iota((TILE_GROUPS, LANES), 1) // GROUP
    return jnp.where(own, base[:, column : column + 1], 0.0).sum(0, keepdims=True)


def own_group():
    return (iota((LANES, LANES), 0) // MODES == iota((LANES, LANES), 1) // GROUP).astype(F32)


def spread(state):
    return (jnp.concatenate([state] * TILE_GROUPS, 0) * own_group()).astype(BF16)


def absorb(powers, signal):
    every = lax.dot_general(
        powers.astype(BF16), signal, (((0,), (0,)), ((), ())), preferred_element_type=F32
    )
    return (every * own_group()).reshape(TILE_GROUPS, MODES, LANES).sum(0)


def store_state(ref, state):
    ref[...] = state.reshape(2, 8, LANES)


def load_state(ref):
    return ref[...].reshape(MODES, LANES)


def margins_before(ref):
    rows = ref[...].astype(F32)
    return rows[0:8], rows[8:16]


def margins_after(ref):
    rows = ref[...].astype(F32)
    return rows[0:8], rows[8:16]


def edges(mr_query, mr_key, mr_value, li_query, li_key, upstream):
    channels = mr_query.shape[1]
    width = min(2048, channels)

    def kernel(q_end, k_end, v_end, lq_end, lk_end, lq, lk, g, k, v, last, first, last_kv, a, b):
        a[0:4, :] = k_end[...].astype(F32)[12:16]
        a[4:8, :] = v_end[...].astype(F32)[12:16]
        a[8:12, :] = q_end[...].astype(F32)[12:16]
        a[12:14, :] = lq_end[...].astype(F32)[14:16]
        a[14:16, :] = lk_end[...].astype(F32)[14:16]
        for n, ref in enumerate((lq, lk, g, k, v)):
            b[2 * n : 2 * n + 2, :] = ref[...].astype(F32)[0:2]
        b[10:16, :] = jnp.zeros((6, width), F32)
        last[...] = a[...].astype(BF16)
        first[...] = b[...].astype(BF16)
        last_kv[...] = a[0:8, :].astype(BF16)

    low = pl.BlockSpec((16, width), lambda i: (ROWS // 16 - 1, i))
    high = pl.BlockSpec((16, width), lambda i: (0, i))
    small = jax.ShapeDtypeStruct((16, channels), BF16)
    return pl.pallas_call(
        kernel,
        name="edges",
        grid=(channels // width,),
        in_specs=[low] * 5 + [high] * 5,
        out_specs=[high, high, pl.BlockSpec((8, width), lambda i: (0, i))],
        out_shape=[small, small, jax.ShapeDtypeStruct((8, channels), BF16)],
        scratch_shapes=[pltpu.VMEM((16, width), F32)] * 2,
        compiler_params=pltpu.CompilerParams(vmem_limit_bytes=VMEM_LIMIT),
        cost_estimate=cost(3.5),
    )(mr_query, mr_key, mr_value, li_query, li_key, li_query, li_key, upstream, mr_key, mr_value)


def make_tables(mr_short, li_short, li_skip, mr_filter, li_rate, li_residue):
    groups = mr_filter.shape[1]
    channels = groups * GROUP
    block = min(128, groups)
    width = block * GROUP

    def kernel(mr, li, skip, filters, rate, residue, table, medium, medium_back, long, long_back):
        for n in range(3):
            table[3 * n : 3 * n + 3, :] = mr[n].astype(F32)
            table[9 + 3 * n : 12 + 3 * n, :] = li[n].astype(F32)
        table[SKIP : SKIP + 1, :] = skip[...]
        table[SKIP + 1 :, :] = jnp.zeros((TABLE_ROWS - SKIP - 1, width), F32)
        row, lane = iota((LANES, LANES), 0), iota((LANES, LANES), 1)
        same = (row == lane).astype(F32).astype(BF16)
        turn = (row == (LANES - lane) % LANES).astype(F32).astype(BF16)
        by_rows = (((0,), (0,)), ((), ()))
        medium[...] = lax.dot_general(filters[...], turn, by_rows, preferred_element_type=F32)
        medium_back[...] = lax.dot_general(filters[...], same, by_rows, preferred_element_type=F32)
        position = iota((block, LANES), 1).astype(F32)
        impulse = jnp.zeros((block, LANES), F32)
        for n in range(MODES):
            impulse += residue[:, n : n + 1] * jnp.exp(-rate[:, n : n + 1] * position)
        long_back[...] = impulse
        long[...] = jnp.dot(impulse.astype(BF16), turn, preferred_element_type=F32)

    shorts = pl.BlockSpec((3, 3, width), lambda i: (0, 0, i))
    modes = pl.BlockSpec((block, MODES), lambda i: (i, 0))
    by_tap = pl.BlockSpec((block, LANES), lambda i: (i, 0))
    shapes = [jax.ShapeDtypeStruct((TABLE_ROWS, channels), F32)]
    shapes += [jax.ShapeDtypeStruct((groups, LANES), F32)] * 4
    return pl.pallas_call(
        kernel,
        name="tables",
        grid=(groups // block,),
        in_specs=[
            shorts, shorts, pl.BlockSpec((1, width), lambda i: (0, i)),
            pl.BlockSpec((MR_TAPS, block), lambda i: (0, i)), modes, modes,
        ],
        out_specs=[pl.BlockSpec((TABLE_ROWS, width), lambda i: (0, i))] + [by_tap] * 4,
        out_shape=shapes,
        compiler_params=pltpu.CompilerParams(vmem_limit_bytes=VMEM_LIMIT),
        cost_estimate=cost(5),
    )(mr_short, li_short, li_skip, mr_filter, li_rate, li_residue)


def product_one_body(key, value, prev, table, out, ext_k, ext_v):
    weights = table[...]
    margin, _ = margins_before(prev)
    fill(ext_k, key[...].astype(F32), turned(margin, 4))
    fill(ext_v, value[...].astype(F32), margin)
    keys_one = short_forward(ext_k, taps(weights, MR_K))
    value_one = short_forward(ext_v, taps(weights, MR_V))
    out[...] = (keys_one * value_one).astype(BF16)


def upstream_body(li_query, upstream, prev, table, rate, cotangent, state, ext):
    weights = table[...]
    _, margin = margins_before(prev)
    fill(ext, li_query[...].astype(F32), turned(margin, 2))
    query_two = short_forward(ext, taps(weights, LI_Q))
    rounded = (upstream[...].astype(F32) * query_two).astype(BF16)
    position = iota((ROWS, LANES), 0).astype(F32)
    store_state(state, absorb(jnp.exp(-rate[...] * position), rounded))
    cotangent[...] = rounded


def long_back_near_body(cotangent, table, base, near):
    signal = cotangent[...]
    product = long_product(base, signal, True)
    near[...] = product + table[SKIP : SKIP + 1, :] * signal.astype(F32)


def long_back_body(
    near, closing, li_query, li_key, query, prev, following, table, rate, residue,
    grad_two, grad_two_after, mixed_grad, mixed_head, out_head, out,
    ext_q, ext_k, ext_g, ext_o,
):
    weights = table[...]
    _, before = margins_before(prev)
    after, _ = margins_after(following)
    fill(ext_q, li_query[...].astype(F32), None, after)
    w = taps(weights, LI_Q)
    base = 8 + ROWS
    query_after = (
        w[0] * ext_q[base : base + 8, :]
        + w[1] * ext_q[base - 1 : base + 7, :]
        + w[2] * ext_q[base - 2 : base + 6, :]
    )
    cot_after = turned(after, 4) * query_after
    state = load_state(closing)
    distance = (ROWS - iota((ROWS + 16, LANES), 0)).astype(F32)
    emit = (residue[...] * jnp.exp(-rate[...] * distance)).astype(BF16)
    emitted = jnp.dot(emit, spread(state), preferred_element_type=F32)
    later = jnp.dot(emit[ROWS:], spread(state - cot_after[0:1]), preferred_element_type=F32)
    skip = weights[SKIP : SKIP + 1]
    own = near[...] + emitted[0:ROWS]
    at_row = iota((8, LANES), 0)
    past = jnp.where(at_row == 0, emitted[ROWS : ROWS + 8], later[0:8]) + skip * cot_after
    past = jnp.where(at_row < 2, past, 0.0)
    grad_two[...] = own.astype(BF16)
    grad_two_after[...] = past[0:2]
    fill(ext_k, li_key[...].astype(F32), before, turned(after, 6))
    keys_two = short_forward(ext_k, taps(weights, LI_K), ROWS + 8)
    fill(ext_g, own * keys_two[0:ROWS], None, past * keys_two[ROWS:])
    mixed = short_backward(ext_g, taps(weights, LI_V))
    fill(ext_o, query[...].astype(F32), turned(before, 4))
    conv_grad = mixed * short_forward(ext_o, taps(weights, MR_Q))
    mixed_grad[...] = mixed.astype(BF16)
    mixed_head[...] = mixed[0:2]
    out[...] = conv_grad.astype(BF16)
    out_head[...] = conv_grad[0:1]


def forward_body(
    before, before_kv, signal, query, li_key, prev, mixed_head, table, base_ref, base_long, rate,
    conv_one, value_two, near, state, head, ext_q, ext_k, ext_m,
):
    weights = table[...]
    earlier = before[...]
    pair = jnp.concatenate([earlier, signal[...]], 0)
    conv, _ = medium_product(base_ref, pair, False)
    base = base_ref[...]
    row, lane = iota((16, LANES), 0), iota((16, LANES), 1)
    left = jnp.concatenate(
        [
            jnp.where(lane <= row + (ROWS - 16), circulant(base, g, 16, ROWS - 16), 0.0).astype(BF16)
            for g in range(TILE_GROUPS)
        ],
        0,
    )
    edge = pick(jnp.dot(left, earlier, preferred_element_type=F32), 16, TILE_GROUPS)
    raw = before_kv[...].astype(F32)
    w_k, w_v = taps(weights, MR_K), taps(weights, MR_V)
    key_last = w_k[0] * raw[3:4] + w_k[1] * raw[2:3] + w_k[2] * raw[1:2]
    value_last = w_v[0] * raw[7:8] + w_v[1] * raw[6:7] + w_v[2] * raw[5:6]
    far = on_channels(base, 1) * (key_last * value_last).astype(BF16).astype(F32)
    conv_before = edge[8:16] + jnp.where(iota((8, LANES), 0) == 6, far, 0.0)
    _, margin = margins_before(prev)
    fill(ext_q, query[...].astype(F32), turned(margin, 4))
    w = taps(weights, MR_Q)
    query_one = short_forward(ext_q, w)
    query_before = w[0] * margin[0:8] + w[1] * turned(margin, 1) + w[2] * turned(margin, 2)
    mixed_before = turned(query_before, 4) * conv_before
    fill(
        ext_m,
        (query_one * conv).astype(BF16).astype(F32),
        mixed_before.astype(BF16).astype(F32),
    )
    value = short_forward(ext_m, taps(weights, LI_V))
    fill(ext_k, li_key[...].astype(F32), margin)
    keys_two = short_forward(ext_k, taps(weights, LI_K))
    product = keys_two * value
    rounded = product.astype(BF16)
    position = (ROWS - 1 - iota((ROWS, LANES), 0)).astype(F32)
    store_state(state, absorb(jnp.exp(-rate[...] * position), rounded))
    conv_one[...] = conv.astype(BF16)
    value_two[...] = value.astype(BF16)
    near[...] = (
        long_product(base_long, rounded, False) + weights[SKIP : SKIP + 1] * product
    )
    head[0:2, :] = product[0:2]
    head[2:4, :] = value[0:2]
    head[4:6, :] = conv[0:2]
    head[6:8, :] = mixed_head[...]


def long_body(
    near, start, end, li_query, upstream, prev, following, next_head, grad_two, grad_two_after,
    value_two, mixed_grad, conv_one, table, rate, residue, base_back,
    out, grad_li_query, grad_li_key, grad_mr_query, ext_q, ext_g, ext_k, ext_m,
):
    weights = table[...]
    distance = (iota((ROWS + 16, LANES), 0) + 1).astype(F32)
    emit = (residue[...] * jnp.exp(-rate[...] * distance)).astype(BF16)
    emitted = jnp.dot(emit, spread(load_state(start)), preferred_element_type=F32)
    conv = near[...] + emitted[0:ROWS]
    _, margin = margins_before(prev)
    fill(ext_q, li_query[...].astype(F32), turned(margin, 2))
    query_two = short_forward(ext_q, taps(weights, LI_Q))
    out[...] = (query_two * conv).astype(BF16)
    ended = jnp.dot(emit[0:16], spread(load_state(end)), preferred_element_type=F32)
    impulse = base_back[...]
    at_once = on_channels(impulse, 0) + weights[SKIP : SKIP + 1]
    first, second = next_head[0:1, :], next_head[1:2, :]
    past = emitted[ROWS : ROWS + 8] + ended[0:8]
    past_first = past[0:1] + at_once * first
    past_second = past[1:2] + on_channels(impulse, 1) * first + at_once * second
    after, _ = margins_after(following)
    fill(ext_g, upstream[...].astype(F32) * conv)
    ext_g[8 + ROWS : 9 + ROWS, :] = after[4:5] * past_first
    ext_g[9 + ROWS : 10 + ROWS, :] = after[5:6] * past_second
    grad_li_query[...] = short_backward(ext_g, taps(weights, LI_Q)).astype(BF16)
    fill(ext_k, grad_two[...].astype(F32) * value_two[...].astype(F32))
    ext_k[8 + ROWS : 10 + ROWS, :] = grad_two_after[...] * next_head[2:4, :]
    grad_li_key[...] = short_backward(ext_k, taps(weights, LI_K)).astype(BF16)
    fill(ext_m, mixed_grad[...].astype(F32) * conv_one[...].astype(F32))
    ext_m[8 + ROWS : 10 + ROWS, :] = next_head[6:8, :] * next_head[4:6, :]
    grad_mr_query[...] = short_backward(ext_m, taps(weights, MR_Q)).astype(BF16)


def medium_back_body(
    conv_grad, after, after_next, key, value, prev, following, table, base_ref,
    grad_key, grad_value, ext_k, ext_v, ext_gk, ext_gv,
):
    weights = table[...]
    later = after[...]
    pair = jnp.concatenate([conv_grad[...], later], 0)
    grad, first_half = medium_product(base_ref, pair, True)
    left = jnp.concatenate([part[0:16] for part in first_half], 0)
    edge = pick(jnp.dot(left, later, preferred_element_type=F32), 16, TILE_GROUPS)
    far = on_channels(base_ref[...], MR_TAPS - 1) * after_next[...].astype(BF16).astype(F32)
    past = edge[0:8] + jnp.where(iota((8, LANES), 0) == 1, far, 0.0)
    before, _ = margins_before(prev)
    next_a, next_b = margins_after(following)
    fill(ext_k, key[...].astype(F32), turned(before, 4), turned(next_a, 2))
    fill(ext_v, value[...].astype(F32), before, next_b)
    keys_one = short_forward(ext_k, taps(weights, MR_K), ROWS + 8)
    value_one = short_forward(ext_v, taps(weights, MR_V), ROWS + 8)
    fill(ext_gk, grad * value_one[0:ROWS], None, past * value_one[ROWS:])
    fill(ext_gv, grad * keys_one[0:ROWS], None, past * keys_one[ROWS:])
    grad_key[...] = short_backward(ext_gk, taps(weights, MR_K)).astype(BF16)
    grad_value[...] = short_backward(ext_gv, taps(weights, MR_V)).astype(BF16)


def scan_states(states, rates, backward):
    count = states.shape[0]

    def kernel(states_ref, rates_ref, out_ref):
        decay = jnp.exp(rates_ref[...] * (-float(ROWS)))

        def step(k, carried):
            b = count - 1 - k if backward else k
            out_ref[b] = carried
            return decay * carried + states_ref[b]

        lax.fori_loop(0, count, step, jnp.zeros((8, LANES), F32), unroll=8)

    out_shape = jax.ShapeDtypeStruct(states.shape, F32)
    return pl.pallas_call(
        kernel,
        name="scan_back" if backward else "scan_forward",
        out_shape=out_shape,
        in_specs=[pl.BlockSpec(memory_space=pltpu.VMEM)] * 2,
        out_specs=pl.BlockSpec(memory_space=pltpu.VMEM),
        cost_estimate=cost(2),
    )(states, rates)


def sent(array, by):
    size = lax.axis_size(AXES)
    pairs = [(i, i + by) for i in range(size) if 0 <= i + by < size]
    return lax.ppermute(array, AXES, pairs)


def exchanged(array):
    return lax.all_to_all(array, AXES, split_axis=0, concat_axis=0, tiled=True)


def after(array, *others):
    return lax.optimization_barrier((array, *others))[0]


def per_device(
    mr_query, mr_key, mr_value, li_query, li_key, upstream,
    mr_short, li_short, mr_filter, li_rate, li_residue, li_skip,
):
    channels = mr_query.shape[1]
    tiles = channels // LANES
    assert mr_query.shape[0] == ROWS and lax.axis_size(AXES) == 2 * tiles
    rows = (ROWS, channels)
    full, full32 = (rows, BF16, "r"), (rows, F32, "r")
    half = ((ROWS, channels // 2), BF16, "r")
    state_out = ((2 * tiles, 8, LANES), F32, "s")
    halves = ((0, 2), (1, 2))

    def few(n):
        return ((n, channels), F32, "r")

    last_rows, first_rows, last_kv = edges(mr_query, mr_key, mr_value, li_query, li_key, upstream)
    prev = sent(last_rows, 1)
    following = sent(first_rows, -1)
    before_kv = sent(last_kv, 2)

    table, medium, medium_turned, long, long_turned = make_tables(
        mr_short, li_short, li_skip[None, :], mr_filter, li_rate, li_residue
    )
    rate = li_rate.reshape(1, channels)
    residue = li_residue.reshape(1, channels)
    me = lax.axis_index(AXES)
    my_rates = lax.dynamic_slice(
        li_rate, ((me // 2) * TILE_GROUPS, (me % 2) * 8), (TILE_GROUPS, 8)
    )
    my_rates = jnp.repeat(my_rates.T, GROUP, axis=1)

    cotangent, state_back = lane_call(
        upstream_body, "upstream", channels,
        [(li_query, "r"), (upstream, "r"), (prev, "r"), (table, "r"), (rate, "r")],
        [full, state_out], [EXT], 7,
    )
    gathered_back = exchanged(state_back)
    (near_back,) = lane_call(
        long_back_near_body, "long_back_near", channels,
        [(cotangent, "r"), (table, "r"), (long_turned, "g")],
        [full32], [], 6, unroll=4,
    )
    gathered_back = after(gathered_back, following, before_kv, near_back)
    signal_one = [
        lane_call(
            product_one_body, "product_one", channels,
            [(mr_key, "r"), (mr_value, "r"), (prev, "r"), (table, "r")],
            [half], [EXT, EXT], 3, part,
        )[0]
        for part in halves
    ]
    closing = exchanged(scan_states(gathered_back, my_rates, True))
    before_one = [sent(after(signal, closing), 1) for signal in signal_one]

    into = {}
    conv_grad = []
    for part in halves:
        got = lane_call(
            long_back_body, "long_back", channels,
            [(near_back, "r"), (closing, "s"), (li_query, "r"), (li_key, "r"), (mr_query, "r"),
             (prev, "r"), (following, "r"), (table, "r"), (rate, "r"), (residue, "r")],
            [full, few(2), full, few(2), few(1), half],
            [EXT, EXT, EXT, EXT], 6, part, into, unroll=4,
        )
        conv_grad.append(got[5])
        into = dict(enumerate(got[:5]))
    grad_two, grad_two_after, mixed_grad, mixed_head, conv_head, _ = got
    after_one = [sent(signal, -1) for signal in conv_grad]
    after_next = sent(conv_head, -2)

    into = {}
    for n, part in enumerate(halves):
        got = lane_call(
            forward_body, "forward", channels,
            [(before_one[n], "r"), (before_kv, "r"), (signal_one[n], "r"), (mr_query, "r"),
             (li_key, "r"), (prev, "r"), (mixed_head, "r"), (table, "r"), (medium, "g"),
             (long, "g"), (rate, "r")],
            [full, full, full32, state_out, few(8)],
            [EXT, EXT, EXT], 14, part, into, unroll=4,
        )
        into = dict(enumerate(got))
    conv_one, value_two, near, state, head = got
    next_head = sent(head, -1)

    def medium_back(n, into):
        return lane_call(
            medium_back_body, "medium_back", channels,
            [(conv_grad[n], "r"), (after_one[n], "r"), (after_next, "r"), (mr_key, "r"),
             (mr_value, "r"), (prev, "r"), (following, "r"), (table, "r"), (medium_turned, "g")],
            [full, full], [EXT, EXT, EXT, EXT], 8, halves[n], into, unroll=4,
        )

    gathered = exchanged(state)
    got = medium_back(0, {})
    gathered = after(gathered, next_head, after_next, *got)
    start = exchanged(scan_states(gathered, my_rates, False))
    grad_mr_key, grad_mr_value = medium_back(1, dict(enumerate(got)))
    start = after(start, grad_mr_key)

    output, grad_li_query, grad_li_key, grad_mr_query = lane_call(
        long_body, "long_forward", channels,
        [(near, "r"), (start, "s"), (state, "s"), (li_query, "r"), (upstream, "r"), (prev, "r"),
         (following, "r"), (next_head, "r"), (grad_two, "r"), (grad_two_after, "r"),
         (value_two, "r"), (mixed_grad, "r"), (conv_one, "r"), (table, "r"), (rate, "r"),
         (residue, "r"), (long_turned, "g")],
        [full, full, full, full], [EXT, EXT, EXT, EXT], 14, unroll=4,
    )
    return (output, grad_mr_query, grad_mr_key, grad_mr_value, grad_li_query, grad_li_key)


def solution(mesh):
    split = P(("ctx", "ch"), None)
    return jax.shard_map(
        per_device,
        mesh=mesh,
        in_specs=(split,) * 6 + (P(),) * 6,
        out_specs=(split,) * 6,
        check_vma=False,
    )
```

```python
import jax
import jax.numpy as jnp
from jax import lax
from jax.experimental import pallas as pl
from jax.experimental.pallas import tpu as pltpu
from jax.sharding import PartitionSpec as P

GROUP = 16
SHORT = 3
MR_TAPS = 128
MODES = 16
ROWS = 128
LANES = 128
STRIP_FORWARD = 32
STRIP_BACK = 64
TILE_GROUPS = LANES // GROUP
AXES = ("ctx", "ch")
BF16 = jnp.bfloat16
F32 = jnp.float32
VMEM_LIMIT = 56 * 1024 * 1024

MR_Q, MR_K, MR_V, LI_Q, LI_K, LI_V, SKIP = 0, 3, 6, 9, 12, 15, 18
TABLE_ROWS = 24


def cost(microseconds):
    return pl.CostEstimate(
        flops=0, bytes_accessed=int(microseconds * 3.6e6), transcendentals=0
    )


def hint(start, of):
    return start if isinstance(start, int) else pl.multiple_of(start, of)


def lane_call(body, name, channels, ins, outs, scratch, us, part=(0, 1), into=None, width=1024, unroll=8, whole=False):
    span = channels // part[1]
    width = min(width, span)
    tiles = width // LANES
    unroll = min(unroll, tiles)
    blocks = span // width
    into = into or {}

    def spec(shape, kind):
        held = {"r": shape[-1], "g": shape[0] * GROUP, "s": shape[0] * (LANES // 2)}[kind]
        first = part[0] * blocks if held == channels else 0
        if kind == "r":
            return pl.BlockSpec((shape[0], width), lambda i: (0, first + i))
        if kind == "g":
            return pl.BlockSpec((width // GROUP, shape[1]), lambda i: (first + i, 0))
        return pl.BlockSpec((2 * tiles, 8, LANES), lambda i: (first + i, 0, 0))

    def view(ref, kind, t):
        if kind == "r":
            return ref.at[:, pl.ds(hint(t * LANES, LANES), LANES)]
        if kind == "g":
            return ref.at[pl.ds(hint(t * TILE_GROUPS, TILE_GROUPS), TILE_GROUPS), :]
        return ref.at[pl.ds(2 * t, 2)]

    kinds = [kind for _, kind in ins] + [kind for _, _, kind in outs]
    count_in, count_out = len(ins), len(outs)

    def kernel(*refs):
        arrays = refs[:count_in] + refs[count_in + len(into) : count_in + len(into) + count_out]
        extra = refs[count_in + len(into) + count_out :]

        if whole:
            body(*arrays, *extra)
            return

        def step(k, unused):
            for u in range(unroll):
                t = u if unroll == tiles else k * unroll + u
                body(
                    *[view(ref, kind, t) for ref, kind in zip(arrays, kinds)],
                    *[ref.at[u] for ref in extra],
                )
            return unused

        if unroll == tiles:
            step(0, 0)
        else:
            lax.fori_loop(0, tiles // unroll, step, 0)

    return pl.pallas_call(
        kernel,
        name=name,
        grid=(blocks,),
        in_specs=[spec(a.shape, kind) for a, kind in ins]
        + [pl.BlockSpec(memory_space=pl.ANY)] * len(into),
        out_specs=[spec(shape, kind) for shape, _, kind in outs],
        out_shape=[jax.ShapeDtypeStruct(shape, dtype) for shape, dtype, _ in outs],
        scratch_shapes=[
            pltpu.VMEM(shape if whole else (unroll, *shape), dtype) for shape, dtype in scratch
        ],
        input_output_aliases={count_in + n: at for n, at in enumerate(into)},
        compiler_params=pltpu.CompilerParams(vmem_limit_bytes=VMEM_LIMIT),
        cost_estimate=cost(us),
    )(*[a for a, _ in ins], *into.values())


EXT = ((ROWS + 16, LANES), F32)


def turned(x, by):
    return pltpu.roll(x, by, 0) if by else x


def fill(ext, value, prev8=None, next8=None):
    ext[8 : 8 + ROWS, :] = value
    if prev8 is not None:
        ext[0:8, :] = prev8
    if next8 is not None:
        ext[8 + ROWS :, :] = next8


def taps(table, first):
    return [table[first + j : first + j + 1, :] for j in range(SHORT)]


def short_forward(ext, weights, rows=ROWS):
    return (
        weights[0] * ext[8 : 8 + rows, :]
        + weights[1] * ext[7 : 7 + rows, :]
        + weights[2] * ext[6 : 6 + rows, :]
    )


def short_backward(ext, weights):
    return (
        weights[0] * ext[8 : 8 + ROWS, :]
        + weights[1] * ext[9 : 9 + ROWS, :]
        + weights[2] * ext[10 : 10 + ROWS, :]
    )


def iota(shape, dim):
    return lax.broadcasted_iota(jnp.int32, shape, dim)


def circulant(base, g, rows, shift=0):
    row = jnp.broadcast_to(base[g : g + 1, :], (rows, LANES))
    return pltpu.roll(row, shift, 1, stride=1, stride_axis=0)


def pick(products, rows, count):
    columns = LANES // count
    owner = iota((rows, LANES), 1) // columns
    picked = []
    for q in range(products.shape[1] // LANES):
        at = slice(q * LANES, (q + 1) * LANES)
        total = products[0:rows, at]
        for p in range(1, count):
            total = jnp.where(owner == p, products[p * rows : (p + 1) * rows, at], total)
        picked.append(total)
    return jnp.concatenate(picked, 0)


def windows(signal, strip, first, length):
    count = signal.shape[0]
    parts = []
    for q in range(ROWS // strip):
        low, high = strip * q + first, strip * q + first + length
        inside = signal[max(low, 0) : min(high, count)]
        pieces = [inside]
        if low < 0:
            pieces.insert(0, jnp.zeros((-low, LANES), signal.dtype))
        if high > count:
            pieces.append(jnp.zeros((high - count, LANES), signal.dtype))
        parts.append(jnp.concatenate(pieces, 0) if len(pieces) > 1 else inside)
    return jnp.concatenate(parts, 1)


def split_groups(signal):
    odd = ((iota(signal.shape, 1) // GROUP) % 2).astype(F32)
    return signal * (1.0 - odd).astype(signal.dtype), signal * odd.astype(signal.dtype)


def long_product(base_ref, signal, backward):
    strip = STRIP_BACK if backward else STRIP_FORWARD
    base = base_ref[...]
    row, lane = iota((strip, LANES), 0), iota((strip, LANES), 1)
    first = 0 if backward else strip - LANES
    keep = lane >= row if backward else lane + first <= row
    tables = [
        jnp.where(keep, circulant(base, g, strip, -first), 0.0).astype(BF16)
        for g in range(TILE_GROUPS)
    ]
    left = jnp.concatenate(
        [jnp.concatenate(tables[0::2], 0), jnp.concatenate(tables[1::2], 0)], 1
    )
    even, odd = split_groups(signal)
    right = jnp.concatenate(
        [windows(even, strip, first, LANES), windows(odd, strip, first, LANES)], 0
    )
    return pick(jnp.dot(left, right, preferred_element_type=F32), strip, TILE_GROUPS // 2)


def medium_product(base_ref, pair, backward):
    strip = STRIP_BACK if backward else STRIP_FORWARD
    base = base_ref[...]
    row, lane = iota((strip, LANES), 0), iota((strip, LANES), 1)
    keep = lane >= row if backward else lane > row
    wholes = [circulant(base, g, strip) for g in range(TILE_GROUPS)]
    first = [jnp.where(keep, whole, 0.0).astype(BF16) for whole in wholes]
    second = [jnp.where(keep, 0.0, whole).astype(BF16) for whole in wholes]
    left = jnp.concatenate([jnp.concatenate(first, 0), jnp.concatenate(second, 0)], 1)
    products = jnp.dot(left, windows(pair, strip, 0, 2 * LANES), preferred_element_type=F32)
    return pick(products, strip, TILE_GROUPS), first


def on_channels(base, column):
    own = iota((TILE_GROUPS, LANES), 0) == iota((TILE_GROUPS, LANES), 1) // GROUP
    return jnp.where(own, base[:, column : column + 1], 0.0).sum(0, keepdims=True)


def own_group():
    return (iota((LANES, LANES), 0) // MODES == iota((LANES, LANES), 1) // GROUP).astype(F32)


def spread(state):
    return (jnp.concatenate([state] * TILE_GROUPS, 0) * own_group()).astype(BF16)


def absorb(powers, signal):
    every = lax.dot_general(
        powers.astype(BF16), signal, (((0,), (0,)), ((), ())), preferred_element_type=F32
    )
    return (every * own_group()).reshape(TILE_GROUPS, MODES, LANES).sum(0)


def store_state(ref, state):
    ref[...] = state.reshape(2, 8, LANES)


def load_state(ref):
    return ref[...].reshape(MODES, LANES)


def margins_before(ref):
    rows = ref[...].astype(F32)
    return rows[0:8], rows[8:16]


def margins_after(ref):
    rows = ref[...].astype(F32)
    return rows[0:8], rows[8:16]


def edges(mr_query, mr_key, mr_value, li_query, li_key, upstream):
    channels = mr_query.shape[1]
    width = min(2048, channels)

    def kernel(q_end, k_end, v_end, lq_end, lk_end, lq, lk, g, k, v, last, first, last_kv, a, b):
        a[0:4, :] = k_end[...].astype(F32)[12:16]
        a[4:8, :] = v_end[...].astype(F32)[12:16]
        a[8:12, :] = q_end[...].astype(F32)[12:16]
        a[12:14, :] = lq_end[...].astype(F32)[14:16]
        a[14:16, :] = lk_end[...].astype(F32)[14:16]
        for n, ref in enumerate((lq, lk, g, k, v)):
            b[2 * n : 2 * n + 2, :] = ref[...].astype(F32)[0:2]
        b[10:16, :] = jnp.zeros((6, width), F32)
        last[...] = a[...].astype(BF16)
        first[...] = b[...].astype(BF16)
        last_kv[...] = a[0:8, :].astype(BF16)

    low = pl.BlockSpec((16, width), lambda i: (ROWS // 16 - 1, i))
    high = pl.BlockSpec((16, width), lambda i: (0, i))
    small = jax.ShapeDtypeStruct((16, channels), BF16)
    return pl.pallas_call(
        kernel,
        name="edges",
        grid=(channels // width,),
        in_specs=[low] * 5 + [high] * 5,
        out_specs=[high, high, pl.BlockSpec((8, width), lambda i: (0, i))],
        out_shape=[small, small, jax.ShapeDtypeStruct((8, channels), BF16)],
        scratch_shapes=[pltpu.VMEM((16, width), F32)] * 2,
        compiler_params=pltpu.CompilerParams(vmem_limit_bytes=VMEM_LIMIT),
        cost_estimate=cost(3.5),
    )(mr_query, mr_key, mr_value, li_query, li_key, li_query, li_key, upstream, mr_key, mr_value)


def make_tables(mr_short, li_short, li_skip, mr_filter, li_rate, li_residue):
    groups = mr_filter.shape[1]
    channels = groups * GROUP
    block = min(128, groups)
    width = block * GROUP

    def kernel(mr, li, skip, filters, rate, residue, table, medium, medium_back, long, long_back):
        for n in range(3):
            table[3 * n : 3 * n + 3, :] = mr[n].astype(F32)
            table[9 + 3 * n : 12 + 3 * n, :] = li[n].astype(F32)
        table[SKIP : SKIP + 1, :] = skip[...]
        table[SKIP + 1 :, :] = jnp.zeros((TABLE_ROWS - SKIP - 1, width), F32)
        row, lane = iota((LANES, LANES), 0), iota((LANES, LANES), 1)
        same = (row == lane).astype(F32).astype(BF16)
        turn = (row == (LANES - lane) % LANES).astype(F32).astype(BF16)
        by_rows = (((0,), (0,)), ((), ()))
        medium[...] = lax.dot_general(filters[...], turn, by_rows, preferred_element_type=F32)
        medium_back[...] = lax.dot_general(filters[...], same, by_rows, preferred_element_type=F32)
        position = iota((block, LANES), 1).astype(F32)
        impulse = jnp.zeros((block, LANES), F32)
        for n in range(MODES):
            impulse += residue[:, n : n + 1] * jnp.exp(-rate[:, n : n + 1] * position)
        long_back[...] = impulse
        long[...] = jnp.dot(impulse.astype(BF16), turn, preferred_element_type=F32)

    shorts = pl.BlockSpec((3, 3, width), lambda i: (0, 0, i))
    modes = pl.BlockSpec((block, MODES), lambda i: (i, 0))
    by_tap = pl.BlockSpec((block, LANES), lambda i: (i, 0))
    shapes = [jax.ShapeDtypeStruct((TABLE_ROWS, channels), F32)]
    shapes += [jax.ShapeDtypeStruct((groups, LANES), F32)] * 4
    return pl.pallas_call(
        kernel,
        name="tables",
        grid=(groups // block,),
        in_specs=[
            shorts, shorts, pl.BlockSpec((1, width), lambda i: (0, i)),
            pl.BlockSpec((MR_TAPS, block), lambda i: (0, i)), modes, modes,
        ],
        out_specs=[pl.BlockSpec((TABLE_ROWS, width), lambda i: (0, i))] + [by_tap] * 4,
        out_shape=shapes,
        compiler_params=pltpu.CompilerParams(vmem_limit_bytes=VMEM_LIMIT),
        cost_estimate=cost(5),
    )(mr_short, li_short, li_skip, mr_filter, li_rate, li_residue)


PITCH = ROWS + 16


def product_one_rows(key, value, prev, following, table, keys_one, value_one, beyond, out, *scratch):
    rows_k, rows_v, weights, out_k, out_v, out_p = scratch
    tiles = key.shape[1] // LANES
    at = [slice(t * LANES, (t + 1) * LANES) for t in range(tiles)]
    for t in range(tiles):
        weights[t * TABLE_ROWS : (t + 1) * TABLE_ROWS, :] = table[:, at[t]]
        before, _ = margins_before(prev.at[:, at[t]])
        after_a, after_b = margins_after(following.at[:, at[t]])
        start = t * PITCH
        rows_k[start : start + 8, :] = turned(before, 4)
        rows_v[start : start + 8, :] = before
        rows_k[start + 8 : start + 8 + ROWS, :] = key[:, at[t]].astype(F32)
        rows_v[start + 8 : start + 8 + ROWS, :] = value[:, at[t]].astype(F32)
        rows_k[start + 8 + ROWS : start + PITCH, :] = turned(after_a, 2)
        rows_v[start + 8 + ROWS : start + PITCH, :] = after_b

    def row(ref, r, pitch=PITCH):
        return ref[pl.ds(r, tiles, stride=pitch), :]

    w_k = [row(weights, MR_K + j, TABLE_ROWS) for j in range(SHORT)]
    w_v = [row(weights, MR_V + j, TABLE_ROWS) for j in range(SHORT)]
    last_k, last_v = [row(rows_k, 7), row(rows_k, 6)], [row(rows_v, 7), row(rows_v, 6)]
    for r in range(ROWS + 2):
        now_k, now_v = row(rows_k, 8 + r), row(rows_v, 8 + r)
        k = w_k[0] * now_k + w_k[1] * last_k[0] + w_k[2] * last_k[1]
        v = w_v[0] * now_v + w_v[1] * last_v[0] + w_v[2] * last_v[1]
        last_k, last_v = [now_k, last_k[0]], [now_v, last_v[0]]
        out_k[pl.ds(r, tiles, stride=PITCH), :] = k
        out_v[pl.ds(r, tiles, stride=PITCH), :] = v
        if r < ROWS:
            out_p[pl.ds(r, tiles, stride=PITCH), :] = k * v
    for t in range(tiles):
        start = t * PITCH
        keys_one[:, at[t]] = out_k[start : start + ROWS, :].astype(BF16)
        value_one[:, at[t]] = out_v[start : start + ROWS, :].astype(BF16)
        out[:, at[t]] = out_p[start : start + ROWS, :].astype(BF16)
        beyond[0:2, at[t]] = out_k[start + ROWS : start + ROWS + 2, :]
        beyond[2:4, at[t]] = out_v[start + ROWS : start + ROWS + 2, :]


def rolled_forward(signal, prev8, weights):
    total = weights[0] * signal
    first = iota((8, LANES), 0)
    for by in (1, 2):
        moved = turned(signal, by)
        top = jnp.where(first < by, turned(prev8, by), moved[0:8])
        rest = [moved[8:]] if signal.shape[0] > 8 else []
        total += weights[by] * jnp.concatenate([top, *rest], 0)
    return total


def product_one_body(key, value, prev, following, table, keys_one, value_one, beyond, out):
    weights = table[...]
    before, _ = margins_before(prev)
    after_a, after_b = margins_after(following)
    w_k, w_v = taps(weights, MR_K), taps(weights, MR_V)
    signal_k, signal_v = key[...].astype(F32), value[...].astype(F32)
    k = rolled_forward(signal_k, turned(before, 4), w_k)
    v = rolled_forward(signal_v, before, w_v)
    keys_one[...] = k.astype(BF16)
    value_one[...] = v.astype(BF16)
    out[...] = (k * v).astype(BF16)
    beyond[0:2, :] = rolled_forward(turned(after_a, 2), signal_k[ROWS - 8 :], w_k)[0:2]
    beyond[2:4, :] = rolled_forward(after_b, signal_v[ROWS - 8 :], w_v)[0:2]


def upstream_body(li_query, upstream, prev, table, rate, query_two_out, cotangent, state, ext):
    weights = table[...]
    _, margin = margins_before(prev)
    fill(ext, li_query[...].astype(F32), turned(margin, 2))
    query_two = short_forward(ext, taps(weights, LI_Q))
    rounded = (upstream[...].astype(F32) * query_two).astype(BF16)
    position = iota((ROWS, LANES), 0).astype(F32)
    store_state(state, absorb(jnp.exp(-rate[...] * position), rounded))
    cotangent[...] = rounded
    query_two_out[...] = query_two.astype(BF16)


def long_back_near_body(cotangent, table, base, near):
    signal = cotangent[...]
    product = long_product(base, signal, True)
    near[...] = product + table[SKIP : SKIP + 1, :] * signal.astype(F32)


def long_back_body(
    near, closing, li_query, li_key, query, prev, following, table, rate, residue,
    grad_two, grad_two_after, mixed_grad, mixed_head, out_head, query_one, keys_two_out, out,
    ext_q, ext_k, ext_g, ext_o,
):
    weights = table[...]
    _, before = margins_before(prev)
    after, _ = margins_after(following)
    base = 8 + ROWS
    ext_q[base - 16 : base, :] = li_query[ROWS - 16 :, :].astype(F32)
    ext_q[base:, :] = after
    w = taps(weights, LI_Q)
    query_after = (
        w[0] * ext_q[base : base + 8, :]
        + w[1] * ext_q[base - 1 : base + 7, :]
        + w[2] * ext_q[base - 2 : base + 6, :]
    )
    cot_after = turned(after, 4) * query_after
    state = load_state(closing)
    distance = (ROWS - iota((ROWS + 16, LANES), 0)).astype(F32)
    emit = (residue[...] * jnp.exp(-rate[...] * distance)).astype(BF16)
    emitted = jnp.dot(emit, spread(state), preferred_element_type=F32)
    later = jnp.dot(emit[ROWS:], spread(state - cot_after[0:1]), preferred_element_type=F32)
    skip = weights[SKIP : SKIP + 1]
    own = near[...] + emitted[0:ROWS]
    at_row = iota((8, LANES), 0)
    past = jnp.where(at_row == 0, emitted[ROWS : ROWS + 8], later[0:8]) + skip * cot_after
    past = jnp.where(at_row < 2, past, 0.0)
    grad_two[...] = own.astype(BF16)
    grad_two_after[...] = past[0:2]
    fill(ext_k, li_key[...].astype(F32), before, turned(after, 6))
    keys_two = short_forward(ext_k, taps(weights, LI_K), ROWS + 8)
    fill(ext_g, own * keys_two[0:ROWS], None, past * keys_two[ROWS:])
    mixed = short_backward(ext_g, taps(weights, LI_V))
    fill(ext_o, query[...].astype(F32), turned(before, 4))
    queries = short_forward(ext_o, taps(weights, MR_Q))
    conv_grad = mixed * queries
    query_one[...] = queries.astype(BF16)
    keys_two_out[...] = keys_two[0:ROWS].astype(BF16)
    mixed_grad[...] = mixed.astype(BF16)
    mixed_head[...] = mixed[0:2]
    out[...] = conv_grad.astype(BF16)
    out_head[...] = conv_grad[0:1]


def forward_body(
    before, before_kv, signal, query_one, keys_two, prev, mixed_head, table, base_ref, base_long,
    rate, conv_one, value_two, near, state, head, ext_m,
):
    weights = table[...]
    earlier = before[...]
    pair = jnp.concatenate([earlier, signal[...]], 0)
    conv, _ = medium_product(base_ref, pair, False)
    base = base_ref[...]
    row, lane = iota((16, LANES), 0), iota((16, LANES), 1)
    left = jnp.concatenate(
        [
            jnp.where(lane <= row + (ROWS - 16), circulant(base, g, 16, ROWS - 16), 0.0).astype(BF16)
            for g in range(TILE_GROUPS)
        ],
        0,
    )
    edge = pick(jnp.dot(left, earlier, preferred_element_type=F32), 16, TILE_GROUPS)
    raw = before_kv[...].astype(F32)
    w_k, w_v = taps(weights, MR_K), taps(weights, MR_V)
    key_last = w_k[0] * raw[3:4] + w_k[1] * raw[2:3] + w_k[2] * raw[1:2]
    value_last = w_v[0] * raw[7:8] + w_v[1] * raw[6:7] + w_v[2] * raw[5:6]
    far = on_channels(base, 1) * (key_last * value_last).astype(BF16).astype(F32)
    conv_before = edge[8:16] + jnp.where(iota((8, LANES), 0) == 6, far, 0.0)
    _, margin = margins_before(prev)
    w = taps(weights, MR_Q)
    query_before = w[0] * margin[0:8] + w[1] * turned(margin, 1) + w[2] * turned(margin, 2)
    mixed_before = turned(query_before, 4) * conv_before
    fill(
        ext_m,
        (query_one[...].astype(F32) * conv).astype(BF16).astype(F32),
        mixed_before.astype(BF16).astype(F32),
    )
    value = short_forward(ext_m, taps(weights, LI_V))
    product = keys_two[...].astype(F32) * value
    rounded = product.astype(BF16)
    position = (ROWS - 1 - iota((ROWS, LANES), 0)).astype(F32)
    store_state(state, absorb(jnp.exp(-rate[...] * position), rounded))
    conv_one[...] = conv.astype(BF16)
    value_two[...] = value.astype(BF16)
    near[...] = (
        long_product(base_long, rounded, False) + weights[SKIP : SKIP + 1] * product
    )
    head[0:2, :] = product[0:2]
    head[2:4, :] = value[0:2]
    head[4:6, :] = conv[0:2]
    head[6:8, :] = mixed_head[...]


def late_body(
    grad_two, grad_two_after, value_two, mixed_grad, conv_one, next_head, table,
    grad_li_key, grad_mr_query, ext_k, ext_m,
):
    weights = table[...]
    fill(ext_k, grad_two[...].astype(F32) * value_two[...].astype(F32))
    ext_k[8 + ROWS : 10 + ROWS, :] = grad_two_after[...] * next_head[2:4, :]
    grad_li_key[...] = short_backward(ext_k, taps(weights, LI_K)).astype(BF16)
    fill(ext_m, mixed_grad[...].astype(F32) * conv_one[...].astype(F32))
    ext_m[8 + ROWS : 10 + ROWS, :] = next_head[6:8, :] * next_head[4:6, :]
    grad_mr_query[...] = short_backward(ext_m, taps(weights, MR_Q)).astype(BF16)


def long_body(
    near, start, end, query_two, upstream, following, next_head, table, rate, residue, base_back,
    out, grad_li_query, ext_g,
):
    weights = table[...]
    distance = (iota((ROWS + 16, LANES), 0) + 1).astype(F32)
    emit = (residue[...] * jnp.exp(-rate[...] * distance)).astype(BF16)
    emitted = jnp.dot(emit, spread(load_state(start)), preferred_element_type=F32)
    conv = near[...] + emitted[0:ROWS]
    out[...] = (query_two[...].astype(F32) * conv).astype(BF16)
    ended = jnp.dot(emit[0:16], spread(load_state(end)), preferred_element_type=F32)
    impulse = base_back[...]
    at_once = on_channels(impulse, 0) + weights[SKIP : SKIP + 1]
    first, second = next_head[0:1, :], next_head[1:2, :]
    past = emitted[ROWS : ROWS + 8] + ended[0:8]
    past_first = past[0:1] + at_once * first
    past_second = past[1:2] + on_channels(impulse, 1) * first + at_once * second
    after, _ = margins_after(following)
    fill(ext_g, upstream[...].astype(F32) * conv)
    ext_g[8 + ROWS : 9 + ROWS, :] = after[4:5] * past_first
    ext_g[9 + ROWS : 10 + ROWS, :] = after[5:6] * past_second
    grad_li_query[...] = short_backward(ext_g, taps(weights, LI_Q)).astype(BF16)


def medium_back_body(
    conv_grad, after, after_next, keys_one, value_one, beyond, table, base_ref,
    grad_key, grad_value, ext_gk, ext_gv,
):
    weights = table[...]
    later = after[...]
    pair = jnp.concatenate([conv_grad[...], later], 0)
    grad, first_half = medium_product(base_ref, pair, True)
    left = jnp.concatenate([part[0:16] for part in first_half], 0)
    edge = pick(jnp.dot(left, later, preferred_element_type=F32), 16, TILE_GROUPS)
    far = on_channels(base_ref[...], MR_TAPS - 1) * after_next[...].astype(BF16).astype(F32)
    past = edge[0:8] + jnp.where(iota((8, LANES), 0) == 1, far, 0.0)
    fill(ext_gk, grad * value_one[...].astype(F32))
    fill(ext_gv, grad * keys_one[...].astype(F32))
    ext_gk[8 + ROWS : 10 + ROWS, :] = past[0:2] * beyond[2:4, :]
    ext_gv[8 + ROWS : 10 + ROWS, :] = past[0:2] * beyond[0:2, :]
    grad_key[...] = short_backward(ext_gk, taps(weights, MR_K)).astype(BF16)
    grad_value[...] = short_backward(ext_gv, taps(weights, MR_V)).astype(BF16)


def state_total(states, rates, copies, backward):
    count = states.shape[0]

    def kernel(states_ref, rates_ref, out_ref):
        decay = jnp.exp(rates_ref[...] * (-float(ROWS)))
        total = jnp.zeros(rates.shape, F32)
        for k in range(count):
            total = decay * total + states_ref[count - 1 - k if backward else k]
        for n in range(copies):
            out_ref[n] = total

    whole = pl.BlockSpec(memory_space=pltpu.VMEM)
    return pl.pallas_call(
        kernel,
        name="total_back" if backward else "total_forward",
        out_shape=jax.ShapeDtypeStruct((copies, *rates.shape), F32),
        in_specs=[whole, whole],
        out_specs=whole,
        cost_estimate=cost(2),
    )(states, rates)


def state_carries(states, totals, rates, place, backward):
    count, segments = states.shape[0], totals.shape[0]

    def kernel(place_ref, states_ref, totals_ref, rates_ref, out_ref):
        mine = place_ref[0]
        decay = jnp.exp(rates_ref[...] * (-float(ROWS)))
        segment_decay = jnp.exp(rates_ref[...] * (-float(ROWS * count)))
        carried = jnp.zeros(rates.shape, F32)
        for k in range(segments):
            n = segments - 1 - k if backward else k
            passed = n > mine if backward else n < mine
            carried = jnp.where(passed, segment_decay * carried + totals_ref[n], carried)
        for k in range(count):
            b = count - 1 - k if backward else k
            out_ref[b] = carried
            carried = decay * carried + states_ref[b]

    whole = pl.BlockSpec(memory_space=pltpu.VMEM)
    return pl.pallas_call(
        kernel,
        name="carry_back" if backward else "carry_forward",
        out_shape=jax.ShapeDtypeStruct(states.shape, F32),
        in_specs=[pl.BlockSpec(memory_space=pltpu.SMEM), whole, whole, whole],
        out_specs=whole,
        cost_estimate=cost(2),
    )(place, states, totals, rates)


def sent(array, by):
    size = lax.axis_size(AXES)
    pairs = [(i, i + by) for i in range(size) if 0 <= i + by < size]
    return lax.ppermute(array, AXES, pairs)


def exchanged(array, axis):
    return lax.all_to_all(array, axis, split_axis=0, concat_axis=0, tiled=True)


def after(array, *others):
    return lax.optimization_barrier((array, *others))[0]


def per_device(
    mr_query, mr_key, mr_value, li_query, li_key, upstream,
    mr_short, li_short, mr_filter, li_rate, li_residue, li_skip,
):
    channels = mr_query.shape[1]
    tiles = channels // LANES
    assert mr_query.shape[0] == ROWS and lax.axis_size(AXES) == 2 * tiles
    rows = (ROWS, channels)
    full, full32 = (rows, BF16, "r"), (rows, F32, "r")
    half = ((ROWS, channels // 2), BF16, "r")
    state_out = ((2 * tiles, 8, LANES), F32, "s")
    halves = ((0, 2), (1, 2))

    def few(n):
        return ((n, channels), F32, "r")

    last_rows, first_rows, last_kv = edges(mr_query, mr_key, mr_value, li_query, li_key, upstream)
    prev = sent(last_rows, 1)
    following = sent(first_rows, -1)
    before_kv = sent(last_kv, 2)

    table, medium, medium_turned, long, long_turned = make_tables(
        mr_short, li_short, li_skip[None, :], mr_filter, li_rate, li_residue
    )
    rate = li_rate.reshape(1, channels)
    residue = li_residue.reshape(1, channels)
    peers = lax.axis_size("ch")
    share = 2 * tiles // peers
    segments = lax.axis_size("ctx")
    place = lax.axis_index("ctx").reshape(1)
    my_groups = share // 2 * TILE_GROUPS
    my_rates = lax.dynamic_slice_in_dim(li_rate, lax.axis_index("ch") * my_groups, my_groups, 0)
    my_rates = my_rates.reshape(share // 2, TILE_GROUPS, 2, 8).transpose(0, 2, 3, 1)
    my_rates = jnp.repeat(my_rates, GROUP, axis=3).reshape(share, 8, LANES)

    def to_scan(state):
        return exchanged(state, "ch").reshape(peers, share, 8, LANES)

    cotangent_inputs = [(li_query, "r"), (upstream, "r"), (prev, "r"), (table, "r"), (rate, "r")]
    query_two, cotangent, state_back = lane_call(
        upstream_body, "upstream", channels, cotangent_inputs,
        [full, full, state_out], [EXT], 7,
    )
    gathered_back = to_scan(state_back)
    (near_back,) = lane_call(
        long_back_near_body, "long_back_near", channels,
        [(cotangent, "r"), (table, "r"), (long_turned, "g")],
        [full32], [], 8, unroll=4,
    )
    gathered_back = after(gathered_back, following, before_kv, near_back)
    totals_back = exchanged(state_total(gathered_back, my_rates, segments, True), "ctx")

    into = {}
    signal_one = []
    for n, part in enumerate(halves):
        tall = (8 * PITCH, LANES), F32
        got = lane_call(
            product_one_body if n else product_one_rows, "product_one", channels,
            [(mr_key, "r"), (mr_value, "r"), (prev, "r"), (following, "r"), (table, "r")],
            [full, full, few(4), half],
            [] if n else [tall, tall, ((8 * TABLE_ROWS, LANES), F32), tall, tall, tall],
            4, part, into, whole=n == 0,
        )
        signal_one.append(got[3])
        into = dict(enumerate(got[:3]))
    keys_one, value_one, beyond_one = got[:3]
    totals_back = after(totals_back, signal_one[0])
    carries = state_carries(gathered_back, totals_back, my_rates, place, True)
    closing = exchanged(carries.reshape(2 * tiles, 8, LANES), "ch")
    before_one = [sent(after(signal, closing), 1) for signal in signal_one]

    into = {}
    conv_grad = []
    for part in halves:
        got = lane_call(
            long_back_body, "long_back", channels,
            [(near_back, "r"), (closing, "s"), (li_query, "r"), (li_key, "r"), (mr_query, "r"),
             (prev, "r"), (following, "r"), (table, "r"), (rate, "r"), (residue, "r")],
            [full, few(2), full, few(2), few(1), full, full, half],
            [EXT, EXT, EXT, EXT], 6, part, into, unroll=4,
        )
        conv_grad.append(got[7])
        into = dict(enumerate(got[:7]))
    grad_two, grad_two_after, mixed_grad, mixed_head, conv_head, query_one, keys_two, _ = got
    after_one = [sent(signal, -1) for signal in conv_grad]
    after_next = sent(conv_head, -2)

    into = {}
    for n, part in enumerate(halves):
        got = lane_call(
            forward_body, "forward", channels,
            [(before_one[n], "r"), (before_kv, "r"), (signal_one[n], "r"), (query_one, "r"),
             (keys_two, "r"), (prev, "r"), (mixed_head, "r"), (table, "r"), (medium, "g"),
             (long, "g"), (rate, "r")],
            [full, full, full32, state_out, few(8)],
            [EXT], 13, part, into, unroll=4,
        )
        into = dict(enumerate(got))
    conv_one, value_two, near, state, head = got
    next_head = sent(head, -1)

    def medium_back(n, into):
        return lane_call(
            medium_back_body, "medium_back", channels,
            [(conv_grad[n], "r"), (after_one[n], "r"), (after_next, "r"), (keys_one, "r"),
             (value_one, "r"), (beyond_one, "r"), (table, "r"), (medium_turned, "g")],
            [full, full], [EXT, EXT], 7, halves[n], into, unroll=4,
        )

    gathered = to_scan(state)
    got = medium_back(0, {})
    gathered = after(gathered, next_head, after_next, *got)
    totals = exchanged(state_total(gathered, my_rates, segments, False), "ctx")
    grad_mr_key, grad_mr_value = medium_back(1, dict(enumerate(got)))
    totals = after(totals, grad_mr_key)
    carries = state_carries(gathered, totals, my_rates, place, False)
    start = exchanged(carries.reshape(2 * tiles, 8, LANES), "ch")
    grad_li_key, grad_mr_query = lane_call(
        late_body, "late", channels,
        [(grad_two, "r"), (grad_two_after, "r"), (value_two, "r"), (mixed_grad, "r"),
         (conv_one, "r"), (next_head, "r"), (table, "r")],
        [full, full], [EXT, EXT], 6,
    )
    start = after(start, grad_li_key)
    output, grad_li_query = lane_call(
        long_body, "long_forward", channels,
        [(near, "r"), (start, "s"), (state, "s"), (query_two, "r"), (upstream, "r"),
         (following, "r"), (next_head, "r"), (table, "r"), (rate, "r"), (residue, "r"),
         (long_turned, "g")],
        [full, full], [EXT], 9,
    )
    return (output, grad_mr_query, grad_mr_key, grad_mr_value, grad_li_query, grad_li_key)


def solution(mesh):
    split = P(("ctx", "ch"), None)
    return jax.shard_map(
        per_device,
        mesh=mesh,
        in_specs=(split,) * 6 + (P(),) * 6,
        out_specs=(split,) * 6,
        check_vma=False,
    )
```

```python
import jax
import jax.numpy as jnp
from jax import lax
from jax.experimental import pallas as pl
from jax.experimental.pallas import tpu as pltpu
from jax.sharding import PartitionSpec as P

GROUP = 16
SHORT = 3
MR_TAPS = 128
MODES = 16
ROWS = 128
LANES = 128
STRIP_FORWARD = 32
STRIP_BACK = 64
TILE_GROUPS = LANES // GROUP
AXES = ("ctx", "ch")
BF16 = jnp.bfloat16
F32 = jnp.float32
VMEM_LIMIT = 56 * 1024 * 1024

MR_Q, MR_K, MR_V, LI_Q, LI_K, LI_V, SKIP = 0, 3, 6, 9, 12, 15, 18
TABLE_ROWS = 24


def cost(microseconds):
    return pl.CostEstimate(
        flops=0, bytes_accessed=int(microseconds * 3.6e6), transcendentals=0
    )


def hint(start, of):
    return start if isinstance(start, int) else pl.multiple_of(start, of)


def lane_call(body, name, channels, ins, outs, us, part=(0, 1), into=None, width=1024, unroll=8):
    span = channels // part[1]
    width = min(width, span)
    tiles = width // LANES
    unroll = min(unroll, tiles)
    blocks = span // width
    into = into or {}

    def spec(shape, kind):
        held = {"r": shape[-1], "g": shape[0] * GROUP, "s": shape[0] * (LANES // 2)}[kind]
        first = part[0] * blocks if held == channels else 0
        if kind == "r":
            return pl.BlockSpec((shape[0], width), lambda i: (0, first + i))
        if kind == "g":
            return pl.BlockSpec((width // GROUP, shape[1]), lambda i: (first + i, 0))
        return pl.BlockSpec((2 * tiles, 8, LANES), lambda i: (first + i, 0, 0))

    def view(ref, kind, t):
        if kind == "r":
            return ref.at[:, pl.ds(hint(t * LANES, LANES), LANES)]
        if kind == "g":
            return ref.at[pl.ds(hint(t * TILE_GROUPS, TILE_GROUPS), TILE_GROUPS), :]
        return ref.at[pl.ds(2 * t, 2)]

    kinds = [kind for _, kind in ins] + [kind for _, _, kind in outs]
    count_in, count_out = len(ins), len(outs)

    def kernel(*refs):
        arrays = refs[:count_in] + refs[count_in + len(into) : count_in + len(into) + count_out]

        def step(k, unused):
            running = []
            for u in range(unroll):
                t = u if unroll == tiles else k * unroll + u
                running.append(body(*[view(ref, kind, t) for ref, kind in zip(arrays, kinds)]))
            while running:
                running = [tile for tile in running if next(tile, False)]
            return unused

        if unroll == tiles:
            step(0, 0)
        else:
            lax.fori_loop(0, tiles // unroll, step, 0)

    return pl.pallas_call(
        kernel,
        name=name,
        grid=(blocks,),
        in_specs=[spec(a.shape, kind) for a, kind in ins]
        + [pl.BlockSpec(memory_space=pl.ANY)] * len(into),
        out_specs=[spec(shape, kind) for shape, _, kind in outs],
        out_shape=[jax.ShapeDtypeStruct(shape, dtype) for shape, dtype, _ in outs],
        input_output_aliases={count_in + n: at for n, at in enumerate(into)},
        compiler_params=pltpu.CompilerParams(vmem_limit_bytes=VMEM_LIMIT),
        cost_estimate=cost(us),
    )(*[a for a, _ in ins], *into.values())


def turned(x, by):
    return pltpu.roll(x, by, 0) if by else x


def taps(table, first):
    return [table[first + j : first + j + 1, :] for j in range(SHORT)]


def short_forward(signal, weights, prev8):
    total = weights[0] * signal
    first = iota((8, LANES), 0)
    for by in (1, 2):
        moved = turned(signal, by)
        top = jnp.where(first < by, turned(prev8, by), moved[0:8])
        rest = [moved[8:]] if signal.shape[0] > 8 else []
        total += weights[by] * jnp.concatenate([top, *rest], 0)
    return total


def short_backward(signal, weights, next8):
    total = weights[0] * signal
    rows = signal.shape[0]
    last = iota((8, LANES), 0)
    for by in (1, 2):
        moved = turned(signal, rows - by)
        bottom = jnp.where(last >= 8 - by, turned(next8, 8 - by), moved[rows - 8 :])
        total += weights[by] * jnp.concatenate([moved[: rows - 8], bottom], 0)
    return total


def two_rows(first, second):
    at = iota((8, LANES), 0)
    return jnp.where(at == 0, first, jnp.where(at == 1, second, 0.0))


def iota(shape, dim):
    return lax.broadcasted_iota(jnp.int32, shape, dim)


def circulant(base, g, rows, shift=0):
    row = jnp.broadcast_to(base[g : g + 1, :], (rows, LANES))
    return pltpu.roll(row, shift, 1, stride=1, stride_axis=0)


def pick(products, rows, count):
    columns = LANES // count
    owner = iota((rows, LANES), 1) // columns
    picked = []
    for q in range(products.shape[1] // LANES):
        at = slice(q * LANES, (q + 1) * LANES)
        total = products[0:rows, at]
        for p in range(1, count):
            total = jnp.where(owner == p, products[p * rows : (p + 1) * rows, at], total)
        picked.append(total)
    return jnp.concatenate(picked, 0)


def windows(signal, strip, first, length):
    count = signal.shape[0]
    parts = []
    for q in range(ROWS // strip):
        low, high = strip * q + first, strip * q + first + length
        inside = signal[max(low, 0) : min(high, count)]
        pieces = [inside]
        if low < 0:
            pieces.insert(0, jnp.zeros((-low, LANES), signal.dtype))
        if high > count:
            pieces.append(jnp.zeros((high - count, LANES), signal.dtype))
        parts.append(jnp.concatenate(pieces, 0) if len(pieces) > 1 else inside)
    return jnp.concatenate(parts, 1)


def split_groups(signal):
    odd = ((iota(signal.shape, 1) // GROUP) % 2).astype(F32)
    return signal * (1.0 - odd).astype(signal.dtype), signal * odd.astype(signal.dtype)


def long_tables(base_ref, backward):
    strip = STRIP_BACK if backward else STRIP_FORWARD
    base = base_ref[...]
    row, lane = iota((strip, LANES), 0), iota((strip, LANES), 1)
    first = 0 if backward else strip - LANES
    keep = lane >= row if backward else lane + first <= row
    tables = [
        jnp.where(keep, circulant(base, g, strip, -first), 0.0).astype(BF16)
        for g in range(TILE_GROUPS)
    ]
    return jnp.concatenate(
        [jnp.concatenate(tables[0::2], 0), jnp.concatenate(tables[1::2], 0)], 1
    )


def long_windows(signal, backward):
    strip = STRIP_BACK if backward else STRIP_FORWARD
    first = 0 if backward else strip - LANES
    even, odd = split_groups(signal)
    return jnp.concatenate(
        [windows(even, strip, first, LANES), windows(odd, strip, first, LANES)], 0
    )


def medium_tables(base, backward):
    strip = STRIP_BACK if backward else STRIP_FORWARD
    row, lane = iota((strip, LANES), 0), iota((strip, LANES), 1)
    keep = lane >= row if backward else lane > row
    wholes = [circulant(base, g, strip) for g in range(TILE_GROUPS)]
    first = [jnp.where(keep, whole, 0.0).astype(BF16) for whole in wholes]
    second = [jnp.where(keep, 0.0, whole).astype(BF16) for whole in wholes]
    return jnp.concatenate([jnp.concatenate(first, 0), jnp.concatenate(second, 0)], 1), first


def on_channels(base, column):
    own = iota((TILE_GROUPS, LANES), 0) == iota((TILE_GROUPS, LANES), 1) // GROUP
    return jnp.where(own, base[:, column : column + 1], 0.0).sum(0, keepdims=True)


def own_group():
    return (iota((LANES, LANES), 0) // MODES == iota((LANES, LANES), 1) // GROUP).astype(F32)


def spread(state):
    return (jnp.concatenate([state] * TILE_GROUPS, 0) * own_group()).astype(BF16)


def absorb(powers, signal):
    every = lax.dot_general(
        powers.astype(BF16), signal, (((0,), (0,)), ((), ())), preferred_element_type=F32
    )
    return (every * own_group()).reshape(TILE_GROUPS, MODES, LANES).sum(0)


def store_state(ref, state):
    ref[...] = state.reshape(2, 8, LANES).astype(ref.dtype)


def load_state(ref):
    return ref[...].astype(F32).reshape(MODES, LANES)


def margins_before(ref):
    rows = ref[...].astype(F32)
    return rows[0:8], rows[8:16]


def margins_after(ref):
    rows = ref[...].astype(F32)
    return rows[0:8], rows[8:16]


def edges(mr_query, mr_key, mr_value, li_query, li_key, upstream):
    channels = mr_query.shape[1]
    width = min(2048, channels)

    def kernel(q_end, k_end, v_end, lq_end, lk_end, lq, lk, g, k, v, last, first, last_kv, a, b):
        a[0:4, :] = k_end[...].astype(F32)[12:16]
        a[4:8, :] = v_end[...].astype(F32)[12:16]
        a[8:12, :] = q_end[...].astype(F32)[12:16]
        a[12:14, :] = lq_end[...].astype(F32)[14:16]
        a[14:16, :] = lk_end[...].astype(F32)[14:16]
        for n, ref in enumerate((lq, lk, g, k, v)):
            b[2 * n : 2 * n + 2, :] = ref[...].astype(F32)[0:2]
        b[10:16, :] = jnp.zeros((6, width), F32)
        last[...] = a[...].astype(BF16)
        first[...] = b[...].astype(BF16)
        last_kv[...] = a[0:8, :].astype(BF16)

    low = pl.BlockSpec((16, width), lambda i: (ROWS // 16 - 1, i))
    high = pl.BlockSpec((16, width), lambda i: (0, i))
    small = jax.ShapeDtypeStruct((16, channels), BF16)
    return pl.pallas_call(
        kernel,
        name="edges",
        grid=(channels // width,),
        in_specs=[low] * 5 + [high] * 5,
        out_specs=[high, high, pl.BlockSpec((8, width), lambda i: (0, i))],
        out_shape=[small, small, jax.ShapeDtypeStruct((8, channels), BF16)],
        scratch_shapes=[pltpu.VMEM((16, width), F32)] * 2,
        compiler_params=pltpu.CompilerParams(vmem_limit_bytes=VMEM_LIMIT),
        cost_estimate=cost(3.5),
    )(mr_query, mr_key, mr_value, li_query, li_key, li_query, li_key, upstream, mr_key, mr_value)


def make_tables(mr_short, li_short, li_skip, mr_filter, li_rate, li_residue):
    groups = mr_filter.shape[1]
    channels = groups * GROUP
    block = min(128, groups)
    width = block * GROUP

    def kernel(mr, li, skip, filters, rate, residue, table, medium, medium_back, long, long_back):
        for n in range(3):
            table[3 * n : 3 * n + 3, :] = mr[n].astype(F32)
            table[9 + 3 * n : 12 + 3 * n, :] = li[n].astype(F32)
        table[SKIP : SKIP + 1, :] = skip[...]
        table[SKIP + 1 :, :] = jnp.zeros((TABLE_ROWS - SKIP - 1, width), F32)
        row, lane = iota((LANES, LANES), 0), iota((LANES, LANES), 1)
        same = (row == lane).astype(F32).astype(BF16)
        turn = (row == (LANES - lane) % LANES).astype(F32).astype(BF16)
        by_rows = (((0,), (0,)), ((), ()))
        medium[...] = lax.dot_general(filters[...], turn, by_rows, preferred_element_type=F32)
        medium_back[...] = lax.dot_general(filters[...], same, by_rows, preferred_element_type=F32)
        position = iota((block, LANES), 1).astype(F32)
        impulse = jnp.zeros((block, LANES), F32)
        for n in range(MODES):
            impulse += residue[:, n : n + 1] * jnp.exp(-rate[:, n : n + 1] * position)
        long_back[...] = impulse
        long[...] = jnp.dot(impulse.astype(BF16), turn, preferred_element_type=F32)

    shorts = pl.BlockSpec((3, 3, width), lambda i: (0, 0, i))
    modes = pl.BlockSpec((block, MODES), lambda i: (i, 0))
    by_tap = pl.BlockSpec((block, LANES), lambda i: (i, 0))
    shapes = [jax.ShapeDtypeStruct((TABLE_ROWS, channels), F32)]
    shapes += [jax.ShapeDtypeStruct((groups, LANES), F32)] * 4
    return pl.pallas_call(
        kernel,
        name="tables",
        grid=(groups // block,),
        in_specs=[
            shorts, shorts, pl.BlockSpec((1, width), lambda i: (0, i)),
            pl.BlockSpec((MR_TAPS, block), lambda i: (0, i)), modes, modes,
        ],
        out_specs=[pl.BlockSpec((TABLE_ROWS, width), lambda i: (0, i))] + [by_tap] * 4,
        out_shape=shapes,
        compiler_params=pltpu.CompilerParams(vmem_limit_bytes=VMEM_LIMIT),
        cost_estimate=cost(5),
    )(mr_short, li_short, li_skip, mr_filter, li_rate, li_residue)


def product_one_body(key, value, prev, following, table, keys_one, value_one, beyond, out):
    weights = table[...]
    before, _ = margins_before(prev)
    after_a, after_b = margins_after(following)
    w_k, w_v = taps(weights, MR_K), taps(weights, MR_V)
    signal_k, signal_v = key[...].astype(F32), value[...].astype(F32)
    yield True
    k = short_forward(signal_k, w_k, turned(before, 4))
    v = short_forward(signal_v, w_v, before)
    yield True
    keys_one[...] = k.astype(BF16)
    value_one[...] = v.astype(BF16)
    out[...] = (k * v).astype(BF16)
    beyond[0:2, :] = short_forward(turned(after_a, 2), w_k, signal_k[ROWS - 8 :])[0:2]
    beyond[2:4, :] = short_forward(after_b, w_v, signal_v[ROWS - 8 :])[0:2]


def upstream_body(li_query, upstream, prev, table, rate, query_two_out, cotangent, state):
    weights = table[...]
    _, margin = margins_before(prev)
    signal, given, decay = li_query[...].astype(F32), upstream[...].astype(F32), rate[...]
    yield True
    powers = jnp.exp(-decay * iota((ROWS, LANES), 0).astype(F32))
    query_two = short_forward(signal, taps(weights, LI_Q), turned(margin, 2))
    rounded = (given * query_two).astype(BF16)
    yield True
    absorbed = absorb(powers, rounded)
    yield True
    store_state(state, absorbed)
    cotangent[...] = rounded
    query_two_out[...] = query_two.astype(BF16)


def long_back_near_body(cotangent, table, base, near):
    signal = cotangent[...]
    skip = table[SKIP : SKIP + 1, :]
    left, right = long_tables(base, True), long_windows(signal, True)
    yield True
    products = jnp.dot(left, right, preferred_element_type=F32)
    yield True
    near[...] = pick(products, STRIP_BACK, TILE_GROUPS // 2) + skip * signal.astype(F32)


def long_back_body(
    near_ref, closing, li_query, li_key, query, prev, following, table, rate, residue,
    grad_two, grad_two_after, mixed_grad, mixed_head, out_head, out,
):
    weights = table[...]
    _, before = margins_before(prev)
    after, _ = margins_after(following)
    near, state = near_ref[...], load_state(closing)
    key, queries = li_key[...].astype(F32), query[...].astype(F32)
    query_end = li_query[ROWS - 16 :, :].astype(F32)[8:16]
    distance = (ROWS - iota((ROWS + 16, LANES), 0)).astype(F32)
    emit = (residue[...] * jnp.exp(-rate[...] * distance)).astype(BF16)
    cot_after = turned(after, 4) * short_forward(after, taps(weights, LI_Q), query_end)
    yield True
    emitted = jnp.dot(emit, spread(state), preferred_element_type=F32)
    later = jnp.dot(emit[ROWS:], spread(state - cot_after[0:1]), preferred_element_type=F32)
    yield True
    skip = weights[SKIP : SKIP + 1]
    own = near + emitted[0:ROWS]
    at_row = iota((8, LANES), 0)
    past = jnp.where(at_row == 0, emitted[ROWS : ROWS + 8], later[0:8]) + skip * cot_after
    past = jnp.where(at_row < 2, past, 0.0)
    w_k = taps(weights, LI_K)
    keys_two = short_forward(key, w_k, before)
    keys_after = short_forward(turned(after, 6), w_k, key[ROWS - 8 :])
    mixed = short_backward(own * keys_two, taps(weights, LI_V), past * keys_after)
    queries = short_forward(queries, taps(weights, MR_Q), turned(before, 4))
    conv_grad = mixed * queries
    yield True
    grad_two[...] = own.astype(BF16)
    grad_two_after[...] = past[0:2]
    mixed_grad[...] = mixed.astype(BF16)
    mixed_head[...] = mixed[0:2]
    out[...] = conv_grad.astype(BF16)
    out_head[...] = conv_grad[0:1]


def forward_body(
    before, before_kv, signal, query, key, prev, table, base_ref, base_long,
    rate, conv_one, value_two, near, state, state_sent, head,
):
    weights = table[...]
    earlier = before[...]
    pair = jnp.concatenate([earlier, signal[...]], 0)
    queries, keys = query[...].astype(F32), key[...].astype(F32)
    _, margin = margins_before(prev)
    raw = before_kv[...].astype(F32)
    base = base_ref[...]
    left, _ = medium_tables(base, False)
    row, lane = iota((16, LANES), 0), iota((16, LANES), 1)
    left_edge = jnp.concatenate(
        [
            jnp.where(lane <= row + (ROWS - 16), circulant(base, g, 16, ROWS - 16), 0.0).astype(BF16)
            for g in range(TILE_GROUPS)
        ],
        0,
    )
    yield True
    products = jnp.dot(
        left, windows(pair, STRIP_FORWARD, 0, 2 * LANES), preferred_element_type=F32
    )
    products_edge = jnp.dot(left_edge, earlier, preferred_element_type=F32)
    yield True
    query_one = short_forward(queries, taps(weights, MR_Q), turned(margin, 4))
    keys_two = short_forward(keys, taps(weights, LI_K), margin)
    conv = pick(products, STRIP_FORWARD, TILE_GROUPS)
    edge = pick(products_edge, 16, TILE_GROUPS)
    w_k, w_v = taps(weights, MR_K), taps(weights, MR_V)
    key_last = w_k[0] * raw[3:4] + w_k[1] * raw[2:3] + w_k[2] * raw[1:2]
    value_last = w_v[0] * raw[7:8] + w_v[1] * raw[6:7] + w_v[2] * raw[5:6]
    far = on_channels(base, 1) * (key_last * value_last).astype(BF16).astype(F32)
    conv_before = edge[8:16] + jnp.where(iota((8, LANES), 0) == 6, far, 0.0)
    w = taps(weights, MR_Q)
    query_before = w[0] * margin + w[1] * turned(margin, 1) + w[2] * turned(margin, 2)
    mixed_before = turned(query_before, 4) * conv_before
    mixed = (query_one * conv).astype(BF16).astype(F32)
    value = short_forward(mixed, taps(weights, LI_V), mixed_before.astype(BF16).astype(F32))
    product = keys_two * value
    rounded = product.astype(BF16)
    yield True
    left, right = long_tables(base_long, False), long_windows(rounded, False)
    powers = jnp.exp(-rate[...] * (ROWS - 1 - iota((ROWS, LANES), 0)).astype(F32))
    yield True
    products = jnp.dot(left, right, preferred_element_type=F32)
    absorbed = absorb(powers, rounded)
    yield True
    store_state(state, absorbed)
    store_state(state_sent, absorbed)
    conv_one[...] = conv.astype(BF16)
    value_two[...] = value.astype(BF16)
    near[...] = (
        pick(products, STRIP_FORWARD, TILE_GROUPS // 2) + weights[SKIP : SKIP + 1] * product
    )
    head[0:2, :] = product[0:2]
    head[2:4, :] = value[0:2]
    head[4:6, :] = conv[0:2]


def late_body(
    grad_two, grad_two_after, value_two, mixed_grad, mixed_after, conv_one, next_head, table,
    grad_li_key, grad_mr_query,
):
    weights = table[...]
    head = next_head[...]
    past_two, past_mixed = grad_two_after[...], mixed_after[...]
    key_grad = grad_two[...].astype(F32) * value_two[...].astype(F32)
    query_grad = mixed_grad[...].astype(F32) * conv_one[...].astype(F32)
    key_past = two_rows(past_two[0:1] * head[2:3], past_two[1:2] * head[3:4])
    query_past = two_rows(past_mixed[0:1] * head[4:5], past_mixed[1:2] * head[5:6])
    yield True
    first = short_backward(key_grad, taps(weights, LI_K), key_past)
    second = short_backward(query_grad, taps(weights, MR_Q), query_past)
    yield True
    grad_li_key[...] = first.astype(BF16)
    grad_mr_query[...] = second.astype(BF16)


def long_body(
    near_ref, start, end, query_two, upstream, following, next_head, table, rate, residue, base_back,
    out, grad_li_query,
):
    weights = table[...]
    near, queries, given = near_ref[...], query_two[...].astype(F32), upstream[...].astype(F32)
    distance = (iota((ROWS + 16, LANES), 0) + 1).astype(F32)
    emit = (residue[...] * jnp.exp(-rate[...] * distance)).astype(BF16)
    started, ending = spread(load_state(start)), spread(load_state(end))
    head = next_head[...]
    impulse = base_back[...]
    after, _ = margins_after(following)
    yield True
    emitted = jnp.dot(emit, started, preferred_element_type=F32)
    ended = jnp.dot(emit[0:16], ending, preferred_element_type=F32)
    yield True
    conv = near + emitted[0:ROWS]
    at_once = on_channels(impulse, 0) + weights[SKIP : SKIP + 1]
    first, second = head[0:1], head[1:2]
    past = emitted[ROWS : ROWS + 8] + ended[0:8]
    past_first = past[0:1] + at_once * first
    past_second = past[1:2] + on_channels(impulse, 1) * first + at_once * second
    grad_past = two_rows(after[4:5] * past_first, after[5:6] * past_second)
    grad = short_backward(given * conv, taps(weights, LI_Q), grad_past)
    yield True
    out[...] = (queries * conv).astype(BF16)
    grad_li_query[...] = grad.astype(BF16)


def medium_back_body(
    conv_grad, after, after_next, keys_one, value_one, beyond, table, base_ref,
    grad_key, grad_value,
):
    weights = table[...]
    later = after[...]
    pair = jnp.concatenate([conv_grad[...], later], 0)
    keys, values = keys_one[...].astype(F32), value_one[...].astype(F32)
    past_kv = beyond[...]
    base = base_ref[...]
    left, first_half = medium_tables(base, True)
    far = on_channels(base, MR_TAPS - 1) * after_next[...].astype(BF16).astype(F32)
    yield True
    products = jnp.dot(left, windows(pair, STRIP_BACK, 0, 2 * LANES), preferred_element_type=F32)
    left_edge = jnp.concatenate([part[0:16] for part in first_half], 0)
    products_edge = jnp.dot(left_edge, later, preferred_element_type=F32)
    yield True
    grad = pick(products, STRIP_BACK, TILE_GROUPS)
    edge = pick(products_edge, 16, TILE_GROUPS)
    past_first, past_second = edge[0:1], edge[1:2] + far
    key_past = two_rows(past_first * past_kv[2:3], past_second * past_kv[3:4])
    value_past = two_rows(past_first * past_kv[0:1], past_second * past_kv[1:2])
    key_grad = short_backward(grad * values, taps(weights, MR_K), key_past)
    value_grad = short_backward(grad * keys, taps(weights, MR_V), value_past)
    yield True
    grad_key[...] = key_grad.astype(BF16)
    grad_value[...] = value_grad.astype(BF16)


def scan_states(states, rates, backward):
    count = states.shape[0]

    def kernel(states_ref, rates_ref, out_ref):
        decay = jnp.exp(rates_ref[...] * (-float(ROWS)))
        carried = jnp.zeros((8, LANES), F32)
        for k in range(count):
            b = count - 1 - k if backward else k
            out_ref[b] = carried.astype(BF16)
            carried = decay * carried + states_ref[b].astype(F32)

    return pl.pallas_call(
        kernel,
        name="scan_back" if backward else "scan_forward",
        out_shape=jax.ShapeDtypeStruct(states.shape, BF16),
        in_specs=[pl.BlockSpec(memory_space=pltpu.VMEM)] * 2,
        out_specs=pl.BlockSpec(memory_space=pltpu.VMEM),
        cost_estimate=cost(2),
    )(states, rates)


def sent(array, by):
    size = lax.axis_size(AXES)
    pairs = [(i, i + by) for i in range(size) if 0 <= i + by < size]
    return lax.ppermute(array, AXES, pairs)


def exchanged(array):
    return lax.all_to_all(array, AXES, split_axis=0, concat_axis=0, tiled=True)


def after(array, *others):
    return lax.optimization_barrier((array, *others))[0]


def per_device(
    mr_query, mr_key, mr_value, li_query, li_key, upstream,
    mr_short, li_short, mr_filter, li_rate, li_residue, li_skip,
):
    channels = mr_query.shape[1]
    tiles = channels // LANES
    assert mr_query.shape[0] == ROWS and lax.axis_size(AXES) == 2 * tiles
    rows = (ROWS, channels)
    full, full32 = (rows, BF16, "r"), (rows, F32, "r")
    half = ((ROWS, channels // 2), BF16, "r")
    state_out = ((2 * tiles, 8, LANES), F32, "s")
    state_sent = ((2 * tiles, 8, LANES), BF16, "s")
    halves = ((0, 2), (1, 2))

    def few(n):
        return ((n, channels), F32, "r")

    last_rows, first_rows, last_kv = edges(mr_query, mr_key, mr_value, li_query, li_key, upstream)
    prev = sent(last_rows, 1)
    following = sent(first_rows, -1)
    before_kv = sent(last_kv, 2)

    table, medium, medium_turned, long, long_turned = make_tables(
        mr_short, li_short, li_skip[None, :], mr_filter, li_rate, li_residue
    )
    rate = li_rate.reshape(1, channels)
    residue = li_residue.reshape(1, channels)
    me = lax.axis_index(AXES)
    my_rates = lax.dynamic_slice(
        li_rate, ((me // 2) * TILE_GROUPS, (me % 2) * 8), (TILE_GROUPS, 8)
    )
    my_rates = jnp.repeat(my_rates.T, GROUP, axis=1)

    key_in = after(mr_key, before_kv, following)
    into = {}
    signal_one = []
    for n, part in enumerate(halves):
        got = lane_call(
            product_one_body, "product_one", channels,
            [(key_in, "r"), (mr_value, "r"), (prev, "r"), (following, "r"), (table, "r")],
            [full, full, few(4), half], 4, part, into,
        )
        signal_one.append(got[3])
        into = dict(enumerate(got[:3]))
    keys_one, value_one, beyond_one = got[:3]
    before_one = [sent(signal, 1) for signal in signal_one]

    query_two, cotangent, state_back = lane_call(
        upstream_body, "upstream", channels,
        [(after(li_query, *signal_one), "r"), (upstream, "r"), (prev, "r"), (table, "r"),
         (rate, "r")],
        [full, full, state_sent], 7,
    )
    gathered_back = exchanged(state_back)
    (near_back,) = lane_call(
        long_back_near_body, "long_back_near", channels,
        [(cotangent, "r"), (table, "r"), (long_turned, "g")],
        [full32], 8, unroll=4,
    )

    def forward(n, into):
        return lane_call(
            forward_body, "forward", channels,
            [(before_one[n], "r"), (before_kv, "r"), (signal_one[n], "r"), (mr_query, "r"),
             (li_key, "r"), (prev, "r"), (table, "r"), (medium, "g"), (long, "g"), (rate, "r")],
            [full, full, full32, state_out, state_sent, few(6)],
            13, halves[n], into, unroll=2,
        )

    got_forward = forward(0, {})
    gathered_back = after(gathered_back, near_back, got_forward[0])
    closing = exchanged(scan_states(gathered_back, my_rates, True))
    conv_one, value_two, near, state, state_outgoing, head = forward(
        1, dict(enumerate(got_forward))
    )
    next_head = sent(head, -1)
    gathered = exchanged(state_outgoing)

    into = {}
    conv_grad = []
    near_later = after(near_back, conv_one)
    for part in halves:
        got = lane_call(
            long_back_body, "long_back", channels,
            [(near_later, "r"), (closing, "s"), (li_query, "r"), (li_key, "r"), (mr_query, "r"),
             (prev, "r"), (following, "r"), (table, "r"), (rate, "r"), (residue, "r")],
            [full, few(2), full, few(2), few(1), half],
            6, part, into, unroll=4,
        )
        conv_grad.append(got[5])
        into = dict(enumerate(got[:5]))
    grad_two, grad_two_after, mixed_grad, mixed_head, conv_head, _ = got
    after_one = [sent(after(signal, next_head), -1) for signal in conv_grad]
    after_next = sent(conv_head, -2)
    mixed_after = sent(mixed_head, -1)

    gathered = after(gathered, next_head)
    start = exchanged(scan_states(gathered, my_rates, False))
    grad_li_key, grad_mr_query = lane_call(
        late_body, "late", channels,
        [(grad_two, "r"), (grad_two_after, "r"), (value_two, "r"), (mixed_grad, "r"),
         (mixed_after, "r"), (conv_one, "r"), (next_head, "r"), (table, "r")],
        [full, full], 6,
    )

    def medium_back(n, into):
        return lane_call(
            medium_back_body, "medium_back", channels,
            [(conv_grad[n], "r"), (after_one[n], "r"), (after_next, "r"), (keys_one, "r"),
             (value_one, "r"), (beyond_one, "r"), (table, "r"), (medium_turned, "g")],
            [full, full], 7, halves[n], into, unroll=4,
        )

    got = medium_back(0, {})
    start = after(start, grad_li_key, *got)
    output, grad_li_query = lane_call(
        long_body, "long_forward", channels,
        [(near, "r"), (start, "s"), (state, "s"), (query_two, "r"), (upstream, "r"),
         (following, "r"), (next_head, "r"), (table, "r"), (rate, "r"), (residue, "r"),
         (long_turned, "g")],
        [full, full], 9, unroll=4,
    )
    grad_mr_key, grad_mr_value = medium_back(1, dict(enumerate(got)))
    return (output, grad_mr_query, grad_mr_key, grad_mr_value, grad_li_query, grad_li_key)


def solution(mesh):
    split = P(("ctx", "ch"), None)
    return jax.shard_map(
        per_device,
        mesh=mesh,
        in_specs=(split,) * 6 + (P(),) * 6,
        out_specs=(split,) * 6,
        check_vma=False,
    )
```

```python
import jax
import jax.numpy as jnp
from jax import lax
from jax.experimental import pallas as pl
from jax.experimental.pallas import tpu as pltpu
from jax.sharding import PartitionSpec as P

GROUP = 16
SHORT = 3
MR_TAPS = 128
MODES = 16
ROWS = 128
LANES = 128
STRIP_FORWARD = 32
STRIP_BACK = 64
TILE_GROUPS = LANES // GROUP
AXES = ("ctx", "ch")
BF16 = jnp.bfloat16
F32 = jnp.float32
VMEM_LIMIT = 56 * 1024 * 1024

MR_Q, MR_K, MR_V, LI_Q, LI_K, LI_V, SKIP = 0, 3, 6, 9, 12, 15, 18
TABLE_ROWS = 24


def cost(microseconds):
    return pl.CostEstimate(
        flops=0, bytes_accessed=int(microseconds * 3.6e6), transcendentals=0
    )


def hint(start, of):
    return start if isinstance(start, int) else pl.multiple_of(start, of)


def lane_call(body, name, channels, ins, outs, us, part=(0, 1), into=None, width=1024, unroll=4):
    span = channels // part[1]
    width = min(width, span)
    tiles = width // LANES
    unroll = min(unroll, tiles)
    blocks = span // width
    into = into or {}
    kinds = [kind for _, kind in ins] + [kind for _, _, kind in outs]
    shapes = [a.shape for a, _ in ins] + [shape for shape, _, _ in outs]
    dtypes = [a.dtype for a, _ in ins] + [dtype for _, dtype, _ in outs]
    count, count_in, count_into = len(kinds), len(ins), len(into)

    def channels_of(shape, kind):
        return {"r": shape[-1], "g": shape[0] * GROUP, "s": shape[0] * (LANES // 2)}[kind]

    def cut(ref, kind, start, size):
        if kind == "r":
            return ref.at[:, pl.ds(hint(start, LANES), size)]
        if kind == "g":
            return ref.at[pl.ds(hint(start // GROUP, TILE_GROUPS), size // GROUP), :]
        return ref.at[pl.ds(start // (LANES // 2), size // (LANES // 2))]

    def kept(shape, kind):
        if kind == "r":
            return (shape[0], span)
        return (span // GROUP, shape[1]) if kind == "g" else (span // (LANES // 2), *shape[1:])

    first = [
        part[0] * span if channels_of(shape, kind) == channels else 0
        for shape, kind in zip(shapes, kinds)
    ]

    def kernel(*refs):
        far = refs[:count_in] + refs[count_in + count_into : count + count_into]
        held = refs[count + count_into : -1]
        arrived = refs[-1]

        def copy(n, b):
            outside = cut(far[n], kinds[n], first[n] + b * width, width)
            inside = cut(held[n], kinds[n], b * width, width)
            if n < count_in:
                return pltpu.make_async_copy(outside, inside, arrived.at[n, b])
            return pltpu.make_async_copy(inside, outside, arrived.at[n, b])

        for b in range(blocks):
            for n in range(count_in):
                copy(n, b).start()

        def block(b, unused):
            for n in range(count_in):
                copy(n, b).wait()

            def step(k, unused):
                running = []
                for u in range(unroll):
                    start = b * width + (k * unroll + u) * LANES
                    running.append(
                        body(*[cut(ref, kind, start, LANES) for ref, kind in zip(held, kinds)])
                    )
                while running:
                    running = [tile for tile in running if next(tile, False)]
                return unused

            lax.fori_loop(0, tiles // unroll, step, 0)
            for n in range(count_in, count):
                copy(n, b).start()
            return unused

        lax.fori_loop(0, blocks, block, 0)
        for b in range(blocks):
            for n in range(count_in, count):
                copy(n, b).wait()

    anywhere = pl.BlockSpec(memory_space=pl.ANY)
    return pl.pallas_call(
        kernel,
        name=name,
        in_specs=[anywhere] * (count_in + count_into),
        out_specs=[anywhere] * len(outs),
        out_shape=[jax.ShapeDtypeStruct(shape, dtype) for shape, dtype, _ in outs],
        scratch_shapes=[
            *[pltpu.VMEM(kept(*which), dtype) for *which, dtype in zip(shapes, kinds, dtypes)],
            pltpu.SemaphoreType.DMA((count, blocks)),
        ],
        input_output_aliases={count_in + n: at for n, at in enumerate(into)},
        compiler_params=pltpu.CompilerParams(vmem_limit_bytes=VMEM_LIMIT),
        cost_estimate=cost(us),
    )(*[a for a, _ in ins], *into.values())


def turned(x, by):
    return pltpu.roll(x, by, 0) if by else x


def taps(table, first):
    return [table[first + j : first + j + 1, :] for j in range(SHORT)]


def short_forward(signal, weights, prev8):
    total = weights[0] * signal
    first = iota((8, LANES), 0)
    for by in (1, 2):
        moved = turned(signal, by)
        top = jnp.where(first < by, turned(prev8, by), moved[0:8])
        rest = [moved[8:]] if signal.shape[0] > 8 else []
        total += weights[by] * jnp.concatenate([top, *rest], 0)
    return total


def short_backward(signal, weights, next8):
    total = weights[0] * signal
    rows = signal.shape[0]
    last = iota((8, LANES), 0)
    for by in (1, 2):
        moved = turned(signal, rows - by)
        bottom = jnp.where(last >= 8 - by, turned(next8, 8 - by), moved[rows - 8 :])
        total += weights[by] * jnp.concatenate([moved[: rows - 8], bottom], 0)
    return total


def two_rows(first, second):
    at = iota((8, LANES), 0)
    return jnp.where(at == 0, first, jnp.where(at == 1, second, 0.0))


def iota(shape, dim):
    return lax.broadcasted_iota(jnp.int32, shape, dim)


def circulant(base, g, rows, shift=0):
    row = jnp.broadcast_to(base[g : g + 1, :], (rows, LANES))
    return pltpu.roll(row, shift, 1, stride=1, stride_axis=0)


def pick(products, rows, count):
    columns = LANES // count
    owner = iota((rows, LANES), 1) // columns
    picked = []
    for q in range(products.shape[1] // LANES):
        at = slice(q * LANES, (q + 1) * LANES)
        total = products[0:rows, at]
        for p in range(1, count):
            total = jnp.where(owner == p, products[p * rows : (p + 1) * rows, at], total)
        picked.append(total)
    return jnp.concatenate(picked, 0)


def windows(signal, strip, first, length):
    count = signal.shape[0]
    parts = []
    for q in range(ROWS // strip):
        low, high = strip * q + first, strip * q + first + length
        inside = signal[max(low, 0) : min(high, count)]
        pieces = [inside]
        if low < 0:
            pieces.insert(0, jnp.zeros((-low, LANES), signal.dtype))
        if high > count:
            pieces.append(jnp.zeros((high - count, LANES), signal.dtype))
        parts.append(jnp.concatenate(pieces, 0) if len(pieces) > 1 else inside)
    return jnp.concatenate(parts, 1)


def split_groups(signal):
    odd = ((iota(signal.shape, 1) // GROUP) % 2).astype(F32)
    return signal * (1.0 - odd).astype(signal.dtype), signal * odd.astype(signal.dtype)


def long_tables(base_ref, backward):
    strip = STRIP_BACK if backward else STRIP_FORWARD
    base = base_ref[...]
    row, lane = iota((strip, LANES), 0), iota((strip, LANES), 1)
    first = 0 if backward else strip - LANES
    keep = lane >= row if backward else lane + first <= row
    tables = [
        jnp.where(keep, circulant(base, g, strip, -first), 0.0).astype(BF16)
        for g in range(TILE_GROUPS)
    ]
    return jnp.concatenate(
        [jnp.concatenate(tables[0::2], 0), jnp.concatenate(tables[1::2], 0)], 1
    )


def long_windows(signal, backward):
    strip = STRIP_BACK if backward else STRIP_FORWARD
    first = 0 if backward else strip - LANES
    even, odd = split_groups(signal)
    return jnp.concatenate(
        [windows(even, strip, first, LANES), windows(odd, strip, first, LANES)], 0
    )


def medium_tables(base, backward):
    strip = STRIP_BACK if backward else STRIP_FORWARD
    row, lane = iota((strip, LANES), 0), iota((strip, LANES), 1)
    keep = lane >= row if backward else lane > row
    wholes = [circulant(base, g, strip) for g in range(TILE_GROUPS)]
    first = [jnp.where(keep, whole, 0.0).astype(BF16) for whole in wholes]
    second = [jnp.where(keep, 0.0, whole).astype(BF16) for whole in wholes]
    return jnp.concatenate([jnp.concatenate(first, 0), jnp.concatenate(second, 0)], 1), first


def on_channels(base, column):
    own = iota((TILE_GROUPS, LANES), 0) == iota((TILE_GROUPS, LANES), 1) // GROUP
    return jnp.where(own, base[:, column : column + 1], 0.0).sum(0, keepdims=True)


def own_group():
    return (iota((LANES, LANES), 0) // MODES == iota((LANES, LANES), 1) // GROUP).astype(F32)


def spread(state):
    return (jnp.concatenate([state] * TILE_GROUPS, 0) * own_group()).astype(BF16)


def absorb(powers, signal):
    every = lax.dot_general(
        powers.astype(BF16), signal, (((0,), (0,)), ((), ())), preferred_element_type=F32
    )
    return (every * own_group()).reshape(TILE_GROUPS, MODES, LANES).sum(0)


def store_state(ref, state):
    ref[...] = state.reshape(2, 8, LANES).astype(ref.dtype)


def load_state(ref):
    return ref[...].astype(F32).reshape(MODES, LANES)


def margins_before(ref):
    rows = ref[...].astype(F32)
    return rows[0:8], rows[8:16]


def margins_after(ref):
    rows = ref[...].astype(F32)
    return rows[0:8], rows[8:16]


def edges(mr_query, mr_key, mr_value, li_query, li_key, upstream):
    channels = mr_query.shape[1]
    width = channels

    def kernel(q_end, k_end, v_end, lq_end, lk_end, lq, lk, g, k, v, last, first, a, b):
        a[0:4, :] = k_end[...].astype(F32)[12:16]
        a[4:8, :] = v_end[...].astype(F32)[12:16]
        a[8:12, :] = q_end[...].astype(F32)[12:16]
        a[12:14, :] = lq_end[...].astype(F32)[14:16]
        a[14:16, :] = lk_end[...].astype(F32)[14:16]
        for n, ref in enumerate((lq, lk, g, k, v)):
            b[2 * n : 2 * n + 2, :] = ref[...].astype(F32)[0:2]
        b[10:16, :] = jnp.zeros((6, width), F32)
        last[...] = a[...].astype(BF16)
        first[...] = b[...].astype(BF16)

    low = pl.BlockSpec((16, width), lambda i: (ROWS // 16 - 1, i))
    high = pl.BlockSpec((16, width), lambda i: (0, i))
    small = jax.ShapeDtypeStruct((16, channels), BF16)
    return pl.pallas_call(
        kernel,
        name="edges",
        grid=(channels // width,),
        in_specs=[low] * 5 + [high] * 5,
        out_specs=[high, high],
        out_shape=[small, small],
        scratch_shapes=[pltpu.VMEM((16, width), F32)] * 2,
        compiler_params=pltpu.CompilerParams(vmem_limit_bytes=VMEM_LIMIT),
        cost_estimate=cost(3.5),
    )(mr_query, mr_key, mr_value, li_query, li_key, li_query, li_key, upstream, mr_key, mr_value)


def make_tables(mr_short, li_short, li_skip, mr_filter, li_rate, li_residue):
    groups = mr_filter.shape[1]
    channels = groups * GROUP
    block = min(128, groups)
    width = block * GROUP

    def kernel(mr, li, skip, filters, rate, residue, table, medium, medium_back, long, long_back):
        for n in range(3):
            table[3 * n : 3 * n + 3, :] = mr[n].astype(F32)
            table[9 + 3 * n : 12 + 3 * n, :] = li[n].astype(F32)
        table[SKIP : SKIP + 1, :] = skip[...]
        table[SKIP + 1 :, :] = jnp.zeros((TABLE_ROWS - SKIP - 1, width), F32)
        row, lane = iota((LANES, LANES), 0), iota((LANES, LANES), 1)
        same = (row == lane).astype(F32).astype(BF16)
        turn = (row == (LANES - lane) % LANES).astype(F32).astype(BF16)
        by_rows = (((0,), (0,)), ((), ()))
        medium[...] = lax.dot_general(filters[...], turn, by_rows, preferred_element_type=F32)
        medium_back[...] = lax.dot_general(filters[...], same, by_rows, preferred_element_type=F32)
        position = iota((block, LANES), 1).astype(F32)
        impulse = jnp.zeros((block, LANES), F32)
        for n in range(MODES):
            impulse += residue[:, n : n + 1] * jnp.exp(-rate[:, n : n + 1] * position)
        long_back[...] = impulse
        long[...] = jnp.dot(impulse.astype(BF16), turn, preferred_element_type=F32)

    shorts = pl.BlockSpec((3, 3, width), lambda i: (0, 0, i))
    modes = pl.BlockSpec((block, MODES), lambda i: (i, 0))
    by_tap = pl.BlockSpec((block, LANES), lambda i: (i, 0))
    shapes = [jax.ShapeDtypeStruct((TABLE_ROWS, channels), F32)]
    shapes += [jax.ShapeDtypeStruct((groups, LANES), F32)] * 4
    return pl.pallas_call(
        kernel,
        name="tables",
        grid=(groups // block,),
        in_specs=[
            shorts, shorts, pl.BlockSpec((1, width), lambda i: (0, i)),
            pl.BlockSpec((MR_TAPS, block), lambda i: (0, i)), modes, modes,
        ],
        out_specs=[pl.BlockSpec((TABLE_ROWS, width), lambda i: (0, i))] + [by_tap] * 4,
        out_shape=shapes,
        compiler_params=pltpu.CompilerParams(vmem_limit_bytes=VMEM_LIMIT),
        cost_estimate=cost(5),
    )(mr_short, li_short, li_skip, mr_filter, li_rate, li_residue)


def product_one_body(key, value, prev, table, out):
    weights = table[...]
    before, _ = margins_before(prev)
    w_k, w_v = taps(weights, MR_K), taps(weights, MR_V)
    signal_k, signal_v = key[...].astype(F32), value[...].astype(F32)
    yield True
    k = short_forward(signal_k, w_k, turned(before, 4))
    v = short_forward(signal_v, w_v, before)
    yield True
    out[...] = (k * v).astype(BF16)


def upstream_body(li_query, upstream, prev, table, rate, cotangent, state):
    weights = table[...]
    _, margin = margins_before(prev)
    signal, given, decay = li_query[...].astype(F32), upstream[...].astype(F32), rate[...]
    yield True
    powers = jnp.exp(-decay * iota((ROWS, LANES), 0).astype(F32))
    query_two = short_forward(signal, taps(weights, LI_Q), turned(margin, 2))
    rounded = (given * query_two).astype(BF16)
    yield True
    absorbed = absorb(powers, rounded)
    yield True
    store_state(state, absorbed)
    cotangent[...] = rounded


def long_back_near_body(cotangent, table, base, near):
    signal = cotangent[...]
    skip = table[SKIP : SKIP + 1, :]
    left, right = long_tables(base, True), long_windows(signal, True)
    yield True
    products = jnp.dot(left, right, preferred_element_type=F32)
    yield True
    product = pick(products, STRIP_BACK, TILE_GROUPS // 2) + skip * signal.astype(F32)
    near[...] = product.astype(BF16)


def long_back_body(
    near_ref, closing, li_query, li_key, query, prev, following, table, rate, residue,
    grad_two, grad_two_after, mixed_grad, mixed_head, out_head, out,
):
    weights = table[...]
    _, before = margins_before(prev)
    after, _ = margins_after(following)
    near, state = near_ref[...].astype(F32), load_state(closing)
    key, queries = li_key[...].astype(F32), query[...].astype(F32)
    query_end = li_query[ROWS - 16 :, :].astype(F32)[8:16]
    distance = (ROWS - iota((ROWS + 16, LANES), 0)).astype(F32)
    emit = (residue[...] * jnp.exp(-rate[...] * distance)).astype(BF16)
    cot_after = turned(after, 4) * short_forward(after, taps(weights, LI_Q), query_end)
    yield True
    emitted = jnp.dot(emit, spread(state), preferred_element_type=F32)
    later = jnp.dot(emit[ROWS:], spread(state - cot_after[0:1]), preferred_element_type=F32)
    yield True
    skip = weights[SKIP : SKIP + 1]
    own = near + emitted[0:ROWS]
    at_row = iota((8, LANES), 0)
    past = jnp.where(at_row == 0, emitted[ROWS : ROWS + 8], later[0:8]) + skip * cot_after
    past = jnp.where(at_row < 2, past, 0.0)
    w_k = taps(weights, LI_K)
    keys_two = short_forward(key, w_k, before)
    keys_after = short_forward(turned(after, 6), w_k, key[ROWS - 8 :])
    mixed = short_backward(own * keys_two, taps(weights, LI_V), past * keys_after)
    queries = short_forward(queries, taps(weights, MR_Q), turned(before, 4))
    conv_grad = mixed * queries
    yield True
    grad_two[...] = own.astype(BF16)
    grad_two_after[...] = past[0:2]
    mixed_grad[...] = mixed.astype(BF16)
    mixed_head[...] = mixed[0:2]
    out[...] = conv_grad.astype(BF16)
    out_head[...] = conv_grad[0:1]


def forward_body(
    before, before_kv, signal, query, key, prev, table, base_ref, base_long,
    rate, conv_one, value_two, near, state, head,
):
    weights = table[...]
    earlier = before[...]
    pair = jnp.concatenate([earlier, signal[...]], 0)
    queries, keys = query[...].astype(F32), key[...].astype(F32)
    _, margin = margins_before(prev)
    raw, _ = margins_before(before_kv)
    base = base_ref[...]
    left, _ = medium_tables(base, False)
    row, lane = iota((16, LANES), 0), iota((16, LANES), 1)
    left_edge = jnp.concatenate(
        [
            jnp.where(lane <= row + (ROWS - 16), circulant(base, g, 16, ROWS - 16), 0.0).astype(BF16)
            for g in range(TILE_GROUPS)
        ],
        0,
    )
    yield True
    products = jnp.dot(
        left, windows(pair, STRIP_FORWARD, 0, 2 * LANES), preferred_element_type=F32
    )
    products_edge = jnp.dot(left_edge, earlier, preferred_element_type=F32)
    yield True
    query_one = short_forward(queries, taps(weights, MR_Q), turned(margin, 4))
    keys_two = short_forward(keys, taps(weights, LI_K), margin)
    conv = pick(products, STRIP_FORWARD, TILE_GROUPS)
    edge = pick(products_edge, 16, TILE_GROUPS)
    w_k, w_v = taps(weights, MR_K), taps(weights, MR_V)
    key_last = w_k[0] * raw[3:4] + w_k[1] * raw[2:3] + w_k[2] * raw[1:2]
    value_last = w_v[0] * raw[7:8] + w_v[1] * raw[6:7] + w_v[2] * raw[5:6]
    far = on_channels(base, 1) * (key_last * value_last).astype(BF16).astype(F32)
    conv_before = edge[8:16] + jnp.where(iota((8, LANES), 0) == 6, far, 0.0)
    w = taps(weights, MR_Q)
    query_before = w[0] * margin + w[1] * turned(margin, 1) + w[2] * turned(margin, 2)
    mixed_before = turned(query_before, 4) * conv_before
    mixed = (query_one * conv).astype(BF16).astype(F32)
    value = short_forward(mixed, taps(weights, LI_V), mixed_before.astype(BF16).astype(F32))
    product = keys_two * value
    rounded = product.astype(BF16)
    yield True
    left, right = long_tables(base_long, False), long_windows(rounded, False)
    powers = jnp.exp(-rate[...] * (ROWS - 1 - iota((ROWS, LANES), 0)).astype(F32))
    yield True
    products = jnp.dot(left, right, preferred_element_type=F32)
    absorbed = absorb(powers, rounded)
    yield True
    store_state(state, absorbed)
    conv_one[...] = conv.astype(BF16)
    value_two[...] = value.astype(BF16)
    own = pick(products, STRIP_FORWARD, TILE_GROUPS // 2) + weights[SKIP : SKIP + 1] * product
    near[...] = own.astype(BF16)
    head[0:2, :] = product[0:2]
    head[2:4, :] = value[0:2]
    head[4:6, :] = conv[0:2]


def late_body(
    grad_two, grad_two_after, value_two, mixed_grad, mixed_after, conv_one, next_head, table,
    grad_li_key, grad_mr_query,
):
    weights = table[...]
    head = next_head[...]
    past_two, past_mixed = grad_two_after[...], mixed_after[...]
    key_grad = grad_two[...].astype(F32) * value_two[...].astype(F32)
    query_grad = mixed_grad[...].astype(F32) * conv_one[...].astype(F32)
    key_past = two_rows(past_two[0:1] * head[2:3], past_two[1:2] * head[3:4])
    query_past = two_rows(past_mixed[0:1] * head[4:5], past_mixed[1:2] * head[5:6])
    yield True
    first = short_backward(key_grad, taps(weights, LI_K), key_past)
    second = short_backward(query_grad, taps(weights, MR_Q), query_past)
    yield True
    grad_li_key[...] = first.astype(BF16)
    grad_mr_query[...] = second.astype(BF16)


def long_body(
    near_ref, start, end, li_query, upstream, prev, following, next_head, table, rate, residue,
    base_back,
    out, grad_li_query,
):
    weights = table[...]
    near, queries, given = (ref[...].astype(F32) for ref in (near_ref, li_query, upstream))
    distance = (iota((ROWS + 16, LANES), 0) + 1).astype(F32)
    emit = (residue[...] * jnp.exp(-rate[...] * distance)).astype(BF16)
    started, ending = spread(load_state(start)), spread(load_state(end))
    head = next_head[...]
    impulse = base_back[...]
    after, _ = margins_after(following)
    _, margin = margins_before(prev)
    yield True
    emitted = jnp.dot(emit, started, preferred_element_type=F32)
    ended = jnp.dot(emit[0:16], ending, preferred_element_type=F32)
    yield True
    conv = near + emitted[0:ROWS]
    queries = short_forward(queries, taps(weights, LI_Q), turned(margin, 2))
    at_once = on_channels(impulse, 0) + weights[SKIP : SKIP + 1]
    first, second = head[0:1], head[1:2]
    past = emitted[ROWS : ROWS + 8] + ended[0:8]
    past_first = past[0:1] + at_once * first
    past_second = past[1:2] + on_channels(impulse, 1) * first + at_once * second
    grad_past = two_rows(after[4:5] * past_first, after[5:6] * past_second)
    grad = short_backward(given * conv, taps(weights, LI_Q), grad_past)
    yield True
    out[...] = (queries * conv).astype(BF16)
    grad_li_query[...] = grad.astype(BF16)


def medium_back_body(
    conv_grad, after, after_next, key, value, prev, following, table, base_ref,
    grad_key, grad_value,
):
    weights = table[...]
    later = after[...]
    pair = jnp.concatenate([conv_grad[...], later], 0)
    keys, values = key[...].astype(F32), value[...].astype(F32)
    before, _ = margins_before(prev)
    next_keys, next_values = margins_after(following)
    base = base_ref[...]
    left, first_half = medium_tables(base, True)
    far = on_channels(base, MR_TAPS - 1) * after_next[...].astype(BF16).astype(F32)
    yield True
    products = jnp.dot(left, windows(pair, STRIP_BACK, 0, 2 * LANES), preferred_element_type=F32)
    left_edge = jnp.concatenate([part[0:16] for part in first_half], 0)
    products_edge = jnp.dot(left_edge, later, preferred_element_type=F32)
    yield True
    grad = pick(products, STRIP_BACK, TILE_GROUPS)
    edge = pick(products_edge, 16, TILE_GROUPS)
    past_first, past_second = edge[0:1], edge[1:2] + far
    w_k, w_v = taps(weights, MR_K), taps(weights, MR_V)
    keys_past = short_forward(turned(next_keys, 2), w_k, keys[ROWS - 8 :])
    values_past = short_forward(next_values, w_v, values[ROWS - 8 :])
    keys = short_forward(keys, w_k, turned(before, 4))
    values = short_forward(values, w_v, before)
    key_past = two_rows(past_first * values_past[0:1], past_second * values_past[1:2])
    value_past = two_rows(past_first * keys_past[0:1], past_second * keys_past[1:2])
    key_grad = short_backward(grad * values, taps(weights, MR_K), key_past)
    value_grad = short_backward(grad * keys, taps(weights, MR_V), value_past)
    yield True
    grad_key[...] = key_grad.astype(BF16)
    grad_value[...] = value_grad.astype(BF16)


def scan_states(states, rates, backward):
    count = states.shape[0]

    def kernel(states_ref, rates_ref, out_ref):
        decay = jnp.exp(rates_ref[...] * (-float(ROWS)))
        carried = jnp.zeros((8, LANES), F32)
        for k in range(count):
            b = count - 1 - k if backward else k
            out_ref[b] = carried
            carried = decay * carried + states_ref[b]

    return pl.pallas_call(
        kernel,
        name="scan_back" if backward else "scan_forward",
        out_shape=jax.ShapeDtypeStruct(states.shape, F32),
        in_specs=[pl.BlockSpec(memory_space=pltpu.VMEM)] * 2,
        out_specs=pl.BlockSpec(memory_space=pltpu.VMEM),
        cost_estimate=cost(2),
    )(states, rates)


def sent(array, by):
    size = lax.axis_size(AXES)
    pairs = [(i, i + by) for i in range(size) if 0 <= i + by < size]
    return lax.ppermute(array, AXES, pairs)


def exchanged(array):
    return lax.all_to_all(array, AXES, split_axis=0, concat_axis=0, tiled=True)


def after(array, *others):
    return lax.optimization_barrier((array, *others))[0]


def per_device(
    mr_query, mr_key, mr_value, li_query, li_key, upstream,
    mr_short, li_short, mr_filter, li_rate, li_residue, li_skip,
):
    channels = mr_query.shape[1]
    tiles = channels // LANES
    assert mr_query.shape[0] == ROWS and lax.axis_size(AXES) == 2 * tiles
    rows = (ROWS, channels)
    full = (rows, BF16, "r")
    half = ((ROWS, channels // 2), BF16, "r")
    state_out = ((2 * tiles, 8, LANES), F32, "s")
    halves = ((0, 2), (1, 2))

    def few(n):
        return ((n, channels), F32, "r")

    last_rows, first_rows = edges(mr_query, mr_key, mr_value, li_query, li_key, upstream)
    prev = sent(last_rows, 1)
    following = sent(first_rows, -1)
    before_kv = sent(last_rows, 2)

    table, medium, medium_turned, long, long_turned = make_tables(
        mr_short, li_short, li_skip[None, :], mr_filter, li_rate, li_residue
    )
    rate = li_rate.reshape(1, channels)
    residue = li_residue.reshape(1, channels)
    me = lax.axis_index(AXES)
    my_rates = lax.dynamic_slice(
        li_rate, ((me // 2) * TILE_GROUPS, (me % 2) * 8), (TILE_GROUPS, 8)
    )
    my_rates = jnp.repeat(my_rates.T, GROUP, axis=1)

    cotangent, state_back = lane_call(
        upstream_body, "upstream", channels,
        [(li_query, "r"), (upstream, "r"), (prev, "r"), (table, "r"), (rate, "r")],
        [full, state_out], 5,
    )
    gathered_back = exchanged(state_back)
    (near_back,) = lane_call(
        long_back_near_body, "long_back_near", channels,
        [(cotangent, "r"), (table, "r"), (long_turned, "g")],
        [full], 6,
    )
    gathered_back = after(gathered_back, following, before_kv, near_back)
    carries_back = scan_states(gathered_back, my_rates, True)
    closing = exchanged(carries_back)

    key_in = after(mr_key, carries_back)
    signal_one = [
        lane_call(
            product_one_body, "product_one", channels,
            [(key_in, "r"), (mr_value, "r"), (prev, "r"), (table, "r")],
            [half], 3, part,
        )[0]
        for part in halves
    ]
    before_one = [sent(signal, 1) for signal in signal_one]

    into = {}
    conv_grad = []
    for part in halves:
        got = lane_call(
            long_back_body, "long_back", channels,
            [(near_back, "r"), (closing, "s"), (li_query, "r"), (li_key, "r"), (mr_query, "r"),
             (prev, "r"), (following, "r"), (table, "r"), (rate, "r"), (residue, "r")],
            [full, few(2), full, few(2), few(1), half],
            5, part, into,
        )
        conv_grad.append(got[5])
        into = dict(enumerate(got[:5]))
    grad_two, grad_two_after, mixed_grad, mixed_head, conv_head, _ = got
    after_one = [sent(signal, -1) for signal in conv_grad]
    after_next = sent(conv_head, -2)
    mixed_after = sent(mixed_head, -1)

    into = {}
    for n, part in enumerate(halves):
        got = lane_call(
            forward_body, "forward", channels,
            [(before_one[n], "r"), (before_kv, "r"), (signal_one[n], "r"), (mr_query, "r"),
             (li_key, "r"), (prev, "r"), (table, "r"), (medium, "g"), (long, "g"), (rate, "r")],
            [full, full, full, state_out, few(6)],
            12, part, into, unroll=2,
        )
        into = dict(enumerate(got))
    conv_one, value_two, near, state, head = got
    next_head = sent(head, -1)
    gathered = exchanged(state)

    def medium_back(n, into):
        return lane_call(
            medium_back_body, "medium_back", channels,
            [(conv_grad[n], "r"), (after_one[n], "r"), (after_next, "r"), (mr_key, "r"),
             (mr_value, "r"), (prev, "r"), (following, "r"), (table, "r"), (medium_turned, "g")],
            [full, full], 6, halves[n], into,
        )

    got = medium_back(0, {})
    gathered = after(gathered, next_head, after_next, *got)
    start = exchanged(scan_states(gathered, my_rates, False))
    grad_mr_key, grad_mr_value = medium_back(1, dict(enumerate(got)))
    grad_li_key, grad_mr_query = lane_call(
        late_body, "late", channels,
        [(grad_two, "r"), (grad_two_after, "r"), (value_two, "r"), (mixed_grad, "r"),
         (mixed_after, "r"), (conv_one, "r"), (next_head, "r"), (table, "r")],
        [full, full], 5,
    )
    start = after(start, grad_li_key, grad_mr_key)
    output, grad_li_query = lane_call(
        long_body, "long_forward", channels,
        [(near, "r"), (start, "s"), (state, "s"), (li_query, "r"), (upstream, "r"),
         (prev, "r"), (following, "r"), (next_head, "r"), (table, "r"), (rate, "r"), (residue, "r"),
         (long_turned, "g")],
        [full, full], 7,
    )
    return (output, grad_mr_query, grad_mr_key, grad_mr_value, grad_li_query, grad_li_key)


def solution(mesh):
    split = P(("ctx", "ch"), None)
    return jax.shard_map(
        per_device,
        mesh=mesh,
        in_specs=(split,) * 6 + (P(),) * 6,
        out_specs=(split,) * 6,
        check_vma=False,
    )
```

```python
import jax
import jax.numpy as jnp
from jax import lax
from jax.experimental import pallas as pl
from jax.experimental.pallas import tpu as pltpu
from jax.sharding import PartitionSpec as P

GROUP = 16
SHORT = 3
MR_TAPS = 128
MODES = 16
ROWS = 128
LANES = 128
STRIP_FORWARD = 32
STRIP_BACK = 32
TILE_GROUPS = LANES // GROUP
AXES = ("ctx", "ch")
BF16 = jnp.bfloat16
F32 = jnp.float32
VMEM_LIMIT = 56 * 1024 * 1024

MR_Q, MR_K, MR_V, LI_Q, LI_K, LI_V, SKIP = 0, 3, 6, 9, 12, 15, 18
TABLE_ROWS = 24


def cost(microseconds):
    return pl.CostEstimate(
        flops=0, bytes_accessed=int(microseconds * 3.6e6), transcendentals=0
    )


def hint(start, of):
    return start if isinstance(start, int) else pl.multiple_of(start, of)


def lane_call(body, name, channels, ins, outs, us, part=(0, 1), into=None, width=1024, unroll=4, exts=0):
    span = channels // part[1]
    width = min(width, span)
    tiles = width // LANES
    unroll = min(unroll, tiles)
    blocks = span // width
    into = into or {}
    kinds = [kind for _, kind in ins] + [kind for _, _, kind in outs]
    shapes = [a.shape for a, _ in ins] + [shape for shape, _, _ in outs]
    dtypes = [a.dtype for a, _ in ins] + [dtype for _, dtype, _ in outs]
    count, count_in, count_into = len(kinds), len(ins), len(into)

    def channels_of(shape, kind):
        return {"r": shape[-1], "g": shape[0] * GROUP, "s": shape[0] * (LANES // 2)}[kind]

    def cut(ref, kind, start, size):
        if kind == "r":
            return ref.at[:, pl.ds(hint(start, LANES), size)]
        if kind == "g":
            return ref.at[pl.ds(hint(start // GROUP, TILE_GROUPS), size // GROUP), :]
        return ref.at[pl.ds(start // (LANES // 2), size // (LANES // 2))]

    def kept(shape, kind):
        if kind == "r":
            return (shape[0], span)
        return (span // GROUP, shape[1]) if kind == "g" else (span // (LANES // 2), *shape[1:])

    first = [
        part[0] * span if channels_of(shape, kind) == channels else 0
        for shape, kind in zip(shapes, kinds)
    ]

    def kernel(*refs):
        far = refs[:count_in] + refs[count_in + count_into : count + count_into]
        held = refs[count + count_into : 2 * count + count_into]
        arrived, *extra = refs[2 * count + count_into :]

        def copy(n, b):
            outside = cut(far[n], kinds[n], first[n] + b * width, width)
            inside = cut(held[n], kinds[n], b * width, width)
            if n < count_in:
                return pltpu.make_async_copy(outside, inside, arrived.at[n, b])
            return pltpu.make_async_copy(inside, outside, arrived.at[n, b])

        for b in range(blocks):
            for n in range(count_in):
                copy(n, b).start()

        def block(b, unused):
            for n in range(count_in):
                copy(n, b).wait()

            def step(k, unused):
                running = []
                for u in range(unroll):
                    start = b * width + (k * unroll + u) * LANES
                    running.append(
                        body(
                            *[cut(ref, kind, start, LANES) for ref, kind in zip(held, kinds)],
                            *[ref.at[u, n] for ref in extra for n in range(exts)],
                        )
                    )
                while running:
                    running = [tile for tile in running if next(tile, False)]
                return unused

            lax.fori_loop(0, tiles // unroll, step, 0)
            for n in range(count_in, count):
                copy(n, b).start()
            return unused

        lax.fori_loop(0, blocks, block, 0)
        for b in range(blocks):
            for n in range(count_in, count):
                copy(n, b).wait()

    anywhere = pl.BlockSpec(memory_space=pl.ANY)
    return pl.pallas_call(
        kernel,
        name=name,
        in_specs=[anywhere] * (count_in + count_into),
        out_specs=[anywhere] * len(outs),
        out_shape=[jax.ShapeDtypeStruct(shape, dtype) for shape, dtype, _ in outs],
        scratch_shapes=[
            *[pltpu.VMEM(kept(*which), dtype) for *which, dtype in zip(shapes, kinds, dtypes)],
            pltpu.SemaphoreType.DMA((count, blocks)),
            *([pltpu.VMEM((unroll, exts, ROWS + 16, LANES), F32)] if exts else []),
        ],
        input_output_aliases={count_in + n: at for n, at in enumerate(into)},
        compiler_params=pltpu.CompilerParams(vmem_limit_bytes=VMEM_LIMIT),
        cost_estimate=cost(us),
    )(*[a for a, _ in ins], *into.values())


def turned(x, by):
    return pltpu.roll(x, by, 0) if by else x


def taps(table, first):
    return [table[first + j : first + j + 1, :] for j in range(SHORT)]


def short_forward(signal, weights, prev8):
    total = weights[0] * signal
    first = iota((8, LANES), 0)
    for by in (1, 2):
        moved = turned(signal, by)
        top = jnp.where(first < by, turned(prev8, by), moved[0:8])
        rest = [moved[8:]] if signal.shape[0] > 8 else []
        total += weights[by] * jnp.concatenate([top, *rest], 0)
    return total


def short_backward(signal, weights, next8):
    total = weights[0] * signal
    rows = signal.shape[0]
    last = iota((8, LANES), 0)
    for by in (1, 2):
        moved = turned(signal, rows - by)
        bottom = jnp.where(last >= 8 - by, turned(next8, 8 - by), moved[rows - 8 :])
        total += weights[by] * jnp.concatenate([moved[: rows - 8], bottom], 0)
    return total


def filled(ext, signal, prev8=None, next8=None):
    ext[8 : 8 + ROWS, :] = signal
    if prev8 is not None:
        ext[0:8, :] = prev8
    if next8 is not None:
        ext[8 + ROWS :, :] = next8


def shifted_sum(ext, weights, way, rows=ROWS):
    parts = [w * ext[8 + way * j : 8 + way * j + rows, :] for j, w in enumerate(weights)]
    return parts[0] + parts[1] + parts[2]


def two_rows(first, second):
    at = iota((8, LANES), 0)
    return jnp.where(at == 0, first, jnp.where(at == 1, second, 0.0))


def iota(shape, dim):
    return lax.broadcasted_iota(jnp.int32, shape, dim)


def circulant(base, g, rows, shift=0):
    row = jnp.broadcast_to(base[g : g + 1, :], (rows, LANES))
    return pltpu.roll(row, shift, 1, stride=1, stride_axis=0)


def pick(products, rows, count):
    columns = LANES // count
    owner = iota((rows, LANES), 1) // columns
    picked = []
    for q in range(products.shape[1] // LANES):
        at = slice(q * LANES, (q + 1) * LANES)
        total = products[0:rows, at]
        for p in range(1, count):
            total = jnp.where(owner == p, products[p * rows : (p + 1) * rows, at], total)
        picked.append(total)
    return jnp.concatenate(picked, 0)


def windows(signal, strip, first, length):
    count = signal.shape[0]
    parts = []
    for q in range(ROWS // strip):
        low, high = strip * q + first, strip * q + first + length
        inside = signal[max(low, 0) : min(high, count)]
        pieces = [inside]
        if low < 0:
            pieces.insert(0, jnp.zeros((-low, LANES), signal.dtype))
        if high > count:
            pieces.append(jnp.zeros((high - count, LANES), signal.dtype))
        parts.append(jnp.concatenate(pieces, 0) if len(pieces) > 1 else inside)
    return jnp.concatenate(parts, 1)


def split_groups(signal):
    odd = ((iota(signal.shape, 1) // GROUP) % 2).astype(F32)
    return signal * (1.0 - odd).astype(signal.dtype), signal * odd.astype(signal.dtype)


def long_tables(base_ref, backward):
    strip = STRIP_BACK if backward else STRIP_FORWARD
    base = base_ref[...]
    row, lane = iota((strip, LANES), 0), iota((strip, LANES), 1)
    first = 0 if backward else strip - LANES
    keep = lane >= row if backward else lane + first <= row
    tables = [
        jnp.where(keep, circulant(base, g, strip, -first), 0.0).astype(BF16)
        for g in range(TILE_GROUPS)
    ]
    return jnp.concatenate(
        [jnp.concatenate(tables[0::2], 0), jnp.concatenate(tables[1::2], 0)], 1
    )


def long_windows(signal, backward):
    strip = STRIP_BACK if backward else STRIP_FORWARD
    first = 0 if backward else strip - LANES
    even, odd = split_groups(signal)
    return jnp.concatenate(
        [windows(even, strip, first, LANES), windows(odd, strip, first, LANES)], 0
    )


def medium_tables(base, backward):
    strip = STRIP_BACK if backward else STRIP_FORWARD
    row, lane = iota((strip, LANES), 0), iota((strip, LANES), 1)
    keep = lane >= row if backward else lane > row
    wholes = [circulant(base, g, strip) for g in range(TILE_GROUPS)]
    first = [jnp.where(keep, whole, 0.0).astype(BF16) for whole in wholes]
    second = [jnp.where(keep, 0.0, whole).astype(BF16) for whole in wholes]
    return jnp.concatenate([jnp.concatenate(first, 0), jnp.concatenate(second, 0)], 1), first


def on_channels(base, column):
    own = iota((TILE_GROUPS, LANES), 0) == iota((TILE_GROUPS, LANES), 1) // GROUP
    return jnp.where(own, base[:, column : column + 1], 0.0).sum(0, keepdims=True)


def own_group():
    return (iota((LANES, LANES), 0) // MODES == iota((LANES, LANES), 1) // GROUP).astype(F32)


def spread(state):
    return (jnp.concatenate([state] * TILE_GROUPS, 0) * own_group()).astype(BF16)


def absorb(powers, signal):
    every = lax.dot_general(
        powers.astype(BF16), signal, (((0,), (0,)), ((), ())), preferred_element_type=F32
    )
    return (every * own_group()).reshape(TILE_GROUPS, MODES, LANES).sum(0)


def store_state(ref, state):
    ref[...] = state.reshape(2, 8, LANES).astype(ref.dtype)


def load_state(ref):
    return ref[...].astype(F32).reshape(MODES, LANES)


def margins_before(ref):
    rows = ref[...].astype(F32)
    return rows[0:8], rows[8:16]


def margins_after(ref):
    rows = ref[...].astype(F32)
    return rows[0:8], rows[8:16]


def edges(mr_query, mr_key, mr_value, li_query, li_key, upstream):
    channels = mr_query.shape[1]
    width = channels

    def kernel(q_end, k_end, v_end, lq_end, lk_end, lq, lk, g, k, v, last, first, a, b):
        a[0:4, :] = k_end[...].astype(F32)[12:16]
        a[4:8, :] = v_end[...].astype(F32)[12:16]
        a[8:12, :] = q_end[...].astype(F32)[12:16]
        a[12:14, :] = lq_end[...].astype(F32)[14:16]
        a[14:16, :] = lk_end[...].astype(F32)[14:16]
        for n, ref in enumerate((lq, lk, g, k, v)):
            b[2 * n : 2 * n + 2, :] = ref[...].astype(F32)[0:2]
        b[10:16, :] = jnp.zeros((6, width), F32)
        last[...] = a[...].astype(BF16)
        first[...] = b[...].astype(BF16)

    low = pl.BlockSpec((16, width), lambda i: (ROWS // 16 - 1, i))
    high = pl.BlockSpec((16, width), lambda i: (0, i))
    small = jax.ShapeDtypeStruct((16, channels), BF16)
    return pl.pallas_call(
        kernel,
        name="edges",
        grid=(channels // width,),
        in_specs=[low] * 5 + [high] * 5,
        out_specs=[high, high],
        out_shape=[small, small],
        scratch_shapes=[pltpu.VMEM((16, width), F32)] * 2,
        compiler_params=pltpu.CompilerParams(vmem_limit_bytes=VMEM_LIMIT),
        cost_estimate=cost(3.5),
    )(mr_query, mr_key, mr_value, li_query, li_key, li_query, li_key, upstream, mr_key, mr_value)


def make_tables(mr_short, li_short, li_skip, mr_filter, li_rate, li_residue):
    groups = mr_filter.shape[1]
    channels = groups * GROUP
    block = min(128, groups)
    width = block * GROUP

    def kernel(mr, li, skip, filters, rate, residue, table, medium, medium_back, long, long_back):
        for n in range(3):
            table[3 * n : 3 * n + 3, :] = mr[n].astype(F32)
            table[9 + 3 * n : 12 + 3 * n, :] = li[n].astype(F32)
        table[SKIP : SKIP + 1, :] = skip[...]
        table[SKIP + 1 :, :] = jnp.zeros((TABLE_ROWS - SKIP - 1, width), F32)
        row, lane = iota((LANES, LANES), 0), iota((LANES, LANES), 1)
        same = (row == lane).astype(F32).astype(BF16)
        turn = (row == (LANES - lane) % LANES).astype(F32).astype(BF16)
        by_rows = (((0,), (0,)), ((), ()))
        medium[...] = lax.dot_general(filters[...], turn, by_rows, preferred_element_type=F32)
        medium_back[...] = lax.dot_general(filters[...], same, by_rows, preferred_element_type=F32)
        position = iota((block, LANES), 1).astype(F32)
        impulse = jnp.zeros((block, LANES), F32)
        for n in range(MODES):
            impulse += residue[:, n : n + 1] * jnp.exp(-rate[:, n : n + 1] * position)
        long_back[...] = impulse
        long[...] = jnp.dot(impulse.astype(BF16), turn, preferred_element_type=F32)

    shorts = pl.BlockSpec((3, 3, width), lambda i: (0, 0, i))
    modes = pl.BlockSpec((block, MODES), lambda i: (i, 0))
    by_tap = pl.BlockSpec((block, LANES), lambda i: (i, 0))
    shapes = [jax.ShapeDtypeStruct((TABLE_ROWS, channels), F32)]
    shapes += [jax.ShapeDtypeStruct((groups, LANES), F32)] * 4
    return pl.pallas_call(
        kernel,
        name="tables",
        grid=(groups // block,),
        in_specs=[
            shorts, shorts, pl.BlockSpec((1, width), lambda i: (0, i)),
            pl.BlockSpec((MR_TAPS, block), lambda i: (0, i)), modes, modes,
        ],
        out_specs=[pl.BlockSpec((TABLE_ROWS, width), lambda i: (0, i))] + [by_tap] * 4,
        out_shape=shapes,
        compiler_params=pltpu.CompilerParams(vmem_limit_bytes=VMEM_LIMIT),
        cost_estimate=cost(5),
    )(mr_short, li_short, li_skip, mr_filter, li_rate, li_residue)


def product_one_body(key, value, prev, table, out):
    weights = table[...]
    before, _ = margins_before(prev)
    w_k, w_v = taps(weights, MR_K), taps(weights, MR_V)
    signal_k, signal_v = key[...].astype(F32), value[...].astype(F32)
    yield True
    k = short_forward(signal_k, w_k, turned(before, 4))
    v = short_forward(signal_v, w_v, before)
    yield True
    out[0:ROWS, :] = (k * v).astype(BF16)
    key_last = w_k[0] * before[3:4] + w_k[1] * before[2:3] + w_k[2] * before[1:2]
    value_last = w_v[0] * before[7:8] + w_v[1] * before[6:7] + w_v[2] * before[5:6]
    out[ROWS:, :] = jnp.broadcast_to(key_last * value_last, (16, LANES)).astype(BF16)


def upstream_body(li_query, upstream, prev, table, rate, cotangent, state):
    weights = table[...]
    _, margin = margins_before(prev)
    signal, given, decay = li_query[...].astype(F32), upstream[...].astype(F32), rate[...]
    yield True
    powers = jnp.exp(-decay * iota((ROWS, LANES), 0).astype(F32))
    query_two = short_forward(signal, taps(weights, LI_Q), turned(margin, 2))
    rounded = (given * query_two).astype(BF16)
    yield True
    absorbed = absorb(powers, rounded)
    yield True
    store_state(state, absorbed)
    cotangent[...] = rounded


def long_back_near_body(cotangent, table, base, near):
    signal = cotangent[...]
    skip = table[SKIP : SKIP + 1, :]
    left, right = long_tables(base, True), long_windows(signal, True)
    yield True
    products = jnp.dot(left, right, preferred_element_type=F32)
    yield True
    product = pick(products, STRIP_BACK, TILE_GROUPS // 2) + skip * signal.astype(F32)
    near[...] = product.astype(BF16)


def long_back_body(
    near_ref, closing, li_query, li_key, query, prev, following, table, rate, residue,
    grad_two, grad_two_after, mixed_grad, mixed_head, out_head, out,
):
    weights = table[...]
    _, before = margins_before(prev)
    after, _ = margins_after(following)
    near, state = near_ref[...].astype(F32), load_state(closing)
    key, queries = li_key[...].astype(F32), query[...].astype(F32)
    query_end = li_query[ROWS - 16 :, :].astype(F32)[8:16]
    distance = (ROWS - iota((ROWS + 16, LANES), 0)).astype(F32)
    emit = (residue[...] * jnp.exp(-rate[...] * distance)).astype(BF16)
    cot_after = turned(after, 4) * short_forward(after, taps(weights, LI_Q), query_end)
    yield True
    emitted = jnp.dot(emit, spread(state), preferred_element_type=F32)
    later = jnp.dot(emit[ROWS:], spread(state - cot_after[0:1]), preferred_element_type=F32)
    yield True
    skip = weights[SKIP : SKIP + 1]
    own = near + emitted[0:ROWS]
    at_row = iota((8, LANES), 0)
    past = jnp.where(at_row == 0, emitted[ROWS : ROWS + 8], later[0:8]) + skip * cot_after
    past = jnp.where(at_row < 2, past, 0.0)
    w_k = taps(weights, LI_K)
    keys_two = short_forward(key, w_k, before)
    keys_after = short_forward(turned(after, 6), w_k, key[ROWS - 8 :])
    mixed = short_backward(own * keys_two, taps(weights, LI_V), past * keys_after)
    queries = short_forward(queries, taps(weights, MR_Q), turned(before, 4))
    conv_grad = mixed * queries
    yield True
    grad_two[...] = own.astype(BF16)
    grad_two_after[...] = past[0:2]
    mixed_grad[...] = mixed.astype(BF16)
    mixed_head[...] = mixed[0:2]
    out[...] = conv_grad.astype(BF16)
    out_head[...] = conv_grad[0:1]


def forward_body(
    before, signal, query, key, prev, table, base_ref, base_long,
    rate, conv_one, value_two, near, state, head,
):
    weights = table[...]
    earlier = before[0:ROWS, :]
    pair = jnp.concatenate([earlier, signal[0:ROWS, :]], 0)
    before_last = before[ROWS:, :].astype(F32)[0:1]
    queries, keys = query[...].astype(F32), key[...].astype(F32)
    _, margin = margins_before(prev)
    base = base_ref[...]
    left, _ = medium_tables(base, False)
    row, lane = iota((16, LANES), 0), iota((16, LANES), 1)
    left_edge = jnp.concatenate(
        [
            jnp.where(lane <= row + (ROWS - 16), circulant(base, g, 16, ROWS - 16), 0.0).astype(BF16)
            for g in range(TILE_GROUPS)
        ],
        0,
    )
    yield True
    products = jnp.dot(
        left, windows(pair, STRIP_FORWARD, 0, 2 * LANES), preferred_element_type=F32
    )
    products_edge = jnp.dot(left_edge, earlier, preferred_element_type=F32)
    yield True
    query_one = short_forward(queries, taps(weights, MR_Q), turned(margin, 4))
    keys_two = short_forward(keys, taps(weights, LI_K), margin)
    conv = pick(products, STRIP_FORWARD, TILE_GROUPS)
    edge = pick(products_edge, 16, TILE_GROUPS)
    far = on_channels(base, 1) * before_last
    conv_before = edge[8:16] + jnp.where(iota((8, LANES), 0) == 6, far, 0.0)
    w = taps(weights, MR_Q)
    query_before = w[0] * margin + w[1] * turned(margin, 1) + w[2] * turned(margin, 2)
    mixed_before = turned(query_before, 4) * conv_before
    mixed = (query_one * conv).astype(BF16).astype(F32)
    value = short_forward(mixed, taps(weights, LI_V), mixed_before.astype(BF16).astype(F32))
    product = keys_two * value
    rounded = product.astype(BF16)
    yield True
    left, right = long_tables(base_long, False), long_windows(rounded, False)
    powers = jnp.exp(-rate[...] * (ROWS - 1 - iota((ROWS, LANES), 0)).astype(F32))
    yield True
    products = jnp.dot(left, right, preferred_element_type=F32)
    absorbed = absorb(powers, rounded)
    yield True
    store_state(state, absorbed)
    conv_one[...] = conv.astype(BF16)
    value_two[...] = value.astype(BF16)
    own = pick(products, STRIP_FORWARD, TILE_GROUPS // 2) + weights[SKIP : SKIP + 1] * product
    near[...] = own.astype(BF16)
    head[0:2, :] = product[0:2]
    head[2:4, :] = value[0:2]
    head[4:6, :] = conv[0:2]


def late_body(
    grad_two, grad_two_after, value_two, mixed_grad, mixed_after, conv_one, next_head, table,
    grad_li_key, grad_mr_query,
):
    weights = table[...]
    head = next_head[...]
    past_two, past_mixed = grad_two_after[...], mixed_after[...]
    key_grad = grad_two[...].astype(F32) * value_two[...].astype(F32)
    query_grad = mixed_grad[...].astype(F32) * conv_one[...].astype(F32)
    key_past = two_rows(past_two[0:1] * head[2:3], past_two[1:2] * head[3:4])
    query_past = two_rows(past_mixed[0:1] * head[4:5], past_mixed[1:2] * head[5:6])
    yield True
    first = short_backward(key_grad, taps(weights, LI_K), key_past)
    second = short_backward(query_grad, taps(weights, MR_Q), query_past)
    yield True
    grad_li_key[...] = first.astype(BF16)
    grad_mr_query[...] = second.astype(BF16)


def long_body(
    near_ref, start, end, li_query, upstream, prev, following, next_head, table, rate, residue,
    base_back,
    out, grad_li_query,
):
    weights = table[...]
    near, queries, given = (ref[...].astype(F32) for ref in (near_ref, li_query, upstream))
    distance = (iota((ROWS + 16, LANES), 0) + 1).astype(F32)
    emit = (residue[...] * jnp.exp(-rate[...] * distance)).astype(BF16)
    started, ending = spread(load_state(start)), spread(load_state(end))
    head = next_head[...]
    impulse = base_back[...]
    after, _ = margins_after(following)
    _, margin = margins_before(prev)
    yield True
    emitted = jnp.dot(emit, started, preferred_element_type=F32)
    ended = jnp.dot(emit[0:16], ending, preferred_element_type=F32)
    yield True
    conv = near + emitted[0:ROWS]
    queries = short_forward(queries, taps(weights, LI_Q), turned(margin, 2))
    at_once = on_channels(impulse, 0) + weights[SKIP : SKIP + 1]
    first, second = head[0:1], head[1:2]
    past = emitted[ROWS : ROWS + 8] + ended[0:8]
    past_first = past[0:1] + at_once * first
    past_second = past[1:2] + on_channels(impulse, 1) * first + at_once * second
    grad_past = two_rows(after[4:5] * past_first, after[5:6] * past_second)
    grad = short_backward(given * conv, taps(weights, LI_Q), grad_past)
    yield True
    out[...] = (queries * conv).astype(BF16)
    grad_li_query[...] = grad.astype(BF16)


def medium_back_body(
    conv_grad, after, after_next, key, value, prev, following, table, base_ref,
    grad_key, grad_value, ext_k, ext_v, ext_gk, ext_gv,
):
    weights = table[...]
    later = after[...]
    pair = jnp.concatenate([conv_grad[...], later], 0)
    keys, values = key[...].astype(F32), value[...].astype(F32)
    before, _ = margins_before(prev)
    next_keys, next_values = margins_after(following)
    base = base_ref[...]
    left, first_half = medium_tables(base, True)
    far = on_channels(base, MR_TAPS - 1) * after_next[...].astype(BF16).astype(F32)
    filled(ext_k, keys, turned(before, 4), turned(next_keys, 2))
    filled(ext_v, values, before, next_values)
    yield True
    products = jnp.dot(left, windows(pair, STRIP_BACK, 0, 2 * LANES), preferred_element_type=F32)
    left_edge = jnp.concatenate([part[0:16] for part in first_half], 0)
    products_edge = jnp.dot(left_edge, later, preferred_element_type=F32)
    keys = shifted_sum(ext_k, taps(weights, MR_K), -1, ROWS + 8)
    values = shifted_sum(ext_v, taps(weights, MR_V), -1, ROWS + 8)
    yield True
    grad = pick(products, STRIP_BACK, TILE_GROUPS)
    edge = pick(products_edge, 16, TILE_GROUPS)
    past = two_rows(edge[0:1], edge[1:2] + far)
    filled(ext_gk, grad * values[0:ROWS], None, past * values[ROWS:])
    filled(ext_gv, grad * keys[0:ROWS], None, past * keys[ROWS:])
    yield True
    grad_key[...] = shifted_sum(ext_gk, taps(weights, MR_K), 1).astype(BF16)
    grad_value[...] = shifted_sum(ext_gv, taps(weights, MR_V), 1).astype(BF16)


def scan_states(states, rates, backward):
    count = states.shape[0]

    def kernel(states_ref, rates_ref, out_ref):
        decay = jnp.exp(rates_ref[...] * (-float(ROWS)))
        carried = jnp.zeros((8, LANES), F32)
        for k in range(count):
            b = count - 1 - k if backward else k
            out_ref[b] = carried
            carried = decay * carried + states_ref[b]

    return pl.pallas_call(
        kernel,
        name="scan_back" if backward else "scan_forward",
        out_shape=jax.ShapeDtypeStruct(states.shape, F32),
        in_specs=[pl.BlockSpec(memory_space=pltpu.VMEM)] * 2,
        out_specs=pl.BlockSpec(memory_space=pltpu.VMEM),
        cost_estimate=cost(2),
    )(states, rates)


def sent(array, by):
    size = lax.axis_size(AXES)
    pairs = [(i, i + by) for i in range(size) if 0 <= i + by < size]
    return lax.ppermute(array, AXES, pairs)


def exchanged(array):
    return lax.all_to_all(array, AXES, split_axis=0, concat_axis=0, tiled=True)


def after(array, *others):
    return lax.optimization_barrier((array, *others))[0]


def per_device(
    mr_query, mr_key, mr_value, li_query, li_key, upstream,
    mr_short, li_short, mr_filter, li_rate, li_residue, li_skip,
):
    channels = mr_query.shape[1]
    tiles = channels // LANES
    assert mr_query.shape[0] == ROWS and lax.axis_size(AXES) == 2 * tiles
    rows = (ROWS, channels)
    full = (rows, BF16, "r")
    half = ((ROWS, channels // 2), BF16, "r")
    halo = ((ROWS + 16, channels // 2), BF16, "r")
    state_out = ((2 * tiles, 8, LANES), F32, "s")
    halves = ((0, 2), (1, 2))

    def few(n):
        return ((n, channels), F32, "r")

    last_rows, first_rows = edges(mr_query, mr_key, mr_value, li_query, li_key, upstream)
    prev = sent(last_rows, 1)
    following = sent(first_rows, -1)

    table, medium, medium_turned, long, long_turned = make_tables(
        mr_short, li_short, li_skip[None, :], mr_filter, li_rate, li_residue
    )
    rate = li_rate.reshape(1, channels)
    residue = li_residue.reshape(1, channels)
    me = lax.axis_index(AXES)
    my_rates = lax.dynamic_slice(
        li_rate, ((me // 2) * TILE_GROUPS, (me % 2) * 8), (TILE_GROUPS, 8)
    )
    my_rates = jnp.repeat(my_rates.T, GROUP, axis=1)

    signal_one = [
        lane_call(
            product_one_body, "product_one", channels,
            [(mr_key, "r"), (mr_value, "r"), (prev, "r"), (table, "r")],
            [halo], 3, part,
        )[0]
        for part in halves
    ]
    before_one = [sent(signal, 1) for signal in signal_one]
    cotangent, state_back = lane_call(
        upstream_body, "upstream", channels,
        [(after(li_query, *signal_one), "r"), (upstream, "r"), (prev, "r"), (table, "r"),
         (rate, "r")],
        [full, state_out], 5,
    )
    gathered_back = exchanged(state_back)
    (near_back,) = lane_call(
        long_back_near_body, "long_back_near", channels,
        [(cotangent, "r"), (table, "r"), (long_turned, "g")],
        [full], 6,
    )

    def forward(n, into):
        return lane_call(
            forward_body, "forward", channels,
            [(before_one[n], "r"), (signal_one[n], "r"), (mr_query, "r"), (li_key, "r"),
             (prev, "r"), (table, "r"), (medium, "g"), (long, "g"), (rate, "r")],
            [full, full, full, state_out, few(6)],
            12, halves[n], into, unroll=2,
        )

    got = forward(0, {})
    gathered_back = after(gathered_back, following, near_back, got[0])
    closing = exchanged(scan_states(gathered_back, my_rates, True))
    conv_one, value_two, near, state, head = forward(1, dict(enumerate(got)))
    next_head = sent(head, -1)
    gathered = exchanged(state)

    into = {}
    conv_grad = []
    near_later = after(near_back, conv_one)
    for part in halves:
        got = lane_call(
            long_back_body, "long_back", channels,
            [(near_later, "r"), (closing, "s"), (li_query, "r"), (li_key, "r"), (mr_query, "r"),
             (prev, "r"), (following, "r"), (table, "r"), (rate, "r"), (residue, "r")],
            [full, few(2), full, few(2), few(1), half],
            5, part, into,
        )
        conv_grad.append(got[5])
        into = dict(enumerate(got[:5]))
    grad_two, grad_two_after, mixed_grad, mixed_head, conv_head, _ = got
    after_next = sent(conv_head, -2)
    mixed_after = sent(mixed_head, -1)

    gathered = after(gathered, next_head, conv_head)
    after_one = [sent(after(conv_grad[0], gathered), -1)]
    start = exchanged(scan_states(gathered, my_rates, False))
    after_one.append(sent(after(conv_grad[1], start), -1))

    def medium_back(n, into):
        return lane_call(
            medium_back_body, "medium_back", channels,
            [(conv_grad[n], "r"), (after_one[n], "r"), (after_next, "r"), (mr_key, "r"),
             (mr_value, "r"), (prev, "r"), (following, "r"), (table, "r"), (medium_turned, "g")],
            [full, full], 6, halves[n], into, exts=4,
        )

    got = medium_back(0, {})
    grad_li_key, grad_mr_query = lane_call(
        late_body, "late", channels,
        [(grad_two, "r"), (grad_two_after, "r"), (value_two, "r"), (mixed_grad, "r"),
         (mixed_after, "r"), (conv_one, "r"), (next_head, "r"), (table, "r")],
        [full, full], 5,
    )
    output, grad_li_query = lane_call(
        long_body, "long_forward", channels,
        [(near, "r"), (start, "s"), (state, "s"), (li_query, "r"), (upstream, "r"),
         (prev, "r"), (following, "r"), (next_head, "r"), (table, "r"), (rate, "r"), (residue, "r"),
         (long_turned, "g")],
        [full, full], 7,
    )
    grad_mr_key, grad_mr_value = medium_back(1, dict(enumerate(got)))
    return (output, grad_mr_query, grad_mr_key, grad_mr_value, grad_li_query, grad_li_key)


def solution(mesh):
    split = P(("ctx", "ch"), None)
    return jax.shard_map(
        per_device,
        mesh=mesh,
        in_specs=(split,) * 6 + (P(),) * 6,
        out_specs=(split,) * 6,
        check_vma=False,
    )
```

```python
import math

import jax
import jax.numpy as jnp
from jax import lax
from jax.experimental import pallas as pl
from jax.experimental.pallas import tpu as pltpu
from jax.sharding import PartitionSpec as P

GROUP = 16
SHORT = 3
MR_TAPS = 128
MODES = 16
ROWS = 128
LANES = 128
STRIP_FORWARD = 32
STRIP_BACK = 32
TILE_GROUPS = LANES // GROUP
AXES = ("ctx", "ch")
BF16 = jnp.bfloat16
F32 = jnp.float32
VMEM_LIMIT = 56 * 1024 * 1024

MR_Q, MR_K, MR_V, LI_Q, LI_K, LI_V, SKIP = 0, 3, 6, 9, 12, 15, 18
TABLE_ROWS = 24


def cost(microseconds):
    return pl.CostEstimate(
        flops=0, bytes_accessed=int(microseconds * 3.6e6), transcendentals=0
    )


def hint(start, of):
    return start if isinstance(start, int) else pl.multiple_of(start, of)


def lane_call(body, name, channels, ins, outs, us, part=None, into=None, width=1024, unroll=4, exts=0):
    begin, end = part or (0, channels)
    span = end - begin
    width = min(width, span)
    tiles = width // LANES
    unroll = math.gcd(unroll, tiles)
    blocks = span // width
    into = into or {}
    kinds = [kind for _, kind in ins] + [kind for _, _, kind in outs]
    shapes = [a.shape for a, _ in ins] + [shape for shape, _, _ in outs]
    dtypes = [a.dtype for a, _ in ins] + [dtype for _, dtype, _ in outs]
    count, count_in, count_into = len(kinds), len(ins), len(into)

    def channels_of(shape, kind):
        return {"r": shape[-1], "g": shape[0] * GROUP, "s": shape[0] * (LANES // 2)}[kind]

    def cut(ref, kind, start, size):
        if kind == "r":
            return ref.at[:, pl.ds(hint(start, LANES), size)]
        if kind == "g":
            return ref.at[pl.ds(hint(start // GROUP, TILE_GROUPS), size // GROUP), :]
        return ref.at[pl.ds(start // (LANES // 2), size // (LANES // 2))]

    def kept(shape, kind):
        if kind == "r":
            return (shape[0], span)
        return (span // GROUP, shape[1]) if kind == "g" else (span // (LANES // 2), *shape[1:])

    first = [
        begin if channels_of(shape, kind) == channels else 0
        for shape, kind in zip(shapes, kinds)
    ]

    def kernel(*refs):
        far = refs[:count_in] + refs[count_in + count_into : count + count_into]
        held = refs[count + count_into : 2 * count + count_into]
        arrived, *extra = refs[2 * count + count_into :]

        def copy(n, b):
            outside = cut(far[n], kinds[n], first[n] + b * width, width)
            inside = cut(held[n], kinds[n], b * width, width)
            if n < count_in:
                return pltpu.make_async_copy(outside, inside, arrived.at[n, b])
            return pltpu.make_async_copy(inside, outside, arrived.at[n, b])

        for b in range(blocks):
            for n in range(count_in):
                copy(n, b).start()

        def block(b, unused):
            for n in range(count_in):
                copy(n, b).wait()

            def step(k, unused):
                running = []
                for u in range(unroll):
                    start = b * width + (k * unroll + u) * LANES
                    running.append(
                        body(
                            *[cut(ref, kind, start, LANES) for ref, kind in zip(held, kinds)],
                            *[ref.at[u, n] for ref in extra for n in range(exts)],
                        )
                    )
                while running:
                    running = [tile for tile in running if next(tile, False)]
                return unused

            lax.fori_loop(0, tiles // unroll, step, 0)
            for n in range(count_in, count):
                copy(n, b).start()
            return unused

        lax.fori_loop(0, blocks, block, 0)
        for b in range(blocks):
            for n in range(count_in, count):
                copy(n, b).wait()

    anywhere = pl.BlockSpec(memory_space=pl.ANY)
    return pl.pallas_call(
        kernel,
        name=name,
        in_specs=[anywhere] * (count_in + count_into),
        out_specs=[anywhere] * len(outs),
        out_shape=[jax.ShapeDtypeStruct(shape, dtype) for shape, dtype, _ in outs],
        scratch_shapes=[
            *[pltpu.VMEM(kept(*which), dtype) for *which, dtype in zip(shapes, kinds, dtypes)],
            pltpu.SemaphoreType.DMA((count, blocks)),
            *([pltpu.VMEM((unroll, exts, ROWS + 16, LANES), F32)] if exts else []),
        ],
        input_output_aliases={count_in + n: at for n, at in enumerate(into)},
        compiler_params=pltpu.CompilerParams(vmem_limit_bytes=VMEM_LIMIT),
        cost_estimate=cost(us),
    )(*[a for a, _ in ins], *into.values())


def turned(x, by):
    return pltpu.roll(x, by, 0) if by else x


def taps(table, first):
    return [table[first + j : first + j + 1, :] for j in range(SHORT)]


def short_forward(signal, weights, prev8):
    total = weights[0] * signal
    first = iota((8, LANES), 0)
    for by in (1, 2):
        moved = turned(signal, by)
        top = jnp.where(first < by, turned(prev8, by), moved[0:8])
        rest = [moved[8:]] if signal.shape[0] > 8 else []
        total += weights[by] * jnp.concatenate([top, *rest], 0)
    return total


def short_backward(signal, weights, next8):
    total = weights[0] * signal
    rows = signal.shape[0]
    last = iota((8, LANES), 0)
    for by in (1, 2):
        moved = turned(signal, rows - by)
        bottom = jnp.where(last >= 8 - by, turned(next8, 8 - by), moved[rows - 8 :])
        total += weights[by] * jnp.concatenate([moved[: rows - 8], bottom], 0)
    return total


def filled(ext, signal, prev8=None, next8=None):
    ext[8 : 8 + ROWS, :] = signal
    if prev8 is not None:
        ext[0:8, :] = prev8
    if next8 is not None:
        ext[8 + ROWS :, :] = next8


def shifted_sum(ext, weights, way, rows=ROWS):
    parts = [w * ext[8 + way * j : 8 + way * j + rows, :] for j, w in enumerate(weights)]
    return parts[0] + parts[1] + parts[2]


def two_rows(first, second):
    at = iota((8, LANES), 0)
    return jnp.where(at == 0, first, jnp.where(at == 1, second, 0.0))


def iota(shape, dim):
    return lax.broadcasted_iota(jnp.int32, shape, dim)


def circulant(base, g, rows, shift=0):
    row = jnp.broadcast_to(base[g : g + 1, :], (rows, LANES))
    return pltpu.roll(row, shift, 1, stride=1, stride_axis=0)


def pick(products, rows, count):
    columns = LANES // count
    owner = iota((rows, LANES), 1) // columns
    picked = []
    for q in range(products.shape[1] // LANES):
        at = slice(q * LANES, (q + 1) * LANES)
        total = products[0:rows, at]
        for p in range(1, count):
            total = jnp.where(owner == p, products[p * rows : (p + 1) * rows, at], total)
        picked.append(total)
    return jnp.concatenate(picked, 0)


def windows(signal, strip, first, length):
    count = signal.shape[0]
    parts = []
    for q in range(ROWS // strip):
        low, high = strip * q + first, strip * q + first + length
        inside = signal[max(low, 0) : min(high, count)]
        pieces = [inside]
        if low < 0:
            pieces.insert(0, jnp.zeros((-low, LANES), signal.dtype))
        if high > count:
            pieces.append(jnp.zeros((high - count, LANES), signal.dtype))
        parts.append(jnp.concatenate(pieces, 0) if len(pieces) > 1 else inside)
    return jnp.concatenate(parts, 1)


def split_groups(signal):
    odd = ((iota(signal.shape, 1) // GROUP) % 2).astype(F32)
    return signal * (1.0 - odd).astype(signal.dtype), signal * odd.astype(signal.dtype)


def long_tables(base_ref, backward):
    strip = STRIP_BACK if backward else STRIP_FORWARD
    base = base_ref[...]
    row, lane = iota((strip, LANES), 0), iota((strip, LANES), 1)
    first = 0 if backward else strip - LANES
    keep = lane >= row if backward else lane + first <= row
    tables = [
        jnp.where(keep, circulant(base, g, strip, -first), 0.0).astype(BF16)
        for g in range(TILE_GROUPS)
    ]
    return jnp.concatenate(
        [jnp.concatenate(tables[0::2], 0), jnp.concatenate(tables[1::2], 0)], 1
    )


def long_windows(signal, backward):
    strip = STRIP_BACK if backward else STRIP_FORWARD
    first = 0 if backward else strip - LANES
    even, odd = split_groups(signal)
    return jnp.concatenate(
        [windows(even, strip, first, LANES), windows(odd, strip, first, LANES)], 0
    )


def medium_tables(base, backward):
    strip = STRIP_BACK if backward else STRIP_FORWARD
    row, lane = iota((strip, LANES), 0), iota((strip, LANES), 1)
    keep = lane >= row if backward else lane > row
    wholes = [circulant(base, g, strip) for g in range(TILE_GROUPS)]
    first = [jnp.where(keep, whole, 0.0).astype(BF16) for whole in wholes]
    second = [jnp.where(keep, 0.0, whole).astype(BF16) for whole in wholes]
    return jnp.concatenate([jnp.concatenate(first, 0), jnp.concatenate(second, 0)], 1), first


def on_channels(base, column):
    own = iota((TILE_GROUPS, LANES), 0) == iota((TILE_GROUPS, LANES), 1) // GROUP
    return jnp.where(own, base[:, column : column + 1], 0.0).sum(0, keepdims=True)


def own_group():
    return (iota((LANES, LANES), 0) // MODES == iota((LANES, LANES), 1) // GROUP).astype(F32)


def spread(state):
    return (jnp.concatenate([state] * TILE_GROUPS, 0) * own_group()).astype(BF16)


def absorb(powers, signal):
    every = lax.dot_general(
        powers.astype(BF16), signal, (((0,), (0,)), ((), ())), preferred_element_type=F32
    )
    return (every * own_group()).reshape(TILE_GROUPS, MODES, LANES).sum(0)


def store_state(ref, state):
    ref[...] = state.reshape(2, 8, LANES).astype(ref.dtype)


def load_state(ref):
    return ref[...].astype(F32).reshape(MODES, LANES)


def margins_before(ref):
    rows = ref[...].astype(F32)
    return rows[0:8], rows[8:16]


def margins_after(ref):
    rows = ref[...].astype(F32)
    return rows[0:8], rows[8:16]


def edges(mr_query, mr_key, mr_value, li_query, li_key, upstream):
    channels = mr_query.shape[1]
    width = channels

    def kernel(q_end, k_end, v_end, lq_end, lk_end, lq, lk, g, k, v, last, first, a, b):
        a[0:4, :] = k_end[...].astype(F32)[12:16]
        a[4:8, :] = v_end[...].astype(F32)[12:16]
        a[8:12, :] = q_end[...].astype(F32)[12:16]
        a[12:14, :] = lq_end[...].astype(F32)[14:16]
        a[14:16, :] = lk_end[...].astype(F32)[14:16]
        for n, ref in enumerate((lq, lk, g, k, v)):
            b[2 * n : 2 * n + 2, :] = ref[...].astype(F32)[0:2]
        b[10:16, :] = jnp.zeros((6, width), F32)
        last[...] = a[...].astype(BF16)
        first[...] = b[...].astype(BF16)

    low = pl.BlockSpec((16, width), lambda i: (ROWS // 16 - 1, i))
    high = pl.BlockSpec((16, width), lambda i: (0, i))
    small = jax.ShapeDtypeStruct((16, channels), BF16)
    return pl.pallas_call(
        kernel,
        name="edges",
        grid=(channels // width,),
        in_specs=[low] * 5 + [high] * 5,
        out_specs=[high, high],
        out_shape=[small, small],
        scratch_shapes=[pltpu.VMEM((16, width), F32)] * 2,
        compiler_params=pltpu.CompilerParams(vmem_limit_bytes=VMEM_LIMIT),
        cost_estimate=cost(3.5),
    )(mr_query, mr_key, mr_value, li_query, li_key, li_query, li_key, upstream, mr_key, mr_value)


def make_tables(mr_short, li_short, li_skip, mr_filter, li_rate, li_residue):
    groups = mr_filter.shape[1]
    channels = groups * GROUP
    block = min(128, groups)
    width = block * GROUP

    def kernel(mr, li, skip, filters, rate, residue, table, medium, medium_back, long, long_back):
        for n in range(3):
            table[3 * n : 3 * n + 3, :] = mr[n].astype(F32)
            table[9 + 3 * n : 12 + 3 * n, :] = li[n].astype(F32)
        table[SKIP : SKIP + 1, :] = skip[...]
        table[SKIP + 1 :, :] = jnp.zeros((TABLE_ROWS - SKIP - 1, width), F32)
        row, lane = iota((LANES, LANES), 0), iota((LANES, LANES), 1)
        same = (row == lane).astype(F32).astype(BF16)
        turn = (row == (LANES - lane) % LANES).astype(F32).astype(BF16)
        by_rows = (((0,), (0,)), ((), ()))
        medium[...] = lax.dot_general(filters[...], turn, by_rows, preferred_element_type=F32)
        medium_back[...] = lax.dot_general(filters[...], same, by_rows, preferred_element_type=F32)
        position = iota((block, LANES), 1).astype(F32)
        impulse = jnp.zeros((block, LANES), F32)
        for n in range(MODES):
            impulse += residue[:, n : n + 1] * jnp.exp(-rate[:, n : n + 1] * position)
        long_back[...] = impulse
        long[...] = jnp.dot(impulse.astype(BF16), turn, preferred_element_type=F32)

    shorts = pl.BlockSpec((3, 3, width), lambda i: (0, 0, i))
    modes = pl.BlockSpec((block, MODES), lambda i: (i, 0))
    by_tap = pl.BlockSpec((block, LANES), lambda i: (i, 0))
    shapes = [jax.ShapeDtypeStruct((TABLE_ROWS, channels), F32)]
    shapes += [jax.ShapeDtypeStruct((groups, LANES), F32)] * 4
    return pl.pallas_call(
        kernel,
        name="tables",
        grid=(groups // block,),
        in_specs=[
            shorts, shorts, pl.BlockSpec((1, width), lambda i: (0, i)),
            pl.BlockSpec((MR_TAPS, block), lambda i: (0, i)), modes, modes,
        ],
        out_specs=[pl.BlockSpec((TABLE_ROWS, width), lambda i: (0, i))] + [by_tap] * 4,
        out_shape=shapes,
        compiler_params=pltpu.CompilerParams(vmem_limit_bytes=VMEM_LIMIT),
        cost_estimate=cost(5),
    )(mr_short, li_short, li_skip, mr_filter, li_rate, li_residue)


def product_one_body(key, value, prev, table, out):
    weights = table[...]
    before, _ = margins_before(prev)
    w_k, w_v = taps(weights, MR_K), taps(weights, MR_V)
    signal_k, signal_v = key[...].astype(F32), value[...].astype(F32)
    yield True
    k = short_forward(signal_k, w_k, turned(before, 4))
    v = short_forward(signal_v, w_v, before)
    yield True
    out[0:ROWS, :] = (k * v).astype(BF16)
    key_last = w_k[0] * before[3:4] + w_k[1] * before[2:3] + w_k[2] * before[1:2]
    value_last = w_v[0] * before[7:8] + w_v[1] * before[6:7] + w_v[2] * before[5:6]
    out[ROWS:, :] = jnp.broadcast_to(key_last * value_last, (16, LANES)).astype(BF16)


def upstream_body(li_query, upstream, prev, table, rate, cotangent, state):
    weights = table[...]
    _, margin = margins_before(prev)
    signal, given, decay = li_query[...].astype(F32), upstream[...].astype(F32), rate[...]
    yield True
    powers = jnp.exp(-decay * iota((ROWS, LANES), 0).astype(F32))
    query_two = short_forward(signal, taps(weights, LI_Q), turned(margin, 2))
    rounded = (given * query_two).astype(BF16)
    yield True
    absorbed = absorb(powers, rounded)
    yield True
    store_state(state, absorbed)
    cotangent[...] = rounded


def long_back_near_body(cotangent, table, base, near):
    signal = cotangent[...]
    skip = table[SKIP : SKIP + 1, :]
    left, right = long_tables(base, True), long_windows(signal, True)
    yield True
    products = jnp.dot(left, right, preferred_element_type=F32)
    yield True
    product = pick(products, STRIP_BACK, TILE_GROUPS // 2) + skip * signal.astype(F32)
    near[...] = product.astype(BF16)


def long_back_body(
    near_ref, closing, li_query, li_key, query, prev, following, table, rate, residue,
    grad_two, grad_two_after, mixed_grad, mixed_head, out_head, out,
):
    weights = table[...]
    _, before = margins_before(prev)
    after, _ = margins_after(following)
    near, state = near_ref[...].astype(F32), load_state(closing)
    key, queries = li_key[...].astype(F32), query[...].astype(F32)
    query_end = li_query[ROWS - 16 :, :].astype(F32)[8:16]
    distance = (ROWS - iota((ROWS + 16, LANES), 0)).astype(F32)
    emit = (residue[...] * jnp.exp(-rate[...] * distance)).astype(BF16)
    cot_after = turned(after, 4) * short_forward(after, taps(weights, LI_Q), query_end)
    yield True
    emitted = jnp.dot(emit, spread(state), preferred_element_type=F32)
    later = jnp.dot(emit[ROWS:], spread(state - cot_after[0:1]), preferred_element_type=F32)
    yield True
    skip = weights[SKIP : SKIP + 1]
    own = near + emitted[0:ROWS]
    at_row = iota((8, LANES), 0)
    past = jnp.where(at_row == 0, emitted[ROWS : ROWS + 8], later[0:8]) + skip * cot_after
    past = jnp.where(at_row < 2, past, 0.0)
    w_k = taps(weights, LI_K)
    keys_two = short_forward(key, w_k, before)
    keys_after = short_forward(turned(after, 6), w_k, key[ROWS - 8 :])
    mixed = short_backward(own * keys_two, taps(weights, LI_V), past * keys_after)
    queries = short_forward(queries, taps(weights, MR_Q), turned(before, 4))
    conv_grad = mixed * queries
    yield True
    grad_two[...] = own.astype(BF16)
    grad_two_after[...] = past[0:2]
    mixed_grad[...] = mixed.astype(BF16)
    mixed_head[...] = mixed[0:2]
    out[...] = conv_grad.astype(BF16)
    out_head[...] = conv_grad[0:1]


def forward_body(
    before, signal, query, key, prev, table, base_ref, base_long,
    rate, conv_one, value_two, near, state, head,
):
    weights = table[...]
    earlier = before[0:ROWS, :]
    pair = jnp.concatenate([earlier, signal[0:ROWS, :]], 0)
    before_last = before[ROWS:, :].astype(F32)[0:1]
    queries, keys = query[...].astype(F32), key[...].astype(F32)
    _, margin = margins_before(prev)
    base = base_ref[...]
    left, _ = medium_tables(base, False)
    row, lane = iota((16, LANES), 0), iota((16, LANES), 1)
    left_edge = jnp.concatenate(
        [
            jnp.where(lane <= row + (ROWS - 16), circulant(base, g, 16, ROWS - 16), 0.0).astype(BF16)
            for g in range(TILE_GROUPS)
        ],
        0,
    )
    yield True
    products = jnp.dot(
        left, windows(pair, STRIP_FORWARD, 0, 2 * LANES), preferred_element_type=F32
    )
    products_edge = jnp.dot(left_edge, earlier, preferred_element_type=F32)
    yield True
    query_one = short_forward(queries, taps(weights, MR_Q), turned(margin, 4))
    keys_two = short_forward(keys, taps(weights, LI_K), margin)
    conv = pick(products, STRIP_FORWARD, TILE_GROUPS)
    edge = pick(products_edge, 16, TILE_GROUPS)
    far = on_channels(base, 1) * before_last
    conv_before = edge[8:16] + jnp.where(iota((8, LANES), 0) == 6, far, 0.0)
    w = taps(weights, MR_Q)
    query_before = w[0] * margin + w[1] * turned(margin, 1) + w[2] * turned(margin, 2)
    mixed_before = turned(query_before, 4) * conv_before
    mixed = (query_one * conv).astype(BF16).astype(F32)
    value = short_forward(mixed, taps(weights, LI_V), mixed_before.astype(BF16).astype(F32))
    product = keys_two * value
    rounded = product.astype(BF16)
    yield True
    left, right = long_tables(base_long, False), long_windows(rounded, False)
    powers = jnp.exp(-rate[...] * (ROWS - 1 - iota((ROWS, LANES), 0)).astype(F32))
    yield True
    products = jnp.dot(left, right, preferred_element_type=F32)
    absorbed = absorb(powers, rounded)
    yield True
    store_state(state, absorbed)
    conv_one[...] = conv.astype(BF16)
    value_two[...] = value.astype(BF16)
    own = pick(products, STRIP_FORWARD, TILE_GROUPS // 2) + weights[SKIP : SKIP + 1] * product
    near[...] = own.astype(BF16)
    head[0:2, :] = product[0:2]
    head[2:4, :] = value[0:2]
    head[4:6, :] = conv[0:2]


def late_body(
    grad_two, grad_two_after, value_two, mixed_grad, mixed_after, conv_one, next_head, table,
    grad_li_key, grad_mr_query,
):
    weights = table[...]
    head = next_head[...]
    past_two, past_mixed = grad_two_after[...], mixed_after[...]
    key_grad = grad_two[...].astype(F32) * value_two[...].astype(F32)
    query_grad = mixed_grad[...].astype(F32) * conv_one[...].astype(F32)
    key_past = two_rows(past_two[0:1] * head[2:3], past_two[1:2] * head[3:4])
    query_past = two_rows(past_mixed[0:1] * head[4:5], past_mixed[1:2] * head[5:6])
    yield True
    first = short_backward(key_grad, taps(weights, LI_K), key_past)
    second = short_backward(query_grad, taps(weights, MR_Q), query_past)
    yield True
    grad_li_key[...] = first.astype(BF16)
    grad_mr_query[...] = second.astype(BF16)


def long_body(
    near_ref, start, end, li_query, upstream, prev, following, next_head, table, rate, residue,
    base_back,
    out, grad_li_query,
):
    weights = table[...]
    near, queries, given = (ref[...].astype(F32) for ref in (near_ref, li_query, upstream))
    distance = (iota((ROWS + 16, LANES), 0) + 1).astype(F32)
    emit = (residue[...] * jnp.exp(-rate[...] * distance)).astype(BF16)
    started, ending = spread(load_state(start)), spread(load_state(end))
    head = next_head[...]
    impulse = base_back[...]
    after, _ = margins_after(following)
    _, margin = margins_before(prev)
    yield True
    emitted = jnp.dot(emit, started, preferred_element_type=F32)
    ended = jnp.dot(emit[0:16], ending, preferred_element_type=F32)
    yield True
    conv = near + emitted[0:ROWS]
    queries = short_forward(queries, taps(weights, LI_Q), turned(margin, 2))
    at_once = on_channels(impulse, 0) + weights[SKIP : SKIP + 1]
    first, second = head[0:1], head[1:2]
    past = emitted[ROWS : ROWS + 8] + ended[0:8]
    past_first = past[0:1] + at_once * first
    past_second = past[1:2] + on_channels(impulse, 1) * first + at_once * second
    grad_past = two_rows(after[4:5] * past_first, after[5:6] * past_second)
    grad = short_backward(given * conv, taps(weights, LI_Q), grad_past)
    yield True
    out[...] = (queries * conv).astype(BF16)
    grad_li_query[...] = grad.astype(BF16)


def medium_back_body(
    conv_grad, after, after_next, key, value, prev, following, table, base_ref,
    grad_key, grad_value, ext_k, ext_v, ext_gk, ext_gv,
):
    weights = table[...]
    later = after[...]
    pair = jnp.concatenate([conv_grad[...], later], 0)
    keys, values = key[...].astype(F32), value[...].astype(F32)
    before, _ = margins_before(prev)
    next_keys, next_values = margins_after(following)
    base = base_ref[...]
    left, first_half = medium_tables(base, True)
    far = on_channels(base, MR_TAPS - 1) * after_next[...].astype(BF16).astype(F32)
    filled(ext_k, keys, turned(before, 4), turned(next_keys, 2))
    filled(ext_v, values, before, next_values)
    yield True
    products = jnp.dot(left, windows(pair, STRIP_BACK, 0, 2 * LANES), preferred_element_type=F32)
    left_edge = jnp.concatenate([part[0:16] for part in first_half], 0)
    products_edge = jnp.dot(left_edge, later, preferred_element_type=F32)
    keys = shifted_sum(ext_k, taps(weights, MR_K), -1, ROWS + 8)
    values = shifted_sum(ext_v, taps(weights, MR_V), -1, ROWS + 8)
    yield True
    grad = pick(products, STRIP_BACK, TILE_GROUPS)
    edge = pick(products_edge, 16, TILE_GROUPS)
    past = two_rows(edge[0:1], edge[1:2] + far)
    filled(ext_gk, grad * values[0:ROWS], None, past * values[ROWS:])
    filled(ext_gv, grad * keys[0:ROWS], None, past * keys[ROWS:])
    yield True
    grad_key[...] = shifted_sum(ext_gk, taps(weights, MR_K), 1).astype(BF16)
    grad_value[...] = shifted_sum(ext_gv, taps(weights, MR_V), 1).astype(BF16)


def scan_states(states, rates, backward):
    count = states.shape[0]

    def kernel(states_ref, rates_ref, out_ref):
        decay = jnp.exp(rates_ref[...] * (-float(ROWS)))
        carried = jnp.zeros((8, LANES), F32)
        for k in range(count):
            b = count - 1 - k if backward else k
            out_ref[b] = carried
            carried = decay * carried + states_ref[b]

    return pl.pallas_call(
        kernel,
        name="scan_back" if backward else "scan_forward",
        out_shape=jax.ShapeDtypeStruct(states.shape, F32),
        in_specs=[pl.BlockSpec(memory_space=pltpu.VMEM)] * 2,
        out_specs=pl.BlockSpec(memory_space=pltpu.VMEM),
        cost_estimate=cost(2),
    )(states, rates)


def sent(array, by):
    size = lax.axis_size(AXES)
    pairs = [(i, i + by) for i in range(size) if 0 <= i + by < size]
    return lax.ppermute(array, AXES, pairs)


def exchanged(array):
    return lax.all_to_all(array, AXES, split_axis=0, concat_axis=0, tiled=True)


def after(array, *others):
    return lax.optimization_barrier((array, *others))[0]


def per_device(
    mr_query, mr_key, mr_value, li_query, li_key, upstream,
    mr_short, li_short, mr_filter, li_rate, li_residue, li_skip,
):
    channels = mr_query.shape[1]
    tiles = channels // LANES
    assert mr_query.shape[0] == ROWS and lax.axis_size(AXES) == 2 * tiles
    rows = (ROWS, channels)
    full = (rows, BF16, "r")
    state_out = ((2 * tiles, 8, LANES), F32, "s")
    cut = tiles * 3 // 4 * LANES
    parts = ((0, cut), (cut, channels))

    def own(n, part):
        return ((n, part[1] - part[0]), BF16, "r")


    def few(n):
        return ((n, channels), F32, "r")

    last_rows, first_rows = edges(mr_query, mr_key, mr_value, li_query, li_key, upstream)
    prev = sent(last_rows, 1)
    following = sent(first_rows, -1)

    table, medium, medium_turned, long, long_turned = make_tables(
        mr_short, li_short, li_skip[None, :], mr_filter, li_rate, li_residue
    )
    rate = li_rate.reshape(1, channels)
    residue = li_residue.reshape(1, channels)
    me = lax.axis_index(AXES)
    my_rates = lax.dynamic_slice(
        li_rate, ((me // 2) * TILE_GROUPS, (me % 2) * 8), (TILE_GROUPS, 8)
    )
    my_rates = jnp.repeat(my_rates.T, GROUP, axis=1)

    signal_one = [
        lane_call(
            product_one_body, "product_one", channels,
            [(mr_key, "r"), (mr_value, "r"), (prev, "r"), (table, "r")],
            [own(ROWS + 16, part)], 3, part,
        )[0]
        for part in parts
    ]
    before_one = [sent(signal, 1) for signal in signal_one]
    cotangent, state_back = lane_call(
        upstream_body, "upstream", channels,
        [(after(li_query, *signal_one), "r"), (upstream, "r"), (prev, "r"), (table, "r"),
         (rate, "r")],
        [full, state_out], 5,
    )
    gathered_back = exchanged(state_back)
    (near_back,) = lane_call(
        long_back_near_body, "long_back_near", channels,
        [(cotangent, "r"), (table, "r"), (long_turned, "g")],
        [full], 6,
    )

    def forward(n, into):
        return lane_call(
            forward_body, "forward", channels,
            [(before_one[n], "r"), (signal_one[n], "r"), (mr_query, "r"), (li_key, "r"),
             (prev, "r"), (table, "r"), (medium, "g"), (long, "g"), (rate, "r")],
            [full, full, full, state_out, few(6)],
            12, parts[n], into, unroll=2,
        )

    got = forward(0, {})
    gathered_back = after(gathered_back, following, near_back, got[0])
    closing = exchanged(scan_states(gathered_back, my_rates, True))
    conv_one, value_two, near, state, head = forward(1, dict(enumerate(got)))
    next_head = sent(head, -1)
    gathered = after(exchanged(state), next_head)

    into = {}
    conv_grad = []
    near_later = after(near_back, conv_one)
    for part in parts:
        near_later = after(near_later, gathered) if into else near_later
        got = lane_call(
            long_back_body, "long_back", channels,
            [(near_later, "r"), (closing, "s"), (li_query, "r"), (li_key, "r"), (mr_query, "r"),
             (prev, "r"), (following, "r"), (table, "r"), (rate, "r"), (residue, "r")],
            [full, few(2), full, few(2), few(1), own(ROWS, part)],
            5, part, into,
        )
        conv_grad.append(got[5])
        into = dict(enumerate(got[:5]))
    grad_two, grad_two_after, mixed_grad, mixed_head, conv_head, _ = got
    after_next = sent(conv_head, -2)
    mixed_after = sent(mixed_head, -1)

    gathered = after(gathered, conv_head)
    after_one = [sent(after(conv_grad[0], gathered, after_next, mixed_after), -1)]
    start = exchanged(scan_states(gathered, my_rates, False))
    after_one.append(sent(after(conv_grad[1], start), -1))

    def medium_back(n, into):
        return lane_call(
            medium_back_body, "medium_back", channels,
            [(conv_grad[n], "r"), (after_one[n], "r"), (after_next, "r"), (mr_key, "r"),
             (mr_value, "r"), (prev, "r"), (following, "r"), (table, "r"), (medium_turned, "g")],
            [full, full], 6, parts[n], into, exts=4,
        )

    grad_li_key, grad_mr_query = lane_call(
        late_body, "late", channels,
        [(grad_two, "r"), (grad_two_after, "r"), (value_two, "r"), (mixed_grad, "r"),
         (mixed_after, "r"), (conv_one, "r"), (next_head, "r"), (table, "r")],
        [full, full], 5,
    )
    start = after(start, grad_li_key)
    output, grad_li_query = lane_call(
        long_body, "long_forward", channels,
        [(near, "r"), (start, "s"), (state, "s"), (li_query, "r"), (upstream, "r"),
         (prev, "r"), (following, "r"), (next_head, "r"), (table, "r"), (rate, "r"), (residue, "r"),
         (long_turned, "g")],
        [full, full], 7,
    )
    conv_grad[0] = after(conv_grad[0], grad_li_query)
    got = medium_back(0, {})
    grad_mr_key, grad_mr_value = medium_back(1, dict(enumerate(got)))
    return (output, grad_mr_query, grad_mr_key, grad_mr_value, grad_li_query, grad_li_key)


def solution(mesh):
    split = P(("ctx", "ch"), None)
    return jax.shard_map(
        per_device,
        mesh=mesh,
        in_specs=(split,) * 6 + (P(),) * 6,
        out_specs=(split,) * 6,
        check_vma=False,
    )
```
